32 devices in a mesh: section: 8 (over y, x, core), shard: 4 (over z).
Axes of the slice: x: 2, y: 2, z: 4, core: 2. Of those that a mesh axis runs over, the one named last changes fastest.
Arguments:
- tokens: bfloat16 [64, 1024, 512], P(('section', 'shard')), may hold values from -6 to 6
- cotangent: bfloat16 [64, 1024, 512], P(('section', 'shard')), may hold values from -6 to 6
- route: int32 [32, 1024], replicated, may hold values from 0 to 1, as said below
- remask: int32 [32, 1024], replicated, may hold values 0 or 1
- timestep: int32 [32], replicated, may hold values from 0 to 49
- enc_qkv: float32 [512, 1536], P('shard'), may hold values from -0.25 to 0.25
- enc_out: float32 [512, 512], P('shard'), may hold values from -2 to 2
- enc_up: float32 [512, 2048], P('shard'), may hold values from -0.25 to 0.25
- enc_down: float32 [2048, 512], P('shard'), may hold values from -0.125 to 0.125
- enc_gains: float32 [2, 512], P(None, 'shard'), may hold values from 0.5 to 1.5
- enc_shifts: float32 [2, 512], P(None, 'shard'), may hold values from -4 to 4
- dec_qkv: float32 [512, 1536], P('shard'), may hold values from -0.25 to 0.25
- dec_out: float32 [512, 512], P('shard'), may hold values from -2 to 2
- cross_query: float32 [512, 512], P('shard'), may hold values from -0.25 to 0.25
- cross_kv: float32 [512, 1024], P('shard'), may hold values from -0.25 to 0.25
- cross_out: float32 [512, 512], P('shard'), may hold values from -2 to 2
- dec_up: float32 [512, 2048], P('shard'), may hold values from -0.25 to 0.25
- dec_down: float32 [2048, 512], P('shard'), may hold values from -0.125 to 0.125
- dec_gains: float32 [3, 512], P(None, 'shard'), may hold values from 0.5 to 1.5
- dec_shifts: float32 [3, 512], P(None, 'shard'), may hold values from -4 to 4
- time_table: float32 [50, 512], P(None, 'shard'), may hold values from -6 to 6
- mask_embed: float32 [512], P('shard'), may hold values from -6 to 6
Outputs:
- layer_out: bfloat16 [64, 1024, 512], P(('section', 'shard'))
- grad_in: float32 [64, 1024, 512], P(('section', 'shard'))
- grad_enc_qkv: float32 [512, 1536], P('shard')
- grad_enc_out: float32 [512, 512], P('shard')
- grad_enc_up: float32 [512, 2048], P('shard')
- grad_enc_down: float32 [2048, 512], P('shard')
- grad_enc_gains: float32 [2, 512], P(None, 'shard')
- grad_enc_shifts: float32 [2, 512], P(None, 'shard')
- grad_dec_qkv: float32 [512, 1536], P('shard')
- grad_dec_out: float32 [512, 512], P('shard')
- grad_cross_query: float32 [512, 512], P('shard')
- grad_cross_kv: float32 [512, 1024], P('shard')
- grad_cross_out: float32 [512, 512], P('shard')
- grad_dec_up: float32 [512, 2048], P('shard')
- grad_dec_down: float32 [2048, 512], P('shard')
- grad_dec_gains: float32 [3, 512], P(None, 'shard')
- grad_dec_shifts: float32 [3, 512], P(None, 'shard')
- grad_time_table: float32 [50, 512], P(None, 'shard')
- grad_mask_embed: float32 [512], P('shard')
The draws below stay inside these ranges and needn't reach their ends.
Inputs may be any that keep to these rules, and one draw needn't show every extreme that they name: route is 1 at the first token of every sequence.
All inputs are finite; a program needn't handle non-finite values.
Results may differ from the reference program's by a relative error of at most 0.024.
The reference program's roundings to bfloat16 on the way count: a program that leaves them out, or rounds other values in their place, can miss the bound.
Values may be sent and summed in bfloat16 or wider, within the bound.
A program may use at most 320 MiB of HBM per device.

```python
import jax
import jax.numpy as jnp
from jax import lax

D = 512
HEADS = 8
FF = 2048
SEQ = 1024
MB = 2
STEPS = 50
ROWS = 64
HALF_ROWS = 32


def draw_route(key, part):
    key = jax.random.fold_in(key, 7)
    rate_key, token_key = jax.random.split(key)
    rates = jax.random.randint(rate_key, (HALF_ROWS, 1), 1, 9)
    marks = jax.random.randint(token_key, (HALF_ROWS, SEQ), 0, 8)
    routed = (marks < rates).astype(jnp.int32)
    first = (jnp.arange(SEQ) == 0)[None, :]
    return jnp.where(first, 1, routed).astype(jnp.int32)


def touch_ends(values, own_key, smallest, largest):
    dims = values.shape
    spot = [jax.random.randint(jax.random.fold_in(own_key, axis), (), 0, dims[axis]) for axis in range(len(dims))]
    values = values.at[tuple(spot)].set(smallest)
    longest = dims.index(max(dims))
    spot[longest] = (spot[longest] + 1) % dims[longest]
    return values.at[tuple(spot)].set(largest)


def block_levels(stream_key, dims, shards, smallest, largest):
    gain, own = 1.0, jax.random.fold_in(stream_key, 6)
    for position, shards_of in shards:
        steps = jnp.exp(jax.random.uniform(jax.random.fold_in(own, position), (shards_of,), jnp.float32, smallest / len(shards), largest / len(shards)))
        gain = gain * jnp.repeat(steps, dims[position] // shards_of).reshape([-1 if axis == position else 1 for axis in range(len(dims))])
    return gain


def noise(key, dims, scale, bound, cuts=(), dtype=jnp.bfloat16):
    array = jax.random.normal(key, dims, jnp.float32) * scale
    if len(cuts) > 0:
        array = block_levels(key, dims, cuts, -0.22, 0.18) * array
    return jnp.clip(array, min=-bound, max=bound).astype(dtype)


def setup_inputs(seed: int = 0) -> dict:
    key_list = jax.random.split(jax.random.key(seed), 23)
    return {
        "tokens": noise(key_list[0], (ROWS, SEQ, D), 1.0, 6.0, ((0, 32),)),
        "cotangent": noise(key_list[1], (ROWS, SEQ, D), 1.0, 6.0, ((0, 32),)),
        "route": draw_route(jax.random.fold_in(key_list[22], 71), 0),
        "remask": touch_ends((jax.random.randint(key_list[3], (HALF_ROWS, SEQ), 0, 2) < 1).astype(jnp.int32), jax.random.fold_in(key_list[3], 1), 0, 1),
        "timestep": touch_ends(jax.random.randint(key_list[4], (HALF_ROWS,), 0, STEPS), jax.random.fold_in(key_list[4], 1), 0, STEPS - 1).astype(jnp.int32),
        "enc_qkv": noise(key_list[5], (D, 3 * D), D ** -0.5, 0.25, ((0, 4),), jnp.float32),
        "enc_out": noise(key_list[6], (D, D), (max(D // 64, 1)) ** -0.5, 2.0, ((0, 4),), jnp.float32),
        "enc_up": noise(key_list[7], (D, FF), D ** -0.5, 0.25, ((0, 4),), jnp.float32),
        "enc_down": noise(key_list[8], (FF, D), FF ** -0.5, 0.125, ((0, 4),), jnp.float32),
        "enc_gains": jnp.clip(1.0 + 0.1 * jax.random.normal(key_list[9], (2, D), jnp.float32), 0.5, 1.5),
        "enc_shifts": noise(key_list[10], (2, D), 0.3, 4.0, ((1, 4),), jnp.float32),
        "dec_qkv": noise(key_list[11], (D, 3 * D), D ** -0.5, 0.25, ((0, 4),), jnp.float32),
        "dec_out": noise(key_list[12], (D, D), (max(D // 64, 1)) ** -0.5, 2.0, ((0, 4),), jnp.float32),
        "cross_query": noise(key_list[13], (D, D), D ** -0.5, 0.25, ((0, 4),), jnp.float32),
        "cross_kv": noise(key_list[14], (D, 2 * D), D ** -0.5, 0.25, ((0, 4),), jnp.float32),
        "cross_out": noise(key_list[15], (D, D), (max(D // 64, 1)) ** -0.5, 2.0, ((0, 4),), jnp.float32),
        "dec_up": noise(key_list[16], (D, FF), D ** -0.5, 0.25, ((0, 4),), jnp.float32),
        "dec_down": noise(key_list[17], (FF, D), FF ** -0.5, 0.125, ((0, 4),), jnp.float32),
        "dec_gains": jnp.clip(1.0 + 0.1 * jax.random.normal(key_list[18], (3, D), jnp.float32), 0.5, 1.5),
        "dec_shifts": noise(key_list[19], (3, D), 0.3, 4.0, ((1, 4),), jnp.float32),
        "time_table": noise(key_list[20], (STEPS, D), 1.0, 6.0, ((1, 4),), jnp.float32),
        "mask_embed": noise(key_list[21], (D,), 1.0, 6.0, ((0, 4),), jnp.float32),
    }


@jax.custom_vjp
def low(v):
    return lax.optimization_barrier(v.astype(jnp.bfloat16)).astype(jnp.float32)

@jax.custom_vjp
def low_back(v):
    return v

def low_keep(v):
    return (low(v), None)

def low_pass(kept, grad):
    return (grad,)

def back_keep(v):
    return (v, None)

def back_low(kept, grad):
    return (low(grad),)
low.defvjp(low_keep, low_pass)
low_back.defvjp(back_keep, back_low)
EPSILON = 1e-05
HIGHEST = lax.Precision.HIGHEST

def rounded(signal):
    return low(low_back(signal))

def product(left, right):
    return jnp.dot(left, right, precision=HIGHEST, preferred_element_type=jnp.float32)

def layer_norm(signal, gain_row, shift_row):
    average = lax.optimization_barrier(jnp.mean(signal, axis=-1, keepdims=True))
    centred = signal - average
    spread = lax.optimization_barrier(jnp.mean(centred * centred, axis=-1, keepdims=True))
    return centred * lax.rsqrt(spread + EPSILON) * gain_row + shift_row

def attend(query_rows, key_rows, value_rows):
    row_count, features = query_rows.shape
    head_size = features // HEADS
    query_heads = query_rows.reshape(row_count, HEADS, head_size)
    key_heads = key_rows.reshape(-1, HEADS, head_size)
    value_heads = value_rows.reshape(-1, HEADS, head_size)
    scores = low_back(jnp.einsum('qhd,khd->hqk', query_heads, key_heads, precision=HIGHEST)) * head_size ** (-0.5)
    weights = jax.nn.softmax(scores, axis=-1)
    mixed = jnp.einsum('hqk,khd->qhd', low(weights), value_heads, precision=HIGHEST)
    return rounded(mixed.reshape(row_count, features))

def self_attention(inputs_b, weight_qkv, weight_out):
    features = inputs_b.shape[1]
    joined = rounded(product(inputs_b, weight_qkv))
    mixed = attend(joined[:, :features], joined[:, features:2 * features], joined[:, 2 * features:])
    return low_back(product(mixed, weight_out))

def feed_forward(hidden_b, weight_up, weight_down):
    lifted = low_back(product(hidden_b, weight_up))
    active = low(jax.nn.gelu(lifted, approximate=True))
    return low_back(product(active, weight_down))

def encoder(source, weights):
    weight_qkv, weight_out, weight_up, weight_down, gains, shifts = weights
    hidden = layer_norm(source + self_attention(source, weight_qkv, weight_out), gains[0], shifts[0])
    return layer_norm(hidden + feed_forward(low(hidden), weight_up, weight_down), gains[1], shifts[1])

def decoder(target, memory, mask_row, step_row, weights):
    weight_qkv, weight_out, weight_query, weight_kv, weight_cross, weight_up, weight_down, gains, shifts, table, mask_vector = weights
    features = target.shape[1]
    picked = (jnp.arange(STEPS) == step_row).astype(jnp.float32)
    chosen = product(picked[None, :], table)
    embedded = jnp.where(mask_row[:, None] == 1, mask_vector[None, :], target) + chosen
    first = embedded + self_attention(low(embedded), weight_qkv, weight_out)
    hidden = layer_norm(first, gains[0], shifts[0])
    query_rows = rounded(product(low(hidden), weight_query))
    key_values = rounded(product(low(memory), weight_kv))
    mixed = attend(query_rows, key_values[:, :features], key_values[:, features:])
    middle = layer_norm(hidden + low_back(product(mixed, weight_cross)), gains[1], shifts[1])
    return layer_norm(middle + feed_forward(low(middle), weight_up, weight_down), gains[2], shifts[2])

def reference(tokens, cotangent, route, remask, timestep, enc_qkv, enc_out, enc_up, enc_down, enc_gains, enc_shifts, dec_qkv, dec_out, cross_query, cross_kv, cross_out, dec_up, dec_down, dec_gains, dec_shifts, time_table, mask_embed):
    masters = (enc_qkv, enc_out, enc_up, enc_down, enc_gains, enc_shifts, dec_qkv, dec_out, cross_query, cross_kv, cross_out, dec_up, dec_down, dec_gains, dec_shifts, time_table, mask_embed)
    counts = lax.optimization_barrier(jnp.sum(route.reshape(-1, MB, SEQ).astype(jnp.float32), axis=(0, 2)))
    total_tokens = HALF_ROWS // MB * SEQ
    scales = route.astype(jnp.float32) * total_tokens / jnp.tile(counts, HALF_ROWS // MB)[:, None]
    source = tokens[:HALF_ROWS].astype(jnp.float32)
    target = tokens[HALF_ROWS:].astype(jnp.float32)
    cot_source = cotangent[:HALF_ROWS].astype(jnp.float32)
    cot_target = cotangent[HALF_ROWS:].astype(jnp.float32) * scales[:, :, None]

    def pair(weights, source_row, target_row, mask_row, step_row):
        used = tuple((low(weight) for weight in weights))
        memory = encoder(source_row, used[:6])
        return (memory, decoder(target_row, memory, mask_row, step_row, used[6:]))

    def step_pair(carry, inputs):
        source_row, target_row, grad_source, grad_target, mask_row, step_row = inputs
        outputs, pullback = jax.vjp(lambda weights, left, right: pair(weights, left, right, mask_row, step_row), masters, source_row, target_row)
        grads, grad_left, grad_right = pullback((grad_source, grad_target))
        carry = jax.tree.map(jnp.add, carry, grads)
        return (carry, (outputs[0], outputs[1], grad_left, grad_right))
    start = jax.tree.map(jnp.zeros_like, masters)
    grads, (memories, results, grads_left, grads_right) = lax.scan(step_pair, start, (source, target, cot_source, cot_target, remask, timestep))
    layer_out = jnp.concatenate([memories, results], axis=0).astype(jnp.bfloat16)
    grad_in = jnp.concatenate([grads_left, grads_right], axis=0)
    return (layer_out, grad_in, grads[0], grads[1], grads[2], grads[3], grads[4], grads[5], grads[6], grads[7], grads[8], grads[9], grads[10], grads[11], grads[12], grads[13], grads[14], grads[15], grads[16])
```

```python
import functools

import jax
import jax.numpy as jnp
from jax import lax
from jax.experimental import pallas as pl
from jax.experimental.pallas import tpu as pltpu
from jax.sharding import PartitionSpec as P

HEADS = 8
EPSILON = 1e-05
BF = jnp.bfloat16
F32 = jnp.float32
NN = (((1,), (0,)), ((), ()))
NT = (((1,), (1,)), ((), ()))
TN = (((0,), (0,)), ((), ()))
RB = 256
LANES = 128
WIDTH = 512
MASK_ROW = 10
STEP_ROW = 11
VEC_ROWS = 12


def dot(left, right, dims=NN):
    return lax.dot_general(left, right, dims, preferred_element_type=F32)


def rows_at(r, count=RB):
    return pl.ds(pl.multiple_of(r * count, count), count)


def lanes_at(c, count=LANES):
    return pl.ds(pl.multiple_of(c * count, count), count)


def low_half(shape):
    return lax.broadcasted_iota(jnp.int32, shape, 1) < LANES // 2


def norm_rows(value):
    average = jnp.mean(value, axis=-1, keepdims=True)
    centred = value - average
    spread = jnp.mean(centred * centred, axis=-1, keepdims=True)
    inverse = lax.rsqrt(spread + EPSILON)
    return centred * inverse, inverse


def norm_rows_back(upstream, normal, inverse, gain):
    scaled = upstream * gain
    first = jnp.mean(scaled, axis=-1, keepdims=True)
    second = jnp.mean(scaled * normal, axis=-1, keepdims=True)
    return inverse * (scaled - first - normal * second)


def gelu_both(p):
    a = 0.7978845608028654
    b = 0.044715
    square = p * p
    t = jnp.tanh(p * (a + (a * b) * square))
    half = 0.5 + 0.5 * t
    slope = half + (0.5 * p) * (1.0 - t * t) * (a + (3.0 * a * b) * square)
    return p * half, slope


def kernel(
    x_in, cot_in, aux, vec, wa, wu, wd,
    lo, gin, ga, gu, gd, gacc, p_hbm, f_hbm,
    x, qkv, oa, xh, rs, hb, res, dfb, dob, cotb, big, dp, kvt, gs, gsd,
    x_sem, cot_sem, big_sem, gs_sem, gsd_sem, lo_sem, gin_sem,
):
    length, features = x.shape[1], x.shape[2]
    hidden = wu.shape[2]
    blocks = length // RB
    pairs = features // LANES
    width = features
    section = lax.axis_index("section")
    role = (section >= lax.axis_size("section") // 2).astype(jnp.int32)
    own, other = role, 1 - role

    def for_rows(body):
        def step(r, carry):
            body(rows_at(r))
            return carry

        lax.fori_loop(0, blocks, step, 0)

    def embed(layer):
        flag = layer.astype(F32)

        def body(rows):
            source = x[layer, rows, :].astype(F32)
            masked = aux[rows, 0:1] * flag > 0.5
            value = jnp.where(masked, vec[MASK_ROW], source) + vec[STEP_ROW] * flag
            res[layer, rows, :] = value
            x[layer, rows, :] = value.astype(BF)

        for_rows(body)

    def project(source, weight, target, first, last):
        for c in range(first, last):
            cols = slice(c * width, (c + 1) * width)

            def body(rows, cols=cols):
                target[rows, cols] = dot(source[rows, :], weight[:, cols]).astype(BF)

            for_rows(body)

    slots = big.shape[0]

    def attend(which):
        source, target, saved = qkv.at[which], oa.at[which], p_hbm.at[which]
        steps = pairs * blocks

        def store(t):
            slot = lax.rem(t, slots)
            return pltpu.make_async_copy(big.at[slot], saved.at[t], big_sem.at[slot])

        def step(t, carry):
            hp, qb = t // blocks, lax.rem(t, blocks)
            slot = lax.rem(t, slots)
            rows = rows_at(qb)
            q = source[rows, lanes_at(hp)] * jnp.asarray(0.125, BF)
            k = source[:, lanes_at(pairs + hp)]
            v = source[:, lanes_at(2 * pairs + hp)]

            @pl.when(t >= slots)
            def _():
                store(t - slots).wait()

            low = low_half((RB, LANES))
            zero = jnp.zeros_like(q)
            parts = []
            for j in range(2):
                s = dot(jnp.where(low if j == 0 else ~low, q, zero), k, NT)
                e = jnp.exp(s - jnp.max(s, axis=-1, keepdims=True))
                total = jnp.sum(e, axis=-1, keepdims=True)
                weights = (e * (1.0 / total)).astype(BF)
                for h in range(2):
                    big[slot, (2 * j + h) * RB : (2 * j + h + 1) * RB, :] = weights[:, h * width : (h + 1) * width]
                parts.append(dot(weights, v))
            target[rows, lanes_at(hp)] = jnp.where(low, parts[0], parts[1]).astype(BF)
            store(t).start()
            return carry

        lax.fori_loop(0, steps, step, 0)
        for t in range(steps - slots, steps):
            store(t).wait()

    def out_norm(which, res_at, xh_at, gain_row, shift_row, hb_at):
        def body(rows):
            value = dot(oa[which, rows, :], wa[which, :, 3 * width :]) + res[res_at, rows, :]
            normal, inverse = norm_rows(value)
            result = normal * vec[gain_row] + vec[shift_row]
            xh[xh_at, rows, :] = normal.astype(BF)
            rs[xh_at, rows, :] = inverse
            res[res_at, rows, :] = result
            hb[hb_at, rows, :] = result.astype(BF)

        for_rows(body)

    chunks = hidden // width

    def feed_store(layer, c):
        slot = c % 2
        return pltpu.make_async_copy(big.at[2 * slot : 2 * slot + 2], f_hbm.at[layer, c], big_sem.at[slot])

    def feed_load(layer, c):
        slot = c % 2
        return pltpu.make_async_copy(f_hbm.at[layer, c], big.at[2 * slot : 2 * slot + 2], big_sem.at[slot])

    def feed(layer, hb_at):
        for c in range(chunks):
            slot = c % 2
            cols = slice(c * width, (c + 1) * width)
            if c >= 2:
                feed_store(layer, c - 2).wait()

            def body(rows, slot=slot, cols=cols):
                value, slope = gelu_both(dot(hb[hb_at, rows, :], wu[layer, :, cols]))
                value = value.astype(BF)
                big[2 * slot, rows, :] = value
                big[2 * slot + 1, rows, :] = slope.astype(BF)
                res[layer, rows, :] += dot(value, wd[layer, cols, :])

            for_rows(body)
            feed_store(layer, c).start()
        for c in range(chunks - 2, chunks):
            feed_store(layer, c).wait()

    def final_norm(layer, xh_at, gain_row, shift_row, target):
        def body(rows):
            normal, inverse = norm_rows(res[layer, rows, :])
            xh[xh_at, rows, :] = normal.astype(BF)
            rs[xh_at, rows, :] = inverse
            target[rows, :] = (normal * vec[gain_row] + vec[shift_row]).astype(BF)

        for_rows(body)

    def norm_back(load, res_at, xh_at, gain_row, shift_row):
        def body(rows):
            upstream = load(rows)
            normal = xh[xh_at, rows, :].astype(F32)
            result = norm_rows_back(upstream, normal, rs[xh_at, rows, :], vec[gain_row])
            gacc[gain_row] += jnp.sum(upstream * normal, axis=0, keepdims=True)
            gacc[shift_row] += jnp.sum(upstream, axis=0, keepdims=True)
            res[res_at, rows, :] = result
            dfb[rows, :] = result.astype(BF)

        for_rows(body)

    def feed_back(layer, hb_at, up, down):
        feed_load(layer, 0).start()
        feed_load(layer, 1).start()
        for c in range(chunks):
            slot = c % 2
            cols = slice(c * width, (c + 1) * width)
            feed_load(layer, c).wait()

            def body(rows, slot=slot, cols=cols):
                grad = dot(dfb[rows, :], wd[layer, cols, :], NT)
                grad = (grad * big[2 * slot + 1, rows, :].astype(F32)).astype(BF)
                dp[rows, :] = grad
                res[layer, rows, :] += dot(grad, wu[layer, :, cols], NT)

            for_rows(body)
            up[:, cols] = dot(hb[hb_at], dp[...], TN).astype(BF)
            down[cols, :] = dot(big[2 * slot], dfb[...], TN).astype(BF)
            if c + 2 < chunks:
                feed_load(layer, c + 2).start()

    def attend_back(which):
        source, output, saved = qkv.at[which], oa.at[which], p_hbm.at[which]
        steps = pairs * blocks

        def fetch(t):
            slot = lax.rem(t, slots)
            return pltpu.make_async_copy(saved.at[t], big.at[slot], big_sem.at[slot])

        for t in range(slots - 1):
            fetch(t).start()

        def step(t, carry):
            hp, qb = t // blocks, lax.rem(t, blocks)
            slot = lax.rem(t, slots)
            rows = rows_at(qb)

            @pl.when(t + slots - 1 < steps)
            def _():
                fetch(t + slots - 1).start()

            fetch(t).wait()

            @pl.when(qb == 0)
            def _():
                kvt[...] = jnp.zeros_like(kvt)

            q = source[rows, lanes_at(hp)]
            k = source[:, lanes_at(pairs + hp)]
            v = source[:, lanes_at(2 * pairs + hp)]
            do = dob[rows, lanes_at(hp)]
            inner = do.astype(F32) * output[rows, lanes_at(hp)].astype(F32)
            low = low_half((RB, LANES))
            zero = jnp.zeros_like(q)
            parts = []
            for j in range(2):
                mine = low if j == 0 else ~low
                dom = jnp.where(mine, do, zero)
                delta = jnp.sum(jnp.where(mine, inner, 0.0), axis=-1, keepdims=True)
                weights = jnp.concatenate(
                    [big[slot, (2 * j + h) * RB : (2 * j + h + 1) * RB, :] for h in range(2)], axis=1
                )
                ds = (weights.astype(F32) * (dot(dom, v, NT) - delta)).astype(BF)
                kvt[1] += dot(dom, weights, TN)
                kvt[0] += dot(jnp.where(mine, q, zero), ds, TN)
                parts.append(dot(ds, k))
            source[rows, lanes_at(hp)] = (jnp.where(low, parts[0], parts[1]) * 0.125).astype(BF)

            @pl.when(qb == blocks - 1)
            def _():
                source[:, lanes_at(pairs + hp)] = jnp.transpose(kvt[0] * 0.125).astype(BF)
                source[:, lanes_at(2 * pairs + hp)] = jnp.transpose(kvt[1]).astype(BF)

            return carry

        lax.fori_loop(0, steps, step, 0)

    def grad_weight(target, first, last, left, which):
        for c in range(first, last):
            cols = slice(c * width, (c + 1) * width)
            target[:, cols] = dot(left[...], qkv[which, :, cols], TN).astype(BF)

    def out_back(which, target):
        target[:, 3 * width :] = dot(oa[which], dfb[...], TN).astype(BF)

        def body(rows):
            dob[rows, :] = dot(dfb[rows, :], wa[which, :, 3 * width :], NT).astype(BF)

        for_rows(body)

    load_x = pltpu.make_async_copy(x_in, x, x_sem)
    load_x.start()
    load_x.wait()
    gacc[...] = jnp.zeros_like(gacc)

    for layer in (own, other):
        embed(layer)
        project(x.at[layer], wa.at[layer], qkv.at[layer], 0, 3)
        attend(layer)
        out_norm(layer, layer, layer, 4 * layer, 2 + 5 * layer, layer)

    feed(0, 0)
    final_norm(0, 2, 1, 3, hb.at[2])
    send_memory = pltpu.make_async_copy(hb.at[2], lo.at[0], lo_sem.at[0])
    send_memory.start()
    load_cot = pltpu.make_async_copy(cot_in.at[1], cotb, cot_sem.at[1])
    load_cot.start()
    project(hb.at[1], wa.at[2], qkv.at[2], 0, 1)
    project(hb.at[2], wa.at[2], qkv.at[2], 1, 3)
    attend(2)
    out_norm(2, 1, 3, 5, 8, 3)
    feed(1, 3)
    final_norm(1, 4, 6, 9, dob)
    send_result = pltpu.make_async_copy(dob, lo.at[1], lo_sem.at[1])
    send_result.start()

    def result_upstream(rows):
        return cotb[rows, :].astype(F32) * aux[rows, 1:2]

    load_cot.wait()
    norm_back(result_upstream, 1, 4, 6, 9)
    load_cot = pltpu.make_async_copy(cot_in.at[0], cotb, cot_sem.at[0])
    load_cot.start()
    feed_back(1, 3, gs.at[0], gsd)
    store_up = pltpu.make_async_copy(gs.at[0], gu.at[1], gs_sem.at[0])
    store_down = pltpu.make_async_copy(gsd, gd.at[1], gsd_sem)
    store_up.start()
    store_down.start()
    norm_back(lambda rows: res[1, rows, :], 1, 3, 5, 8)
    send_result.wait()
    out_back(2, gs.at[1])
    attend_back(2)
    grad_weight(gs.at[1], 0, 1, hb.at[1], 2)
    grad_weight(gs.at[1], 1, 3, hb.at[2], 2)
    store_cross = pltpu.make_async_copy(gs.at[1], ga.at[2], gs_sem.at[1])
    store_cross.start()
    load_cot.wait()

    def cross_body(rows):
        res[1, rows, :] += dot(qkv[2, rows, :width], wa[2, :, :width], NT)
        res[0, rows, :] = cotb[rows, :].astype(F32) + dot(
            qkv[2, rows, width:], wa[2, :, width : 3 * width], NT
        )

    for_rows(cross_body)
    norm_back(lambda rows: res[0, rows, :], 0, 2, 1, 3)
    store_up.wait()
    store_down.wait()
    feed_back(0, 0, gs.at[0], gsd)
    store_up = pltpu.make_async_copy(gs.at[0], gu.at[0], gs_sem.at[0])
    store_down = pltpu.make_async_copy(gsd, gd.at[0], gsd_sem)
    store_up.start()
    store_down.start()
    store_cross.wait()
    for turn, layer in enumerate((other, own)):
        slot = 1 - turn
        flag = layer.astype(F32)
        norm_back(lambda rows: res[layer, rows, :], layer, layer, 4 * layer, 2 + 5 * layer)
        if turn == 1:
            store_up.wait()
        out_back(layer, gs.at[slot])
        attend_back(layer)
        grad_weight(gs.at[slot], 0, 3, x.at[layer], layer)
        pltpu.make_async_copy(gs.at[slot], ga.at[layer], gs_sem.at[slot]).start()

        def body(rows):
            value = res[layer, rows, :] + dot(qkv[layer, rows, :], wa[layer, :, : 3 * width], NT)
            masked = aux[rows, 0:1] * flag > 0.5
            gacc[MASK_ROW] += jnp.sum(jnp.where(masked, value, 0.0), axis=0, keepdims=True)
            gacc[STEP_ROW] += jnp.sum(value, axis=0, keepdims=True) * flag
            res[layer, rows, :] = jnp.where(masked, 0.0, value)

        for_rows(body)
        pltpu.make_async_copy(res.at[layer], gin.at[layer], gin_sem.at[turn]).start()
    for turn, layer in enumerate((other, own)):
        slot = 1 - turn
        pltpu.make_async_copy(gs.at[slot], ga.at[layer], gs_sem.at[slot]).wait()
        pltpu.make_async_copy(res.at[layer], gin.at[layer], gin_sem.at[turn]).wait()
    store_down.wait()
    send_memory.wait()


def run_pair(x2, cot2, aux, vec, wa, wu, wd):
    _, length, features = x2.shape
    hidden = wu.shape[2]
    blocks = length // RB
    pairs = features // LANES
    hbm = pl.BlockSpec(memory_space=pl.ANY)
    vmem = pl.BlockSpec(memory_space=pltpu.VMEM)
    dma = pltpu.SemaphoreType.DMA
    return pl.pallas_call(
        kernel,
        name="pair",
        out_shape=[
            jax.ShapeDtypeStruct(x2.shape, BF),
            jax.ShapeDtypeStruct(x2.shape, F32),
            jax.ShapeDtypeStruct(wa.shape, BF),
            jax.ShapeDtypeStruct(wu.shape, BF),
            jax.ShapeDtypeStruct(wd.shape, BF),
            jax.ShapeDtypeStruct(vec.shape, F32),
            jax.ShapeDtypeStruct((3, pairs * blocks, length, features), BF),
            jax.ShapeDtypeStruct((2, hidden // features, 2, length, features), BF),
        ],
        in_specs=[hbm, hbm, vmem, vmem, vmem, vmem, vmem],
        out_specs=[hbm] * 5 + [vmem] + [hbm] * 2,
        scratch_shapes=[
            pltpu.VMEM((2, length, features), BF),
            pltpu.VMEM((3, length, 3 * features), BF),
            pltpu.VMEM((3, length, features), BF),
            pltpu.VMEM((5, length, features), BF),
            pltpu.VMEM((5, length, 1), F32),
            pltpu.VMEM((4, length, features), BF),
            pltpu.VMEM((2, length, features), F32),
            pltpu.VMEM((length, features), BF),
            pltpu.VMEM((length, features), BF),
            pltpu.VMEM((length, features), BF),
            pltpu.VMEM((4, length, features), BF),
            pltpu.VMEM((length, features), BF),
            pltpu.VMEM((2, LANES, length), F32),
            pltpu.VMEM((2, features, hidden), BF),
            pltpu.VMEM((hidden, features), BF),
            dma,
            dma((2,)),
            dma((4,)),
            dma((2,)),
            dma,
            dma((2,)),
            dma((2,)),
        ],
        compiler_params=pltpu.CompilerParams(
            vmem_limit_bytes=64 << 20, has_side_effects=True
        ),
    )(x2, cot2, aux, vec, wa, wu, wd)


def per_device(
    tokens, cotangent, route, remask, timestep,
    enc_qkv, enc_out, enc_up, enc_down, enc_gains, enc_shifts,
    dec_qkv, dec_out, cross_query, cross_kv, cross_out, dec_up, dec_down, dec_gains, dec_shifts,
    time_table, mask_embed,
):
    sections = lax.axis_size("section")
    half = sections // 2
    shards = lax.axis_size("shard")
    section = lax.axis_index("section")
    shard = lax.axis_index("shard")
    role = (section >= half).astype(jnp.int32)
    batches, length, features = tokens.shape
    pair_row = ((section - half * role) * shards + shard) * batches + role
    steps = time_table.shape[0]

    def one(array, index):
        return lax.dynamic_index_in_dim(array, index, 0, keepdims=False)

    counts = jnp.sum(route.reshape(-1, batches, length).astype(F32), axis=(0, 2))
    total_tokens = float(route.shape[0] // batches * length)
    scale = one(route, pair_row).astype(F32) * total_tokens / one(counts, role)
    masked = one(remask, pair_row).astype(F32)
    lane = lax.broadcasted_iota(jnp.int32, (length, LANES), 1)
    aux = jnp.where(lane == 0, masked[:, None], jnp.where(lane == 1, scale[:, None], 0.0))

    swap = [(i, (i + half) % sections) for i in range(sections)]

    def swapped(array):
        return lax.ppermute(array, "section", swap)

    def both(array):
        mine = one(array, role)
        theirs = swapped(one(array, 1 - role))
        return jnp.stack([jnp.where(role == 0, mine, theirs), jnp.where(role == 0, theirs, mine)])

    x2, cot2 = both(tokens), both(cotangent)

    small = jnp.concatenate(
        [enc_gains, enc_shifts, dec_gains, dec_shifts, mask_embed[None, :], time_table], axis=0
    ).astype(BF)
    small = lax.all_gather(small, "shard", axis=1, tiled=True).astype(F32)
    step = one(timestep, pair_row)
    vec = jnp.concatenate([small[: MASK_ROW + 1], one(small, MASK_ROW + 1 + step)[None]], axis=0)
    wa = jnp.stack(
        [
            jnp.concatenate([enc_qkv, enc_out], axis=1),
            jnp.concatenate([dec_qkv, dec_out], axis=1),
            jnp.concatenate([cross_query, cross_kv, cross_out], axis=1),
        ]
    ).astype(BF)
    wu = jnp.stack([enc_up, dec_up]).astype(BF)
    wd = jnp.stack([enc_down, dec_down]).astype(BF)

    def gathered(array):
        return lax.all_gather(array, "shard", axis=1, tiled=True)

    lo, gin, ga, gu, gd, gacc, _, _ = run_pair(
        x2, cot2, aux, vec[:, None, :], gathered(wa), gathered(wu), gathered(wd)
    )

    def back(array):
        mine = one(array, role)
        theirs = swapped(one(array, 1 - role))
        return jnp.stack([jnp.where(role == 0, mine, theirs), jnp.where(role == 0, theirs, mine)])

    layer_out = back(lo)
    grad_in = back(gin)

    def reduced(array, axis):
        owned = lax.psum_scatter(array, "shard", scatter_dimension=axis, tiled=True)
        return lax.psum(owned.astype(F32), "section")

    ga, gu, gd = reduced(ga, 1), reduced(gu, 1), reduced(gd, 1)
    gacc = gacc[:, 0, :]
    picked = (jnp.arange(steps) == step).astype(F32)
    table = picked[:, None] * gacc[STEP_ROW][None, :]
    gv = reduced(jnp.concatenate([gacc[: MASK_ROW + 1], table], axis=0), 1)
    d = features
    return (
        layer_out, grad_in,
        ga[0, :, : 3 * d], ga[0, :, 3 * d :], gu[0], gd[0], gv[0:2], gv[2:4],
        ga[1, :, : 3 * d], ga[1, :, 3 * d :],
        ga[2, :, :d], ga[2, :, d : 3 * d], ga[2, :, 3 * d :],
        gu[1], gd[1], gv[4:7], gv[7:10], gv[MASK_ROW + 1 :], gv[MASK_ROW],
    )


def solution(mesh):
    rows = P(("section", "shard"), None, None)
    first, second, copied = P("shard", None), P(None, "shard"), P()
    return jax.shard_map(
        per_device,
        mesh=mesh,
        in_specs=(rows, rows, copied, copied, copied)
        + (first,) * 4 + (second,) * 2 + (first,) * 7 + (second,) * 3 + (P("shard"),),
        out_specs=(rows, rows)
        + (first,) * 4 + (second,) * 2 + (first,) * 7 + (second,) * 3 + (P("shard"),),
        check_vma=False,
    )
```

```python
import functools

import jax
import jax.numpy as jnp
from jax import lax
from jax.experimental import pallas as pl
from jax.experimental.pallas import tpu as pltpu
from jax.sharding import PartitionSpec as P

HEADS = 8
EPSILON = 1e-05
BF = jnp.bfloat16
F32 = jnp.float32
NN = (((1,), (0,)), ((), ()))
NT = (((1,), (1,)), ((), ()))
TN = (((0,), (0,)), ((), ()))
RB = 256
LANES = 128
WIDTH = 512
MASK_ROW = 10
STEP_ROW = 11
VEC_ROWS = 12
SMALL_ROWS = 64
MESH = pl.DeviceIdType.MESH


def dot(left, right, dims=NN):
    return lax.dot_general(left, right, dims, preferred_element_type=F32)


def rows_at(r, count=RB):
    return pl.ds(pl.multiple_of(r * count, count), count)


def lanes_at(c, count=LANES):
    return pl.ds(pl.multiple_of(c * count, count), count)


def low_half(shape):
    return lax.broadcasted_iota(jnp.int32, shape, 1) < LANES // 2


def norm_rows(value):
    average = jnp.mean(value, axis=-1, keepdims=True)
    centred = value - average
    spread = jnp.mean(centred * centred, axis=-1, keepdims=True)
    inverse = lax.rsqrt(spread + EPSILON)
    return centred * inverse, inverse


def norm_rows_back(upstream, normal, inverse, gain):
    scaled = upstream * gain
    first = jnp.mean(scaled, axis=-1, keepdims=True)
    second = jnp.mean(scaled * normal, axis=-1, keepdims=True)
    return inverse * (scaled - first - normal * second)


def gelu_both(p):
    a = 0.7978845608028654
    b = 0.044715
    square = p * p
    t = jnp.tanh(p * (a + (a * b) * square))
    half = 0.5 + 0.5 * t
    slope = half + (0.5 * p) * (1.0 - t * t) * (a + (3.0 * a * b) * square)
    return p * half, slope


def kernel(
    x_in, cot_in, aux, small_in, pick, wa_in, wu_in, wd_in,
    lo, gin, ga, gu, gd, gacc, p_hbm, f_hbm, cot_land, out_land, gin_land,
    wa, wu, wd, small, vec,
    x, qkv, oa, xh, rs, hb, res, dfb, dob, cotb, big, dp, kvt, gs, gsd,
    send_sem, recv_sem, own_sem, small_sem, swap_sem,
    cot_sem, big_sem, gs_sem, gsd_sem, lo_sem, gin_sem,
):
    length, features = x.shape[1], x.shape[2]
    hidden = wu.shape[2]
    blocks = length // RB
    pairs = features // LANES
    width = features
    section = lax.axis_index("section")
    role = (section >= lax.axis_size("section") // 2).astype(jnp.int32)
    own, other = role, 1 - role
    sections, shards = lax.axis_size("section"), lax.axis_size("shard")
    shard = lax.axis_index("shard")
    core = lax.rem(section, 2)
    side = lax.rem(section // 2, 2)
    quarter = 2 * core + side
    core_peer = (section + 1 - 2 * core, shard)
    side_peer = (section + 2 - 4 * side, shard)
    half_peer = (section + (sections // 2) * (1 - 2 * role), shard)
    turns = range(1, shards)

    def later(k):
        return lax.rem(shard + k, shards)

    def part(ref, lead, cols):
        if cols is None:
            return ref.at[lead]
        return ref.at[lead, :, cols]

    items = [
        (wa_in, wa, own, slice(0, 3 * width)),
        (wa_in, wa, own, slice(3 * width, 4 * width)),
        (wa_in, wa, other, slice(0, 4 * width)),
        (wu_in, wu, 0, slice(0, hidden)),
        (wd_in, wd, 0, slice(0, width)),
        (wa_in, wa, 2, slice(0, 4 * width)),
        (wu_in, wu, 1, slice(0, hidden)),
        (wd_in, wd, 1, slice(0, width)),
    ]

    def remote(src, dst, sems, peer):
        return pltpu.make_async_remote_copy(
            src_ref=src, dst_ref=dst, send_sem=send_sem.at[sems], recv_sem=recv_sem.at[sems],
            device_id=peer, device_id_type=MESH,
        )

    def piece(item, owner, first, count):
        _, full, lead, cols = items[item]
        size = full.shape[1] // (4 * shards)
        start = pl.multiple_of(owner * (4 * size) + first * size, size)
        return full.at[lead, pl.ds(start, count * size), cols]

    def hop(item, stage, k):
        if stage == 0:
            source, full, lead, cols = items[item]
            size = full.shape[1] // (4 * shards)
            src = source.at[lead, pl.ds(pl.multiple_of(quarter * size, size), size), cols]
            return src, piece(item, shard, quarter, 1), (section, later(k))
        if stage == 1:
            src = piece(item, later(k), quarter, 1)
            return src, src, side_peer
        src = piece(item, later(k), 2 * core, 2)
        return src, src, core_peer

    def arrival(item, stage, k):
        if stage == 0:
            return piece(item, later(shards - k), quarter, 1)
        if stage == 1:
            return piece(item, later(k), 2 * core + 1 - side, 1)
        return piece(item, later(k), 2 - 2 * core, 2)

    def send(item, stage):
        for k in turns:
            src, dst, peer = hop(item, stage, k)
            remote(src, dst, (item, stage, k - 1), peer).start()

    def take(item, stage):
        for k in turns:
            dst = arrival(item, stage, k)
            remote(dst, dst, (item, stage, k - 1), core_peer).wait_recv()

    def own_copy(item):
        source, full, lead, cols = items[item]
        size = full.shape[1] // shards
        return pltpu.make_async_copy(
            source.at[lead, :, cols],
            full.at[lead, pl.ds(pl.multiple_of(shard * size, size), size), cols],
            own_sem.at[item],
        )

    def small_copy(k):
        return pltpu.make_async_remote_copy(
            src_ref=small_in, dst_ref=small.at[shard], send_sem=small_sem.at[0, k - 1],
            recv_sem=small_sem.at[1, k - 1], device_id=(section, later(k)), device_id_type=MESH,
        )

    def swap_copy(src, dst, index):
        return pltpu.make_async_remote_copy(
            src_ref=src, dst_ref=dst, send_sem=swap_sem.at[0, index], recv_sem=swap_sem.at[1, index],
            device_id=half_peer, device_id_type=MESH,
        )

    def for_rows(body):
        def step(r, carry):
            body(rows_at(r))
            return carry

        lax.fori_loop(0, blocks, step, 0)

    def embed(layer):
        flag = layer.astype(F32)

        def body(rows):
            source = x[layer, rows, :].astype(F32)
            masked = aux[rows, 0:1] * flag > 0.5
            value = jnp.where(masked, vec[MASK_ROW], source) + vec[STEP_ROW] * flag
            res[layer, rows, :] = value
            x[layer, rows, :] = value.astype(BF)

        for_rows(body)

    def project(source, weight, target, first, last):
        for c in range(first, last):
            cols = slice(c * width, (c + 1) * width)

            def body(rows, cols=cols):
                target[rows, cols] = dot(source[rows, :], weight[:, cols]).astype(BF)

            for_rows(body)

    slots = big.shape[0]

    def attend(which, polls=()):
        source, target, saved = qkv.at[which], oa.at[which], p_hbm.at[which]
        steps = pairs * blocks

        def store(t):
            slot = lax.rem(t, slots)
            return pltpu.make_async_copy(big.at[slot], saved.at[t], big_sem.at[slot])

        def step(t, carry):
            hp, qb = t // blocks, lax.rem(t, blocks)
            slot = lax.rem(t, slots)
            rows = rows_at(qb)
            q = source[rows, lanes_at(hp)] * jnp.asarray(0.125, BF)
            k = source[:, lanes_at(pairs + hp)]
            v = source[:, lanes_at(2 * pairs + hp)]

            @pl.when(t >= slots)
            def _():
                store(t - slots).wait()

            for when, act in polls:
                pl.when(t == when)(act)

            low = low_half((RB, LANES))
            zero = jnp.zeros_like(q)
            parts = []
            for j in range(2):
                s = dot(jnp.where(low if j == 0 else ~low, q, zero), k, NT)
                e = jnp.exp(s - jnp.max(s, axis=-1, keepdims=True))
                total = jnp.sum(e, axis=-1, keepdims=True)
                weights = (e * (1.0 / total)).astype(BF)
                for h in range(2):
                    big[slot, (2 * j + h) * RB : (2 * j + h + 1) * RB, :] = weights[:, h * width : (h + 1) * width]
                parts.append(dot(weights, v))
            target[rows, lanes_at(hp)] = jnp.where(low, parts[0], parts[1]).astype(BF)
            store(t).start()
            return carry

        lax.fori_loop(0, steps, step, 0)
        for t in range(steps - slots, steps):
            store(t).wait()

    def out_norm(which, res_at, xh_at, gain_row, shift_row, hb_at):
        def body(rows):
            value = dot(oa[which, rows, :], wa[which, :, 3 * width :]) + res[res_at, rows, :]
            normal, inverse = norm_rows(value)
            result = normal * vec[gain_row] + vec[shift_row]
            xh[xh_at, rows, :] = normal.astype(BF)
            rs[xh_at, rows, :] = inverse
            res[res_at, rows, :] = result
            hb[hb_at, rows, :] = result.astype(BF)

        for_rows(body)

    chunks = hidden // width

    def feed_store(layer, c):
        slot = c % 2
        return pltpu.make_async_copy(big.at[2 * slot : 2 * slot + 2], f_hbm.at[layer, c], big_sem.at[slot])

    def feed_load(layer, c):
        slot = c % 2
        return pltpu.make_async_copy(f_hbm.at[layer, c], big.at[2 * slot : 2 * slot + 2], big_sem.at[slot])

    def feed(layer, hb_at, polls=()):
        for c in range(chunks):
            slot = c % 2
            cols = slice(c * width, (c + 1) * width)
            if c >= 2:
                feed_store(layer, c - 2).wait()

            def body(rows, slot=slot, cols=cols):
                value, slope = gelu_both(dot(hb[hb_at, rows, :], wu[layer, :, cols]))
                value = value.astype(BF)
                big[2 * slot, rows, :] = value
                big[2 * slot + 1, rows, :] = slope.astype(BF)
                res[layer, rows, :] += dot(value, wd[layer, cols, :])

            for_rows(body)
            feed_store(layer, c).start()
            for when, act in polls:
                if when == c:
                    act()
        for c in range(chunks - 2, chunks):
            feed_store(layer, c).wait()

    def final_norm(layer, xh_at, gain_row, shift_row, target):
        def body(rows):
            normal, inverse = norm_rows(res[layer, rows, :])
            xh[xh_at, rows, :] = normal.astype(BF)
            rs[xh_at, rows, :] = inverse
            target[rows, :] = (normal * vec[gain_row] + vec[shift_row]).astype(BF)

        for_rows(body)

    def norm_back(load, res_at, xh_at, gain_row, shift_row):
        def body(rows):
            upstream = load(rows)
            normal = xh[xh_at, rows, :].astype(F32)
            result = norm_rows_back(upstream, normal, rs[xh_at, rows, :], vec[gain_row])
            gacc[gain_row] += jnp.sum(upstream * normal, axis=0, keepdims=True)
            gacc[shift_row] += jnp.sum(upstream, axis=0, keepdims=True)
            res[res_at, rows, :] = result
            dfb[rows, :] = result.astype(BF)

        for_rows(body)

    def feed_back(layer, hb_at, up, down):
        feed_load(layer, 0).start()
        feed_load(layer, 1).start()
        for c in range(chunks):
            slot = c % 2
            cols = slice(c * width, (c + 1) * width)
            feed_load(layer, c).wait()

            def body(rows, slot=slot, cols=cols):
                grad = dot(dfb[rows, :], wd[layer, cols, :], NT)
                grad = (grad * big[2 * slot + 1, rows, :].astype(F32)).astype(BF)
                dp[rows, :] = grad
                res[layer, rows, :] += dot(grad, wu[layer, :, cols], NT)

            for_rows(body)
            up[:, cols] = dot(hb[hb_at], dp[...], TN).astype(BF)
            down[cols, :] = dot(big[2 * slot], dfb[...], TN).astype(BF)
            if c + 2 < chunks:
                feed_load(layer, c + 2).start()

    def attend_back(which):
        source, output, saved = qkv.at[which], oa.at[which], p_hbm.at[which]
        steps = pairs * blocks

        def fetch(t):
            slot = lax.rem(t, slots)
            return pltpu.make_async_copy(saved.at[t], big.at[slot], big_sem.at[slot])

        for t in range(slots - 1):
            fetch(t).start()

        def step(t, carry):
            hp, qb = t // blocks, lax.rem(t, blocks)
            slot = lax.rem(t, slots)
            rows = rows_at(qb)

            @pl.when(t + slots - 1 < steps)
            def _():
                fetch(t + slots - 1).start()

            fetch(t).wait()

            @pl.when(qb == 0)
            def _():
                kvt[...] = jnp.zeros_like(kvt)

            q = source[rows, lanes_at(hp)]
            k = source[:, lanes_at(pairs + hp)]
            v = source[:, lanes_at(2 * pairs + hp)]
            do = dob[rows, lanes_at(hp)]
            inner = do.astype(F32) * output[rows, lanes_at(hp)].astype(F32)
            low = low_half((RB, LANES))
            zero = jnp.zeros_like(q)
            parts = []
            for j in range(2):
                mine = low if j == 0 else ~low
                dom = jnp.where(mine, do, zero)
                delta = jnp.sum(jnp.where(mine, inner, 0.0), axis=-1, keepdims=True)
                weights = jnp.concatenate(
                    [big[slot, (2 * j + h) * RB : (2 * j + h + 1) * RB, :] for h in range(2)], axis=1
                )
                ds = (weights.astype(F32) * (dot(dom, v, NT) - delta)).astype(BF)
                kvt[1] += dot(dom, weights, TN)
                kvt[0] += dot(jnp.where(mine, q, zero), ds, TN)
                parts.append(dot(ds, k))
            source[rows, lanes_at(hp)] = (jnp.where(low, parts[0], parts[1]) * 0.125).astype(BF)

            @pl.when(qb == blocks - 1)
            def _():
                source[:, lanes_at(pairs + hp)] = jnp.transpose(kvt[0] * 0.125).astype(BF)
                source[:, lanes_at(2 * pairs + hp)] = jnp.transpose(kvt[1]).astype(BF)

            return carry

        lax.fori_loop(0, steps, step, 0)

    def grad_weight(target, first, last, left, which):
        for c in range(first, last):
            cols = slice(c * width, (c + 1) * width)
            target[:, cols] = dot(left[...], qkv[which, :, cols], TN).astype(BF)

    def out_back(which, target):
        target[:, 3 * width :] = dot(oa[which], dfb[...], TN).astype(BF)

        def body(rows):
            dob[rows, :] = dot(dfb[rows, :], wa[which, :, 3 * width :], NT).astype(BF)

        for_rows(body)

    barrier = pltpu.get_barrier_semaphore()
    peers = [(section, later(k)) for k in turns] + [core_peer, side_peer, half_peer]
    for peer in peers:
        pl.semaphore_signal(barrier, inc=1, device_id=peer, device_id_type=MESH)
    pl.semaphore_wait(barrier, len(peers))

    for k in turns:
        small_copy(k).start()
    send(0, 0)
    load_small = pltpu.make_async_copy(small_in, small.at[shard], small_sem.at[2, 0])
    load_small.start()
    load_x = pltpu.make_async_copy(x_in.at[own], x.at[own], cot_sem.at[0])
    load_x.start()
    swap_x = swap_copy(x_in.at[other], x.at[own], 0)
    swap_x.start()
    for item in range(len(items)):
        own_copy(item).start()
    send(1, 0)
    send(2, 0)
    gacc[...] = jnp.zeros_like(gacc)
    swap_cot = swap_copy(cot_in.at[other], cot_land.at[own], 1)
    swap_cot.start()
    load_cot = pltpu.make_async_copy(cot_in.at[own], cot_land.at[own], cot_sem.at[1])
    load_small.wait()
    for k in turns:
        small_copy(k).wait_recv()
    for owner in range(shards):
        values = small[owner].astype(F32)
        cols = slice(owner * LANES, (owner + 1) * LANES)
        for row in range(MASK_ROW + 1):
            vec[row, :, cols] = values[row : row + 1, :]
        vec[STEP_ROW, :, cols] = jnp.sum(values * pick[...], axis=0, keepdims=True)
    load_x.wait()
    embed(own)
    take(0, 0)
    send(0, 1)
    send(3, 0)
    take(0, 1)
    send(0, 2)
    own_copy(0).wait()
    take(0, 2)
    project(x.at[own], wa.at[own], qkv.at[own], 0, 3)
    take(1, 0)
    send(1, 1)

    def poll_0():
        take(1, 1)
        send(1, 2)

    def poll_1():
        take(2, 0)
        send(2, 1)
        send(4, 0)

    def poll_2():
        take(2, 1)
        send(2, 2)
        send(5, 0)

    attend(own, [(2, poll_0), (5, poll_1), (11, poll_2)])
    own_copy(1).wait()
    take(1, 2)
    out_norm(own, own, own, 4 * own, 2 + 5 * own, own)
    swap_copy(x_in.at[other], x.at[other], 0).wait_recv()
    embed(other)
    own_copy(2).wait()
    take(2, 2)
    project(x.at[other], wa.at[other], qkv.at[other], 0, 3)

    def poll_3():
        take(3, 0)
        send(3, 1)
        send(6, 0)

    def poll_4():
        take(3, 1)
        send(3, 2)
        take(4, 0)
        send(4, 1)
        send(7, 0)

    def poll_5():
        take(4, 1)
        send(4, 2)

    attend(other, [(1, poll_3), (7, poll_4), (13, poll_5)])
    out_norm(other, other, other, 4 * other, 2 + 5 * other, other)
    own_copy(3).wait()
    own_copy(4).wait()
    take(3, 2)
    take(4, 2)
    take(5, 0)
    send(5, 1)

    def poll_6():
        take(5, 1)
        send(5, 2)
        take(6, 0)
        send(6, 1)

    feed(0, 0, [(1, poll_6)])
    final_norm(0, 2, 1, 3, hb.at[2])
    stage_memory = pltpu.make_async_copy(hb.at[2], out_land.at[0], lo_sem.at[0])
    stage_memory.start()
    own_copy(5).wait()
    take(5, 2)
    project(hb.at[1], wa.at[2], qkv.at[2], 0, 1)
    project(hb.at[2], wa.at[2], qkv.at[2], 1, 3)

    def poll_7():
        take(6, 1)
        send(6, 2)
        take(7, 0)
        send(7, 1)

    def poll_8():
        take(7, 1)
        send(7, 2)

    attend(2, [(1, poll_7), (8, poll_8)])
    out_norm(2, 1, 3, 5, 8, 3)
    own_copy(6).wait()
    own_copy(7).wait()
    take(6, 2)
    take(7, 2)
    load_cot_1 = pltpu.make_async_copy(cot_land.at[1], cotb, cot_sem.at[0])
    load_cot_0 = pltpu.make_async_copy(cot_land.at[0], cotb, cot_sem.at[0])
    load_cot.start()
    feed(1, 3)
    load_cot.wait()
    swap_copy(cot_in.at[other], cot_land.at[other], 1).wait_recv()
    load_cot_1.start()
    final_norm(1, 4, 6, 9, dob)
    stage_memory.wait()
    stage_result = pltpu.make_async_copy(dob, out_land.at[1], lo_sem.at[1])
    stage_result.start()

    def result_upstream(rows):
        return cotb[rows, :].astype(F32) * aux[rows, 1:2]

    load_cot_1.wait()
    norm_back(result_upstream, 1, 4, 6, 9)
    load_cot_0.start()
    stage_result.wait()
    send_result = swap_copy(out_land.at[other], lo.at[own], 2)
    send_result.start()
    keep_result = pltpu.make_async_copy(out_land.at[own], lo.at[own], lo_sem.at[0])
    keep_result.start()
    feed_back(1, 3, gs.at[0], gsd)
    store_up = pltpu.make_async_copy(gs.at[0], gu.at[1], gs_sem.at[0])
    store_down = pltpu.make_async_copy(gsd, gd.at[1], gsd_sem)
    store_up.start()
    store_down.start()
    norm_back(lambda rows: res[1, rows, :], 1, 3, 5, 8)
    out_back(2, gs.at[1])
    attend_back(2)
    grad_weight(gs.at[1], 0, 1, hb.at[1], 2)
    grad_weight(gs.at[1], 1, 3, hb.at[2], 2)
    store_cross = pltpu.make_async_copy(gs.at[1], ga.at[2], gs_sem.at[1])
    store_cross.start()
    load_cot_0.wait()

    def cross_body(rows):
        res[1, rows, :] += dot(qkv[2, rows, :width], wa[2, :, :width], NT)
        res[0, rows, :] = cotb[rows, :].astype(F32) + dot(
            qkv[2, rows, width:], wa[2, :, width : 3 * width], NT
        )

    for_rows(cross_body)
    norm_back(lambda rows: res[0, rows, :], 0, 2, 1, 3)
    store_up.wait()
    store_down.wait()
    feed_back(0, 0, gs.at[0], gsd)
    store_up = pltpu.make_async_copy(gs.at[0], gu.at[0], gs_sem.at[0])
    store_down = pltpu.make_async_copy(gsd, gd.at[0], gsd_sem)
    store_up.start()
    store_down.start()
    store_cross.wait()
    for turn, layer in enumerate((other, own)):
        slot = 1 - turn
        flag = layer.astype(F32)
        norm_back(lambda rows: res[layer, rows, :], layer, layer, 4 * layer, 2 + 5 * layer)
        if turn == 1:
            store_up.wait()
        out_back(layer, gs.at[slot])
        attend_back(layer)
        grad_weight(gs.at[slot], 0, 3, x.at[layer], layer)
        pltpu.make_async_copy(gs.at[slot], ga.at[layer], gs_sem.at[slot]).start()

        def body(rows):
            value = res[layer, rows, :] + dot(qkv[layer, rows, :], wa[layer, :, : 3 * width], NT)
            masked = aux[rows, 0:1] * flag > 0.5
            gacc[MASK_ROW] += jnp.sum(jnp.where(masked, value, 0.0), axis=0, keepdims=True)
            gacc[STEP_ROW] += jnp.sum(value, axis=0, keepdims=True) * flag
            value = jnp.where(masked, 0.0, value)
            res[layer, rows, :] = value
            if turn == 0:
                cotb[rows, :] = value.astype(BF)

        for_rows(body)
        if turn == 0:
            send_gin = swap_copy(cotb, gin_land, 3)
            send_gin.start()
        else:
            keep_gin = pltpu.make_async_copy(res.at[layer], gin.at[layer], gin_sem.at[0])
            keep_gin.start()
    for turn, layer in enumerate((other, own)):
        slot = 1 - turn
        pltpu.make_async_copy(gs.at[slot], ga.at[layer], gs_sem.at[slot]).wait()
    store_down.wait()
    send_gin.wait()
    load_gin = pltpu.make_async_copy(gin_land, dob, gin_sem.at[1])
    load_gin.start()
    load_gin.wait()

    def widen(rows):
        res[other, rows, :] = dob[rows, :].astype(F32)

    for_rows(widen)
    keep_other = pltpu.make_async_copy(res.at[other], gin.at[other], gin_sem.at[1])
    keep_other.start()
    keep_other.wait()
    keep_gin.wait()
    keep_result.wait()
    send_result.wait()
    swap_x.wait_send()
    swap_cot.wait_send()
    for k in turns:
        small_copy(k).wait_send()
    for item in range(len(items)):
        for stage in range(3):
            for k in turns:
                src, dst, peer = hop(item, stage, k)
                remote(src, dst, (item, stage, k - 1), peer).wait_send()


def run_pair(x2, cot2, aux, small, pick, wa, wu, wd):
    _, length, features = x2.shape
    shards = lax.axis_size("shard")
    hidden = wu.shape[2]
    blocks = length // RB
    pairs = features // LANES
    hbm = pl.BlockSpec(memory_space=pl.ANY)
    vmem = pl.BlockSpec(memory_space=pltpu.VMEM)
    dma = pltpu.SemaphoreType.DMA
    full_a = (3, features, 4 * features)
    full_u = (2, features, hidden)
    full_d = (2, hidden, features)
    out = jax.ShapeDtypeStruct
    return pl.pallas_call(
        kernel,
        name="pair",
        out_shape=[
            out(x2.shape, BF),
            out(x2.shape, F32),
            out(full_a, BF),
            out(full_u, BF),
            out(full_d, BF),
            out((VEC_ROWS, 1, features), F32),
            out((3, pairs * blocks, length, features), BF),
            out((2, hidden // features, 2, length, features), BF),
            out(x2.shape, BF),
            out(x2.shape, BF),
            out(x2.shape[1:], BF),
        ],
        in_specs=[hbm, hbm, vmem, vmem, vmem, hbm, hbm, hbm],
        out_specs=[hbm] * 5 + [vmem] + [hbm] * 5,
        scratch_shapes=[
            pltpu.VMEM(full_a, BF),
            pltpu.VMEM(full_u, BF),
            pltpu.VMEM(full_d, BF),
            pltpu.VMEM((shards, SMALL_ROWS, LANES), BF),
            pltpu.VMEM((VEC_ROWS, 1, features), F32),
            pltpu.VMEM((2, length, features), BF),
            pltpu.VMEM((3, length, 3 * features), BF),
            pltpu.VMEM((3, length, features), BF),
            pltpu.VMEM((5, length, features), BF),
            pltpu.VMEM((5, length, 1), F32),
            pltpu.VMEM((4, length, features), BF),
            pltpu.VMEM((2, length, features), F32),
            pltpu.VMEM((length, features), BF),
            pltpu.VMEM((length, features), BF),
            pltpu.VMEM((length, features), BF),
            pltpu.VMEM((4, length, features), BF),
            pltpu.VMEM((length, features), BF),
            pltpu.VMEM((2, LANES, length), F32),
            pltpu.VMEM((2, features, hidden), BF),
            pltpu.VMEM((hidden, features), BF),
            dma((8, 3, shards - 1)),
            dma((8, 3, shards - 1)),
            dma((8,)),
            dma((3, shards - 1)),
            dma((2, 4)),
            dma((2,)),
            dma((4,)),
            dma((2,)),
            dma,
            dma((2,)),
            dma((2,)),
        ],
        compiler_params=pltpu.CompilerParams(
            vmem_limit_bytes=64 << 20, has_side_effects=True, collective_id=0
        ),
    )(x2, cot2, aux, small, pick, wa, wu, wd)


def per_device(
    tokens, cotangent, route, remask, timestep,
    enc_qkv, enc_out, enc_up, enc_down, enc_gains, enc_shifts,
    dec_qkv, dec_out, cross_query, cross_kv, cross_out, dec_up, dec_down, dec_gains, dec_shifts,
    time_table, mask_embed,
):
    sections = lax.axis_size("section")
    half = sections // 2
    shards = lax.axis_size("shard")
    section = lax.axis_index("section")
    shard = lax.axis_index("shard")
    role = (section >= half).astype(jnp.int32)
    batches, length, features = tokens.shape
    pair_row = ((section - half * role) * shards + shard) * batches + role
    steps = time_table.shape[0]

    def one(array, index):
        return lax.dynamic_index_in_dim(array, index, 0, keepdims=False)

    counts = jnp.sum(route.reshape(-1, batches, length).astype(F32), axis=(0, 2))
    total_tokens = float(route.shape[0] // batches * length)
    scale = one(route, pair_row).astype(F32) * total_tokens / one(counts, role)
    masked = one(remask, pair_row).astype(F32)
    lane = lax.broadcasted_iota(jnp.int32, (length, LANES), 1)
    aux = jnp.where(lane == 0, masked[:, None], jnp.where(lane == 1, scale[:, None], 0.0))

    small = jnp.concatenate(
        [enc_gains, enc_shifts, dec_gains, dec_shifts, mask_embed[None, :], time_table], axis=0
    ).astype(BF)
    small = jnp.pad(small, ((0, SMALL_ROWS - small.shape[0]), (0, 0)))
    step = one(timestep, pair_row)
    row = lax.broadcasted_iota(jnp.int32, (SMALL_ROWS, LANES), 0)
    pick = (row == MASK_ROW + 1 + step).astype(F32)
    wa = jnp.stack(
        [
            jnp.concatenate([enc_qkv, enc_out], axis=1),
            jnp.concatenate([dec_qkv, dec_out], axis=1),
            jnp.concatenate([cross_query, cross_kv, cross_out], axis=1),
        ]
    ).astype(BF)
    wu = jnp.stack([enc_up, dec_up]).astype(BF)
    wd = jnp.stack([enc_down, dec_down]).astype(BF)

    layer_out, grad_in, ga, gu, gd, gacc = run_pair(
        tokens, cotangent, aux, small, pick, wa, wu, wd
    )[:6]

    def reduced(array, axis):
        owned = lax.psum_scatter(array, "shard", scatter_dimension=axis, tiled=True)
        return lax.psum(owned.astype(F32), "section")

    ga, gu, gd = reduced(ga, 1), reduced(gu, 1), reduced(gd, 1)
    gacc = gacc[:, 0, :]
    picked = (jnp.arange(steps) == step).astype(F32)
    table = picked[:, None] * gacc[STEP_ROW][None, :]
    gv = reduced(jnp.concatenate([gacc[: MASK_ROW + 1], table], axis=0), 1)
    d = features
    return (
        layer_out, grad_in,
        ga[0, :, : 3 * d], ga[0, :, 3 * d :], gu[0], gd[0], gv[0:2], gv[2:4],
        ga[1, :, : 3 * d], ga[1, :, 3 * d :],
        ga[2, :, :d], ga[2, :, d : 3 * d], ga[2, :, 3 * d :],
        gu[1], gd[1], gv[4:7], gv[7:10], gv[MASK_ROW + 1 :], gv[MASK_ROW],
    )


def solution(mesh):
    rows = P(("section", "shard"), None, None)
    first, second, copied = P("shard", None), P(None, "shard"), P()
    return jax.shard_map(
        per_device,
        mesh=mesh,
        in_specs=(rows, rows, copied, copied, copied)
        + (first,) * 4 + (second,) * 2 + (first,) * 7 + (second,) * 3 + (P("shard"),),
        out_specs=(rows, rows)
        + (first,) * 4 + (second,) * 2 + (first,) * 7 + (second,) * 3 + (P("shard"),),
        check_vma=False,
    )
```

```python
import functools

import jax
import jax.numpy as jnp
from jax import lax
from jax.experimental import pallas as pl
from jax.experimental.pallas import tpu as pltpu
from jax.sharding import PartitionSpec as P

HEADS = 8
EPSILON = 1e-05
BF = jnp.bfloat16
F32 = jnp.float32
NN = (((1,), (0,)), ((), ()))
NT = (((1,), (1,)), ((), ()))
TN = (((0,), (0,)), ((), ()))
RB = 256
AB = 512
LANES = 128
WIDTH = 512
MASK_ROW = 10
STEP_ROW = 11
VEC_ROWS = 12
SMALL_ROWS = 64
UNITS = 7
MESH = pl.DeviceIdType.MESH


def dot(left, right, dims=NN):
    return lax.dot_general(left, right, dims, preferred_element_type=F32)


def rows_at(r, count=RB):
    return pl.ds(pl.multiple_of(r * count, count), count)


def lanes_at(c, count=LANES):
    return pl.ds(pl.multiple_of(c * count, count), count)


def low_half(shape):
    return lax.broadcasted_iota(jnp.int32, shape, 1) < LANES // 2


def norm_rows(value):
    average = jnp.mean(value, axis=-1, keepdims=True)
    centred = value - average
    spread = jnp.mean(centred * centred, axis=-1, keepdims=True)
    inverse = lax.rsqrt(spread + EPSILON)
    return centred * inverse, inverse


def norm_rows_back(upstream, normal, inverse, gain):
    scaled = upstream * gain
    first = jnp.mean(scaled, axis=-1, keepdims=True)
    second = jnp.mean(scaled * normal, axis=-1, keepdims=True)
    return inverse * (scaled - first - normal * second)


def gelu_both(p):
    a = 0.7978845608028654
    b = 0.044715
    square = p * p
    t = jnp.tanh(p * (a + (a * b) * square))
    half = 0.5 + 0.5 * t
    slope = half + (0.5 * p) * (1.0 - t * t) * (a + (3.0 * a * b) * square)
    return p * half, slope


def kernel(
    x_in, cot_in, aux, small_in, pick, wa_in, wu_in, wd_in,
    lo, gin, gout, gv, p_hbm, f_hbm, cot_land, out_land, gin_land, h_land,
    wa, wu, wd, small, vec,
    gacc, x, qkv, oa, xh, rs, hb, res, dfb, dob, big, dp, kvt, gs,
    r0, r1, r2, r3s, r3r, sg, sgr, sgz,
    send_sem, recv_sem, own_sem, small_sem, swap_sem,
    cot_sem, h_sem, big_sem, lo_sem, gin_sem, rs_send, rs_recv, rs_keep, sg_send, sg_recv, free,
):
    length, features = x.shape[1], x.shape[2]
    hidden = wu.shape[2]
    blocks = length // RB
    pairs = features // LANES
    width = features
    section = lax.axis_index("section")
    role = (section >= lax.axis_size("section") // 2).astype(jnp.int32)
    own, other = role, 1 - role
    sections, shards = lax.axis_size("section"), lax.axis_size("shard")
    shard = lax.axis_index("shard")
    core = lax.rem(section, 2)
    side = lax.rem(section // 2, 2)
    quarter = 2 * core + side
    core_peer = (section + 1 - 2 * core, shard)
    side_peer = (section + 2 - 4 * side, shard)
    turns = range(1, shards)

    def bit_peer(bit):
        return (section + bit * (1 - 2 * lax.rem(section // bit, 2)), shard)

    far_peers = [bit_peer(4 << b) for b in range((sections // 4).bit_length() - 1)]
    half_peer = far_peers[-1]

    def later(k):
        return lax.rem(shard + k, shards)

    def part(ref, lead, cols):
        if cols is None:
            return ref.at[lead]
        return ref.at[lead, :, cols]

    items = [
        (wa_in, wa, own, slice(0, 3 * width)),
        (wa_in, wa, own, slice(3 * width, 4 * width)),
        (wa_in, wa, other, slice(0, 4 * width)),
        (wu_in, wu, 0, slice(0, hidden)),
        (wd_in, wd, 0, slice(0, width)),
        (wa_in, wa, 2, slice(0, 4 * width)),
        (wu_in, wu, 1, slice(0, hidden)),
        (wd_in, wd, 1, slice(0, width)),
    ]

    def remote(src, dst, sems, peer):
        return pltpu.make_async_remote_copy(
            src_ref=src, dst_ref=dst, send_sem=send_sem.at[sems], recv_sem=recv_sem.at[sems],
            device_id=peer, device_id_type=MESH,
        )

    def piece(item, owner, first, count):
        _, full, lead, cols = items[item]
        size = full.shape[1] // (4 * shards)
        start = pl.multiple_of(owner * (4 * size) + first * size, size)
        return full.at[lead, pl.ds(start, count * size), cols]

    def hop(item, stage, k):
        if stage == 0:
            source, full, lead, cols = items[item]
            size = full.shape[1] // (4 * shards)
            src = source.at[lead, pl.ds(pl.multiple_of(quarter * size, size), size), cols]
            return src, piece(item, shard, quarter, 1), (section, later(k))
        if stage == 1:
            src = piece(item, later(k), quarter, 1)
            return src, src, side_peer
        src = piece(item, later(k), 2 * core, 2)
        return src, src, core_peer

    def arrival(item, stage, k):
        if stage == 0:
            return piece(item, later(shards - k), quarter, 1)
        if stage == 1:
            return piece(item, later(k), 2 * core + 1 - side, 1)
        return piece(item, later(k), 2 - 2 * core, 2)

    def send(item, stage):
        for k in turns:
            src, dst, peer = hop(item, stage, k)
            remote(src, dst, (item, stage, k - 1), peer).start()

    def take(item, stage):
        for k in turns:
            dst = arrival(item, stage, k)
            remote(dst, dst, (item, stage, k - 1), core_peer).wait_recv()

    def own_copy(item):
        source, full, lead, cols = items[item]
        size = full.shape[1] // shards
        return pltpu.make_async_copy(
            source.at[lead, :, cols],
            full.at[lead, pl.ds(pl.multiple_of(shard * size, size), size), cols],
            own_sem.at[item],
        )

    def small_copy(k):
        return pltpu.make_async_remote_copy(
            src_ref=small_in, dst_ref=small.at[shard], send_sem=small_sem.at[0, k - 1],
            recv_sem=small_sem.at[1, k - 1], device_id=(section, later(k)), device_id_type=MESH,
        )

    def swap_copy(src, dst, index):
        return pltpu.make_async_remote_copy(
            src_ref=src, dst_ref=dst, send_sem=swap_sem.at[0, index], recv_sem=swap_sem.at[1, index],
            device_id=half_peer, device_id_type=MESH,
        )

    def for_rows(body):
        def step(r, carry):
            body(rows_at(r))
            return carry

        lax.fori_loop(0, blocks, step, 0)

    lane_ids = lax.broadcasted_iota(jnp.int32, (RB, LANES), 1)

    def keep_inverse(index, rows, inverse):
        rs[rows, :] = jnp.where(lane_ids == index, inverse, rs[rows, :])

    def kept_inverse(index, rows):
        return jnp.sum(jnp.where(lane_ids == index, rs[rows, :], 0.0), axis=-1, keepdims=True)

    piece_rows = features // shards // 4
    far = len(far_peers)
    AT_Z, AT_FAR, AT_SIDE, AT_CORE = 2, 2 + len(turns), 2 + len(turns) + far, 3 + len(turns) + far
    FREE_Z, FREE_FAR = 2, 3

    def reduce_copy(unit, stage, src, dst, peer):
        return pltpu.make_async_remote_copy(
            src_ref=src, dst_ref=dst, send_sem=rs_send.at[unit, stage], recv_sem=rs_recv.at[unit, stage],
            device_id=peer, device_id_type=MESH,
        )

    def rows_of(first, count):
        return pl.ds(pl.multiple_of(first * piece_rows, piece_rows), count * piece_rows)

    def copy_core(unit):
        return reduce_copy(unit, 0, gs.at[unit % 2, :, rows_of(2 - 2 * core, 2), :], r0.at[unit % 2], core_peer)

    def copy_side(unit):
        return reduce_copy(unit, 1, r0.at[unit % 2, :, rows_of(1 - side, 1), :], r1.at[unit % 2], side_peer)

    def copy_z(unit, k):
        return reduce_copy(
            unit, AT_Z + k - 1, r1.at[unit % 2, later(k)], r2.at[unit % 2, k - 1], (section, later(k))
        )

    def far_unit(unit, b):
        return 11 - unit if unit >= 5 and b == far - 1 else unit

    def copy_far(unit, b):
        there = far_unit(unit, b)
        return pltpu.make_async_remote_copy(
            src_ref=r3s.at[unit % 2], dst_ref=r3r.at[there % 2, b],
            send_sem=rs_send.at[unit, AT_FAR + b], recv_sem=rs_recv.at[there, AT_FAR + b],
            device_id=far_peers[b], device_id_type=MESH,
        )

    def start_far(unit, b):
        if unit >= 2:
            pl.semaphore_wait(free.at[FREE_FAR + b, far_unit(unit, b) % 2], 1)
        copy_far(unit, b).start()

    def out_rows(unit, first, count):
        return gout.at[unit_at[unit], rows_of(first, count), :]

    def copy_back_side(unit):
        return reduce_copy(unit, AT_SIDE, r3s.at[unit % 2], out_rows(unit, quarter, 1), side_peer)

    def copy_keep(unit):
        return pltpu.make_async_copy(r3s.at[unit % 2], out_rows(unit, quarter, 1), rs_keep.at[unit % 2])

    def copy_back_core(unit):
        rows = out_rows(unit, 2 * core, 2)
        return reduce_copy(unit, AT_CORE, rows, rows, core_peer)

    unit_at = [4, 6, 2, 3, 5, other, own]

    def gain_credit(unit, kind, peers_of):
        if unit + 2 < UNITS:
            for peer in peers_of:
                pl.semaphore_signal(free.at[kind, unit % 2], inc=1, device_id=peer, device_id_type=MESH)

    def spend_credit(unit, kind, count=1):
        if unit >= 2:
            pl.semaphore_wait(free.at[kind, unit % 2], count)

    def sum_start(unit):
        spend_credit(unit, 0)
        copy_core(unit).start()

    def sum_core(unit):
        copy_core(unit).wait()

        def add(block, carry):
            mine = gs[unit % 2, block, rows_of(2 * core, 2), :].astype(F32)
            r0[unit % 2, block] = (r0[unit % 2, block].astype(F32) + mine).astype(BF)
            return carry

        lax.fori_loop(0, shards, add, 0)
        spend_credit(unit, 1)
        copy_side(unit).start()

    def sum_side(unit):
        copy_side(unit).wait()

        def add(block, carry):
            mine = r0[unit % 2, block, rows_of(side, 1), :].astype(F32)
            r1[unit % 2, block] = (r1[unit % 2, block].astype(F32) + mine).astype(BF)
            return carry

        lax.fori_loop(0, shards, add, 0)
        gain_credit(unit, 0, [core_peer])
        spend_credit(unit, FREE_Z, len(turns))
        for k in turns:
            copy_z(unit, k).start()

    def sum_z(unit):
        for k in turns:
            copy_z(unit, k).wait()
        total = r1[unit % 2, shard].astype(F32)
        for k in turns:
            total += r2[unit % 2, k - 1].astype(F32)
        r3s[unit % 2] = total.astype(BF)
        gain_credit(unit, 1, [side_peer])
        gain_credit(unit, FREE_Z, [(section, later(k)) for k in turns])
        start_far(unit, 0)

    def sum_far(unit):
        for b in range(far):
            copy_far(unit, b).wait_send()
            arrived = r3r.at[unit % 2, b]
            reduce_copy(unit, AT_FAR + b, arrived, arrived, far_peers[b]).wait_recv()
            total = r3s[unit % 2].astype(F32) + r3r[unit % 2, b].astype(F32)
            r3s[unit % 2] = total.astype(BF)
            gain_credit(unit, FREE_FAR + b, [far_peers[b]])
            if b + 1 < far:
                start_far(unit, b + 1)
        copy_keep(unit).start()
        copy_back_side(unit).start()

    def sum_back(unit):
        copy_keep(unit).wait()
        copy_back_side(unit).wait_send()
        arrived = out_rows(unit, 2 * core + 1 - side, 1)
        reduce_copy(unit, AT_SIDE, arrived, arrived, side_peer).wait_recv()
        copy_back_core(unit).start()

    def sum_end(unit):
        copy_back_core(unit).wait_send()
        arrived = out_rows(unit, 2 - 2 * core, 2)
        reduce_copy(unit, AT_CORE, arrived, arrived, core_peer).wait_recv()

    small_peers = [core_peer, side_peer]

    def copy_small(b):
        src = sg if b < 2 else sg.at[shard]
        dst = sgr.at[b] if b < 2 else sgz.at[len(turns) + b - 2]
        peer = small_peers[b] if b < 2 else far_peers[b - 2]
        return pltpu.make_async_remote_copy(
            src_ref=src, dst_ref=dst, send_sem=sg_send.at[len(turns) + b],
            recv_sem=sg_recv.at[len(turns) + b], device_id=peer, device_id_type=MESH,
        )

    def copy_small_z(k):
        return pltpu.make_async_remote_copy(
            src_ref=sg.at[later(k)], dst_ref=sgz.at[k - 1], send_sem=sg_send.at[k - 1],
            recv_sem=sg_recv.at[k - 1], device_id=(section, later(k)), device_id_type=MESH,
        )

    def small_start():
        for owner in range(shards):
            cols = slice(owner * LANES, (owner + 1) * LANES)
            rows = [gacc[row, :, cols] for row in range(MASK_ROW + 1)]
            rest = jnp.zeros((SMALL_ROWS - MASK_ROW - 1, LANES), F32)
            sg[owner] = jnp.concatenate(rows + [rest], axis=0) + pick[...] * gacc[STEP_ROW, :, cols]
        copy_small(0).start()

    def small_add(b):
        copy_small(b).wait()
        sg[...] += sgr[b]
        if b == 0:
            copy_small(1).start()
        else:
            for k in turns:
                copy_small_z(k).start()

    def small_z():
        for k in turns:
            copy_small_z(k).wait()
        sg[shard] += sum(sgz[k - 1] for k in turns)
        copy_small(2).start()

    def small_far():
        for b in range(far):
            copy_small(2 + b).wait()
            sg[shard] += sgz[len(turns) + b]
            if b + 1 < far:
                copy_small(3 + b).start()
        gv[...] = sg[shard]

    def embed(layer):
        flag = layer.astype(F32)

        def body(rows):
            source = x[layer, rows, :].astype(F32)
            masked = aux[rows, 0:1] * flag > 0.5
            value = jnp.where(masked, vec[MASK_ROW], source) + vec[STEP_ROW] * flag
            res[layer, rows, :] = value
            x[layer, rows, :] = value.astype(BF)

        for_rows(body)

    def project(source, weight, target, first, last):
        for c in range(first, last):
            cols = slice(c * width, (c + 1) * width)

            def body(rows, cols=cols):
                target[rows, cols] = dot(source[rows, :], weight[:, cols]).astype(BF)

            for_rows(body)

    queries = length // AB

    def attend(which, polls=()):
        source, target, saved = qkv.at[which], oa.at[which], p_hbm.at[which]
        steps = pairs * queries

        def store(t):
            slot = lax.rem(t, 2)
            return pltpu.make_async_copy(big.at[pl.ds(2 * slot, 2)], saved.at[t], big_sem.at[slot])

        def step(t, carry):
            hp, qb = t // queries, lax.rem(t, queries)
            slot = lax.rem(t, 2)
            rows = rows_at(qb, AB)
            q = source[rows, lanes_at(hp)] * jnp.asarray(0.125, BF)
            k = source[:, lanes_at(pairs + hp)]
            v = source[:, lanes_at(2 * pairs + hp)]

            @pl.when(t >= 2)
            def _():
                store(t - 2).wait()

            for when, act in polls:
                pl.when(t == when)(act)

            low = low_half((AB, LANES))
            zero = jnp.zeros_like(q)
            scores = [dot(jnp.where(low if j == 0 else ~low, q, zero), k, NT) for j in range(2)]
            parts = []
            for j in range(2):
                e = jnp.exp(scores[j] - jnp.max(scores[j], axis=-1, keepdims=True))
                weights = (e * (1.0 / jnp.sum(e, axis=-1, keepdims=True))).astype(BF)
                for h in range(2):
                    big[2 * slot + j, h * AB : (h + 1) * AB, :] = weights[:, h * width : (h + 1) * width]
                parts.append(dot(weights, v))
            target[rows, lanes_at(hp)] = jnp.where(low, parts[0], parts[1]).astype(BF)
            store(t).start()
            return carry

        lax.fori_loop(0, steps, step, 0)
        for t in range(steps - 2, steps):
            store(t).wait()

    def out_norm(which, res_at, xh_at, gain_row, shift_row, hb_at):
        def body(rows):
            value = dot(oa[which, rows, :], wa[which, :, 3 * width :]) + res[res_at, rows, :]
            normal, inverse = norm_rows(value)
            result = normal * vec[gain_row] + vec[shift_row]
            xh[xh_at, rows, :] = normal.astype(BF)
            keep_inverse(xh_at, rows, inverse)
            res[res_at, rows, :] = result
            hb[hb_at, rows, :] = result.astype(BF)

        for_rows(body)

    chunks = hidden // width

    def feed_store(layer, c):
        slot = c % 2
        return pltpu.make_async_copy(big.at[2 * slot : 2 * slot + 2], f_hbm.at[layer, c], big_sem.at[slot])

    def feed_load(layer, c):
        slot = c % 2
        return pltpu.make_async_copy(f_hbm.at[layer, c], big.at[2 * slot : 2 * slot + 2], big_sem.at[slot])

    def feed(layer, hb_at, polls=()):
        for c in range(chunks):
            slot = c % 2
            cols = slice(c * width, (c + 1) * width)
            if c >= 2:
                feed_store(layer, c - 2).wait()

            def body(rows, slot=slot, cols=cols):
                value, slope = gelu_both(dot(hb[hb_at, rows, :], wu[layer, :, cols]))
                value = value.astype(BF)
                big[2 * slot, rows, :] = value
                big[2 * slot + 1, rows, :] = slope.astype(BF)
                res[layer, rows, :] += dot(value, wd[layer, cols, :])

            for_rows(body)
            feed_store(layer, c).start()
            for when, act in polls:
                if when == c:
                    act()
        for c in range(chunks - 2, chunks):
            feed_store(layer, c).wait()

    def final_norm(layer, xh_at, gain_row, shift_row, target, kept=None):
        kept = xh.at[xh_at] if kept is None else kept

        def body(rows):
            normal, inverse = norm_rows(res[layer, rows, :])
            kept[rows, :] = normal.astype(BF)
            keep_inverse(xh_at, rows, inverse)
            target[rows, :] = (normal * vec[gain_row] + vec[shift_row]).astype(BF)

        for_rows(body)

    def norm_back(load, res_at, xh_at, gain_row, shift_row, kept=None):
        kept = xh.at[xh_at] if kept is None else kept

        def body(rows):
            upstream = load(rows)
            normal = kept[rows, :].astype(F32)
            result = norm_rows_back(upstream, normal, kept_inverse(xh_at, rows), vec[gain_row])
            gacc[gain_row] += jnp.sum(upstream * normal, axis=0, keepdims=True)
            gacc[shift_row] += jnp.sum(upstream, axis=0, keepdims=True)
            res[res_at, rows, :] = result
            dfb[rows, :] = result.astype(BF)

        for_rows(body)

    def feed_back(layer, hb_at, up, down, polls=()):
        feed_load(layer, 0).start()
        feed_load(layer, 1).start()
        for c in range(chunks):
            slot = c % 2
            cols = slice(c * width, (c + 1) * width)
            feed_load(layer, c).wait()

            def body(rows, slot=slot, cols=cols):
                grad = dot(dfb[rows, :], wd[layer, cols, :], NT)
                grad = (grad * big[2 * slot + 1, rows, :].astype(F32)).astype(BF)
                dp[rows, :] = grad
                res[layer, rows, :] += dot(grad, wu[layer, :, cols], NT)

            for_rows(body)
            by_owner(up, cols, dot(hb[hb_at], dp[...], TN))
            rest = dot(big[2 * slot], dfb[...], TN).astype(BF)
            count = width // shards
            for j in range(shards):
                down[c, :, j * width : (j + 1) * width] = rest[j * count : (j + 1) * count, :]
            if c + 2 < chunks:
                feed_load(layer, c + 2).start()
            for when, act in polls:
                if when == c:
                    act()

    def by_owner(target, cols, value):
        target[:, :, cols] = value.astype(BF).reshape(shards, features // shards, -1)

    def attend_back(which, polls=()):
        source, output, saved = qkv.at[which], oa.at[which], p_hbm.at[which]
        steps = pairs * queries

        def fetch(t):
            slot = lax.rem(t, 2)
            return pltpu.make_async_copy(saved.at[t], big.at[pl.ds(2 * slot, 2)], big_sem.at[slot])

        fetch(0).start()

        def step(t, carry):
            hp, qb = t // queries, lax.rem(t, queries)
            slot = lax.rem(t, 2)
            rows = rows_at(qb, AB)

            @pl.when(t + 1 < steps)
            def _():
                fetch(t + 1).start()

            for when, act in polls:
                pl.when(t == when)(act)

            fetch(t).wait()

            @pl.when(qb == 0)
            def _():
                kvt[...] = jnp.zeros_like(kvt)

            q = source[rows, lanes_at(hp)]
            k = source[:, lanes_at(pairs + hp)]
            v = source[:, lanes_at(2 * pairs + hp)]
            do = dob[rows, lanes_at(hp)]
            inner = do.astype(F32) * output[rows, lanes_at(hp)].astype(F32)
            low = low_half((AB, LANES))
            zero = jnp.zeros_like(q)
            parts = []
            for j in range(2):
                mine = low if j == 0 else ~low
                dom = jnp.where(mine, do, zero)
                delta = jnp.sum(jnp.where(mine, inner, 0.0), axis=-1, keepdims=True)
                weights = jnp.concatenate(
                    [big[2 * slot + j, h * AB : (h + 1) * AB, :] for h in range(2)], axis=1
                )
                ds = (weights.astype(F32) * (dot(dom, v, NT) - delta)).astype(BF)
                kvt[1] += dot(dom, weights, TN)
                kvt[0] += dot(jnp.where(mine, q, zero), ds, TN)
                parts.append(dot(ds, k))
            source[rows, lanes_at(hp)] = (jnp.where(low, parts[0], parts[1]) * 0.125).astype(BF)

            @pl.when(qb == queries - 1)
            def _():
                source[:, lanes_at(pairs + hp)] = jnp.transpose(kvt[0] * 0.125).astype(BF)
                source[:, lanes_at(2 * pairs + hp)] = jnp.transpose(kvt[1]).astype(BF)

            return carry

        lax.fori_loop(0, steps, step, 0)

    def grad_weight(target, first, last, left, which):
        for c in range(first, last):
            cols = slice(c * width, (c + 1) * width)
            by_owner(target, cols, dot(left[...], qkv[which, :, cols], TN))

    def out_grad(which, target):
        by_owner(target, slice(3 * width, 4 * width), dot(oa[which], dfb[...], TN))

    def out_back(which):

        def body(rows):
            dob[rows, :] = dot(dfb[rows, :], wa[which, :, 3 * width :], NT).astype(BF)

        for_rows(body)

    barrier = pltpu.get_barrier_semaphore()
    peers = [(section, later(k)) for k in turns] + [core_peer, side_peer] + far_peers
    for peer in peers:
        pl.semaphore_signal(barrier, inc=1, device_id=peer, device_id_type=MESH)
    pl.semaphore_wait(barrier, len(peers))

    for k in turns:
        small_copy(k).start()
    send(0, 0)
    load_small = pltpu.make_async_copy(small_in, small.at[shard], small_sem.at[2, 0])
    load_small.start()
    load_x = pltpu.make_async_copy(x_in.at[own], x.at[own], cot_sem.at[0])
    load_x.start()
    swap_x = swap_copy(x_in.at[other], x.at[own], 0)
    swap_x.start()
    for item in range(len(items)):
        own_copy(item).start()
    send(1, 0)
    send(2, 0)
    gacc[...] = jnp.zeros_like(gacc)
    swap_cot = swap_copy(cot_in.at[other], cot_land.at[own], 1)
    swap_cot.start()
    load_cot = pltpu.make_async_copy(cot_in.at[own], cot_land.at[own], cot_sem.at[1])
    load_small.wait()
    for k in turns:
        small_copy(k).wait_recv()
    for owner in range(shards):
        values = small[owner].astype(F32)
        cols = slice(owner * LANES, (owner + 1) * LANES)
        for row in range(MASK_ROW + 1):
            vec[row, :, cols] = values[row : row + 1, :]
        vec[STEP_ROW, :, cols] = jnp.sum(values * pick[...], axis=0, keepdims=True)
    load_x.wait()
    embed(own)
    take(0, 0)
    send(0, 1)
    send(3, 0)
    take(0, 1)
    send(0, 2)
    own_copy(0).wait()
    take(0, 2)
    project(x.at[own], wa.at[own], qkv.at[own], 0, 3)
    take(1, 0)
    send(1, 1)

    def poll_0():
        take(1, 1)
        send(1, 2)

    def poll_1():
        take(2, 0)
        send(2, 1)
        send(4, 0)

    def poll_2():
        take(2, 1)
        send(2, 2)
        send(5, 0)

    attend(own, [(1, poll_0), (2, poll_1), (5, poll_2)])
    own_copy(1).wait()
    take(1, 2)
    out_norm(own, own, own, 4 * own, 2 + 5 * own, own)
    swap_copy(x_in.at[other], x.at[other], 0).wait_recv()
    embed(other)
    own_copy(2).wait()
    take(2, 2)
    project(x.at[other], wa.at[other], qkv.at[other], 0, 3)

    def poll_3():
        take(3, 0)
        send(3, 1)
        send(6, 0)

    def poll_4():
        take(3, 1)
        send(3, 2)
        take(4, 0)
        send(4, 1)
        send(7, 0)

    def poll_5():
        take(4, 1)
        send(4, 2)

    attend(other, [(0, poll_3), (3, poll_4), (6, poll_5)])
    out_norm(other, other, other, 4 * other, 2 + 5 * other, other)
    own_copy(3).wait()
    own_copy(4).wait()
    take(3, 2)
    take(4, 2)
    take(5, 0)
    send(5, 1)

    def poll_6():
        take(5, 1)
        send(5, 2)
        take(6, 0)
        send(6, 1)

    h_store = pltpu.make_async_copy(hb.at[0], h_land, h_sem)
    h_load = pltpu.make_async_copy(h_land, hb.at[0], h_sem)
    h_store.start()
    feed(0, 0, [(1, poll_6)])
    h_store.wait()
    final_norm(0, 2, 1, 3, hb.at[2])
    stage_memory = pltpu.make_async_copy(hb.at[2], out_land.at[0], lo_sem.at[0])
    stage_memory.start()
    own_copy(5).wait()
    take(5, 2)
    project(hb.at[1], wa.at[2], qkv.at[2], 0, 1)
    project(hb.at[2], wa.at[2], qkv.at[2], 1, 3)

    def poll_7():
        take(6, 1)
        send(6, 2)
        take(7, 0)
        send(7, 1)

    def poll_8():
        take(7, 1)
        send(7, 2)

    attend(2, [(0, poll_7), (4, poll_8)])
    out_norm(2, 1, 3, 5, 8, 0)
    own_copy(6).wait()
    own_copy(7).wait()
    take(6, 2)
    take(7, 2)
    load_cot_1 = pltpu.make_async_copy(cot_land.at[1], dp, cot_sem.at[0])
    load_cot_0 = pltpu.make_async_copy(cot_land.at[0], dp, cot_sem.at[0])
    load_cot.start()
    feed(1, 0)
    load_cot.wait()
    swap_copy(cot_in.at[other], cot_land.at[other], 1).wait_recv()
    load_cot_1.start()
    final_norm(1, 4, 6, 9, dob, big.at[3])
    stage_memory.wait()
    stage_result = pltpu.make_async_copy(dob, out_land.at[1], lo_sem.at[1])
    stage_result.start()

    def result_upstream(rows):
        return dp[rows, :].astype(F32) * aux[rows, 1:2]

    load_cot_1.wait()
    norm_back(result_upstream, 1, 4, 6, 9, big.at[3])
    stage_result.wait()
    send_result = swap_copy(out_land.at[other], lo.at[own], 2)
    send_result.start()
    keep_result = pltpu.make_async_copy(out_land.at[own], lo.at[own], lo_sem.at[0])
    keep_result.start()
    feed_back(1, 0, gs.at[0], gs.at[1])
    h_load.start()
    load_cot_0.start()
    sum_start(0)
    sum_start(1)
    norm_back(lambda rows: res[1, rows, :], 1, 3, 5, 8)
    out_back(2)

    def polls_of(*acts):
        return [(when, functools.partial(act, unit)) for when, act, unit in acts]

    attend_back(2, polls_of((0, sum_core, 0), (0, sum_core, 1), (3, sum_side, 0), (5, sum_side, 1)))
    sum_z(0)
    out_grad(2, gs.at[0])
    grad_weight(gs.at[0], 0, 1, hb.at[1], 2)
    grad_weight(gs.at[0], 1, 3, hb.at[2], 2)
    sum_start(2)
    load_cot_0.wait()

    def cross_body(rows):
        res[1, rows, :] += dot(qkv[2, rows, :width], wa[2, :, :width], NT)
        res[0, rows, :] = dp[rows, :].astype(F32) + dot(
            qkv[2, rows, width:], wa[2, :, width : 3 * width], NT
        )

    for_rows(cross_body)
    sum_core(2)
    norm_back(lambda rows: res[0, rows, :], 0, 2, 1, 3)
    sum_z(1)
    sum_far(0)
    h_load.wait()
    feed_back(
        0, 0, gs.at[1], gs.at[0],
        polls_of(
            (0, sum_side, 2), (0, sum_far, 1), (0, sum_back, 0), (1, sum_back, 1), (1, sum_end, 0),
            (2, sum_z, 2), (2, sum_end, 1),
        ),
    )
    sum_start(3)
    sum_start(4)
    sum_far(2)
    for turn, layer in enumerate((other, own)):
        unit = 5 + turn
        slot = unit % 2
        flag = layer.astype(F32)
        norm_back(lambda rows: res[layer, rows, :], layer, layer, 4 * layer, 2 + 5 * layer)
        out_back(layer)
        if turn == 0:
            acts = polls_of(
                (0, sum_core, 3), (0, sum_core, 4), (0, sum_back, 2), (2, sum_end, 2), (3, sum_side, 3),
                (5, sum_side, 4), (6, sum_z, 3), (7, sum_far, 3),
            )
        else:
            acts = polls_of(
                (0, sum_back, 4), (1, sum_side, 5), (1, sum_end, 4), (4, sum_z, 5),
            )
        attend_back(layer, acts)
        if turn == 0:
            sum_z(4)
            sum_back(3)
        out_grad(layer, gs.at[slot])
        grad_weight(gs.at[slot], 0, 3, x.at[layer], layer)
        sum_start(unit)

        def body(rows):
            value = res[layer, rows, :] + dot(qkv[layer, rows, :], wa[layer, :, : 3 * width], NT)
            masked = aux[rows, 0:1] * flag > 0.5
            gacc[MASK_ROW] += jnp.sum(jnp.where(masked, value, 0.0), axis=0, keepdims=True)
            gacc[STEP_ROW] += jnp.sum(value, axis=0, keepdims=True) * flag
            value = jnp.where(masked, 0.0, value)
            res[layer, rows, :] = value
            if turn == 0:
                dp[rows, :] = value.astype(BF)

        for_rows(body)
        if turn == 0:
            send_gin = swap_copy(dp, gin_land, 3)
            send_gin.start()
            sum_core(unit)
            sum_far(4)
            sum_end(3)
        else:
            keep_gin = pltpu.make_async_copy(res.at[layer], gin.at[layer], gin_sem.at[0])
            keep_gin.start()
    small_start()
    sum_core(6)
    small_add(0)
    send_gin.wait()
    load_gin = pltpu.make_async_copy(gin_land, dob, gin_sem.at[1])
    load_gin.start()
    load_gin.wait()

    def widen(rows):
        res[other, rows, :] = dob[rows, :].astype(F32)

    for_rows(widen)
    keep_other = pltpu.make_async_copy(res.at[other], gin.at[other], gin_sem.at[1])
    keep_other.start()
    small_add(1)
    sum_side(6)
    small_z()
    sum_z(6)
    small_far()
    sum_far(5)
    sum_far(6)
    sum_back(5)
    sum_back(6)
    sum_end(5)
    sum_end(6)
    keep_other.wait()
    keep_gin.wait()
    keep_result.wait()
    send_result.wait()
    swap_x.wait_send()
    swap_cot.wait_send()
    for k in turns:
        small_copy(k).wait_send()
    for item in range(len(items)):
        for stage in range(3):
            for k in turns:
                src, dst, peer = hop(item, stage, k)
                remote(src, dst, (item, stage, k - 1), peer).wait_send()


def run_pair(x2, cot2, aux, small, pick, wa, wu, wd):
    _, length, features = x2.shape
    shards = lax.axis_size("shard")
    hidden = wu.shape[2]
    pairs = features // LANES
    quarters = features // shards
    far = (lax.axis_size("section") // 4).bit_length() - 1
    hbm = pl.BlockSpec(memory_space=pl.ANY)
    vmem = pl.BlockSpec(memory_space=pltpu.VMEM)
    dma = pltpu.SemaphoreType.DMA
    full_a = (3, features, 4 * features)
    full_u = (2, features, hidden)
    full_d = (2, hidden, features)
    out = jax.ShapeDtypeStruct
    return pl.pallas_call(
        kernel,
        name="pair",
        out_shape=[
            out(x2.shape, BF),
            out(x2.shape, F32),
            out((UNITS, features // shards, 4 * features), BF),
            out((SMALL_ROWS, LANES), F32),
            out((3, pairs * (length // AB), 2, length, features), BF),
            out((2, hidden // features, 2, length, features), BF),
            out(x2.shape, BF),
            out(x2.shape, BF),
            out(x2.shape[1:], BF),
            out(x2.shape[1:], BF),
        ],
        in_specs=[hbm, hbm, vmem, vmem, vmem, hbm, hbm, hbm],
        out_specs=[hbm] * 3 + [vmem] + [hbm] * 6,
        scratch_shapes=[
            pltpu.VMEM(full_a, BF),
            pltpu.VMEM(full_u, BF),
            pltpu.VMEM(full_d, BF),
            pltpu.VMEM((shards, SMALL_ROWS, LANES), BF),
            pltpu.VMEM((VEC_ROWS, 1, features), F32),
            pltpu.VMEM((VEC_ROWS, 1, features), F32),
            pltpu.VMEM((2, length, features), BF),
            pltpu.VMEM((3, length, 3 * features), BF),
            pltpu.VMEM((3, length, features), BF),
            pltpu.VMEM((4, length, features), BF),
            pltpu.VMEM((length, LANES), F32),
            pltpu.VMEM((3, length, features), BF),
            pltpu.VMEM((2, length, features), F32),
            pltpu.VMEM((length, features), BF),
            pltpu.VMEM((length, features), BF),
            pltpu.VMEM((4, length, features), BF),
            pltpu.VMEM((length, features), BF),
            pltpu.VMEM((2, LANES, length), F32),
            pltpu.VMEM((2, shards, quarters, hidden), BF),
            pltpu.VMEM((2, shards, quarters // 2, hidden), BF),
            pltpu.VMEM((2, shards, quarters // 4, hidden), BF),
            pltpu.VMEM((2, shards - 1, quarters // 4, hidden), BF),
            pltpu.VMEM((2, quarters // 4, hidden), BF),
            pltpu.VMEM((2, far, quarters // 4, hidden), BF),
            pltpu.VMEM((shards, SMALL_ROWS, LANES), F32),
            pltpu.VMEM((2, shards, SMALL_ROWS, LANES), F32),
            pltpu.VMEM((shards - 1 + far, SMALL_ROWS, LANES), F32),
            dma((8, 3, shards - 1)),
            dma((8, 3, shards - 1)),
            dma((8,)),
            dma((3, shards - 1)),
            dma((2, 4)),
            dma((2,)),
            dma,
            dma((4,)),
            dma((2,)),
            dma((2,)),
            dma((UNITS, 3 + shards + far)),
            dma((UNITS, 3 + shards + far)),
            dma((2,)),
            dma((shards + 1 + far,)),
            dma((shards + 1 + far,)),
            pltpu.SemaphoreType.REGULAR((3 + far, 2)),
        ],
        compiler_params=pltpu.CompilerParams(
            vmem_limit_bytes=64 << 20, has_side_effects=True, collective_id=0
        ),
    )(x2, cot2, aux, small, pick, wa, wu, wd)


def per_device(
    tokens, cotangent, route, remask, timestep,
    enc_qkv, enc_out, enc_up, enc_down, enc_gains, enc_shifts,
    dec_qkv, dec_out, cross_query, cross_kv, cross_out, dec_up, dec_down, dec_gains, dec_shifts,
    time_table, mask_embed,
):
    sections = lax.axis_size("section")
    half = sections // 2
    shards = lax.axis_size("shard")
    section = lax.axis_index("section")
    shard = lax.axis_index("shard")
    role = (section >= half).astype(jnp.int32)
    batches, length, features = tokens.shape
    pair_row = ((section - half * role) * shards + shard) * batches + role
    steps = time_table.shape[0]

    def one(array, index):
        return lax.dynamic_index_in_dim(array, index, 0, keepdims=False)

    counts = jnp.sum(route.reshape(-1, batches, length).astype(F32), axis=(0, 2))
    total_tokens = float(route.shape[0] // batches * length)
    scale = one(route, pair_row).astype(F32) * total_tokens / one(counts, role)
    masked = one(remask, pair_row).astype(F32)
    lane = lax.broadcasted_iota(jnp.int32, (length, LANES), 1)
    aux = jnp.where(lane == 0, masked[:, None], jnp.where(lane == 1, scale[:, None], 0.0))

    small = jnp.concatenate(
        [enc_gains, enc_shifts, dec_gains, dec_shifts, mask_embed[None, :], time_table], axis=0
    ).astype(BF)
    small = jnp.pad(small, ((0, SMALL_ROWS - small.shape[0]), (0, 0)))
    step = one(timestep, pair_row)
    row = lax.broadcasted_iota(jnp.int32, (SMALL_ROWS, LANES), 0)
    pick = (row == MASK_ROW + 1 + step).astype(F32)
    wa = jnp.stack(
        [
            jnp.concatenate([enc_qkv, enc_out], axis=1),
            jnp.concatenate([dec_qkv, dec_out], axis=1),
            jnp.concatenate([cross_query, cross_kv, cross_out], axis=1),
        ]
    ).astype(BF)
    wu = jnp.stack([enc_up, dec_up]).astype(BF)
    wd = jnp.stack([enc_down, dec_down]).astype(BF)

    layer_out, grad_in, gout, gv = run_pair(
        tokens, cotangent, aux, small, pick, wa, wu, wd
    )[:4]
    d = features

    def down(block):
        return block.reshape(-1, shards, d).transpose(1, 0, 2).reshape(-1, d).astype(F32)

    ga = [block.astype(F32) for block in gout[:5]]
    return (
        layer_out, grad_in,
        ga[0][:, : 3 * d], ga[0][:, 3 * d :], ga[3], down(gout[5]), gv[0:2], gv[2:4],
        ga[1][:, : 3 * d], ga[1][:, 3 * d :],
        ga[2][:, :d], ga[2][:, d : 3 * d], ga[2][:, 3 * d :],
        ga[4], down(gout[6]), gv[4:7], gv[7:10], gv[MASK_ROW + 1 : MASK_ROW + 1 + steps], gv[MASK_ROW],
    )


def solution(mesh):
    rows = P(("section", "shard"), None, None)
    first, second, copied = P("shard", None), P(None, "shard"), P()
    return jax.shard_map(
        per_device,
        mesh=mesh,
        in_specs=(rows, rows, copied, copied, copied)
        + (first,) * 4 + (second,) * 2 + (first,) * 7 + (second,) * 3 + (P("shard"),),
        out_specs=(rows, rows)
        + (first,) * 4 + (second,) * 2 + (first,) * 7 + (second,) * 3 + (P("shard"),),
        check_vma=False,
    )
```

```python
import functools

import jax
import jax.numpy as jnp
from jax import lax
from jax.experimental import pallas as pl
from jax.experimental.pallas import tpu as pltpu
from jax.sharding import PartitionSpec as P

HEADS = 8
EPSILON = 1e-05
BF = jnp.bfloat16
F32 = jnp.float32
NN = (((1,), (0,)), ((), ()))
NT = (((1,), (1,)), ((), ()))
TN = (((0,), (0,)), ((), ()))
RB = 256
AB = 512
LANES = 128
WIDTH = 512
MASK_ROW = 10
STEP_ROW = 11
VEC_ROWS = 12
SMALL_ROWS = 64
OWNED = 7
UNITS = 10
ITEMS = 10
MESH = pl.DeviceIdType.MESH


def dot(left, right, dims=NN):
    return lax.dot_general(left, right, dims, preferred_element_type=F32)


def rows_at(r, count=RB):
    return pl.ds(pl.multiple_of(r * count, count), count)


def lanes_at(c, count=LANES):
    return pl.ds(pl.multiple_of(c * count, count), count)


def low_half(shape):
    return lax.broadcasted_iota(jnp.int32, shape, 1) < LANES // 2


def norm_rows(value):
    average = jnp.mean(value, axis=-1, keepdims=True)
    centred = value - average
    spread = jnp.mean(centred * centred, axis=-1, keepdims=True)
    inverse = lax.rsqrt(spread + EPSILON)
    return centred * inverse, inverse


def norm_rows_back(upstream, normal, inverse, gain):
    scaled = upstream * gain
    first = jnp.mean(scaled, axis=-1, keepdims=True)
    second = jnp.mean(scaled * normal, axis=-1, keepdims=True)
    return inverse * (scaled - first - normal * second)


def gelu_both(p):
    a = 0.7978845608028654
    b = 0.044715
    square = p * p
    t = jnp.tanh(p * (a + (a * b) * square))
    half = 0.5 + 0.5 * t
    slope = half + (0.5 * p) * (1.0 - t * t) * (a + (3.0 * a * b) * square)
    return p * half, slope


def kernel(
    x_in, cot_in, route, remask, timestep,
    enc_qkv, enc_out, enc_up, enc_down, dec_qkv, dec_out,
    cross_query, cross_kv, cross_out, dec_up, dec_down,
    enc_gains, enc_shifts, dec_gains, dec_shifts, mask_embed, time_table,
    lo, gin, gout, gv, p_hbm, f_hbm, cot_land, out_land, gin_land, h_land,
    wa, wu, wd, small, vec, aux, pick, marks,
    gacc, x, qkv, oa, xh, rs, hb, res, dfb, dob, big, dp, kvt, gs,
    r0, r1, r2, r3s, r3r, sg, sgr, sgz,
    send_sem, recv_sem, load_sem, small_sem, swap_sem,
    cot_sem, h_sem, big_sem, lo_sem, gin_sem, rs_send, rs_recv, rs_keep, sg_send, sg_recv, free,
):
    length, features = x.shape[1], x.shape[2]
    hidden = wu.shape[2]
    blocks = length // RB
    pairs = features // LANES
    width = features
    section = lax.axis_index("section")
    role = (section >= lax.axis_size("section") // 2).astype(jnp.int32)
    own, other = role, 1 - role
    sections, shards = lax.axis_size("section"), lax.axis_size("shard")
    shard = lax.axis_index("shard")
    core = lax.rem(section, 2)
    side = lax.rem(section // 2, 2)
    quarter = 2 * core + side
    core_peer = (section + 1 - 2 * core, shard)
    side_peer = (section + 2 - 4 * side, shard)
    turns = range(1, shards)

    def bit_peer(bit):
        return (section + bit * (1 - 2 * lax.rem(section // bit, 2)), shard)

    far_peers = [bit_peer(4 << b) for b in range((sections // 4).bit_length() - 1)]
    half_peer = far_peers[-1]

    def later(k):
        return lax.rem(shard + k, shards)

    items = [(wa, own, slice(c * width, (c + 1) * width)) for c in range(4)] + [
        (wa, other, slice(0, 4 * width)),
        (wu, 0, slice(0, hidden)),
        (wd, 0, slice(0, width)),
        (wa, 2, slice(0, 4 * width)),
        (wu, 1, slice(0, hidden)),
        (wd, 1, slice(0, width)),
    ]

    block_rows = width // shards

    def columns(*refs):
        return [
            ref.at[:, c * width : (c + 1) * width] for ref in refs for c in range(ref.shape[1] // width)
        ]

    def row_blocks(ref):
        return [ref.at[j * block_rows : (j + 1) * block_rows, :] for j in range(shards)]

    masters = [
        columns(enc_qkv, enc_out), columns(dec_qkv, dec_out), columns(enc_up), row_blocks(enc_down),
        columns(cross_query, cross_kv, cross_out), columns(dec_up), row_blocks(dec_down),
    ]

    def staged(unit, j):
        if unit == 4:
            return kvt.at[j // 2, 0:block_rows, (j % 2) * width : (j % 2 + 1) * width]
        half, start = [(0, 0), (0, 1), (1, 0), (1, 1), None, (0, 0), (0, 1)][unit]
        first = start * 4 * block_rows + j * block_rows
        return res.at[half, first : first + block_rows, :]

    def load_master(unit, j):
        return pltpu.make_async_copy(masters[unit][j], staged(unit, j), load_sem.at[unit, j])

    def load_masters(unit):
        for j in range(4):
            load_master(unit, j).start()

    def round_master(unit, full, lead, by_rows=False):
        for j in range(4):
            load_master(unit, j).wait()
            value = staged(unit, j)[...].astype(BF)
            if by_rows:
                first = shard * (4 * block_rows) + j * block_rows
                full[lead, pl.ds(pl.multiple_of(first, block_rows), block_rows), :] = value
            else:
                first = pl.multiple_of(shard * block_rows, block_rows)
                full[lead, pl.ds(first, block_rows), j * width : (j + 1) * width] = value

    def round_layer(layer):
        for j in range(4):
            first = pl.multiple_of(layer * (4 * block_rows) + j * block_rows, block_rows)
            place = res.at[0, pl.ds(first, block_rows), :]
            pltpu.make_async_copy(place, place, load_sem.at[layer, j]).wait()
            rows = pl.ds(pl.multiple_of(shard * block_rows, block_rows), block_rows)
            wa[layer, rows, j * width : (j + 1) * width] = place[...].astype(BF)

    def remote(src, dst, sems, peer):
        return pltpu.make_async_remote_copy(
            src_ref=src, dst_ref=dst, send_sem=send_sem.at[sems], recv_sem=recv_sem.at[sems],
            device_id=peer, device_id_type=MESH,
        )

    def piece(item, owner, first, count):
        full, lead, cols = items[item]
        size = full.shape[1] // (4 * shards)
        start = pl.multiple_of(owner * (4 * size) + first * size, size)
        return full.at[lead, pl.ds(start, count * size), cols]

    def hop(item, stage, k):
        if stage == 0:
            src = piece(item, shard, quarter, 1)
            return src, src, (section, later(k))
        if stage == 1:
            src = piece(item, later(k), quarter, 1)
            return src, src, side_peer
        src = piece(item, later(k), 2 * core, 2)
        return src, src, core_peer

    def arrival(item, stage, k):
        if stage == 0:
            return piece(item, later(shards - k), quarter, 1)
        if stage == 1:
            return piece(item, later(k), 2 * core + 1 - side, 1)
        return piece(item, later(k), 2 - 2 * core, 2)

    def send(item, stage):
        for k in turns:
            src, dst, peer = hop(item, stage, k)
            remote(src, dst, (item, stage, k - 1), peer).start()

    def take(item, stage):
        for k in turns:
            dst = arrival(item, stage, k)
            remote(dst, dst, (item, stage, k - 1), core_peer).wait_recv()

    def small_copy(k):
        return pltpu.make_async_remote_copy(
            src_ref=small.at[shard], dst_ref=small.at[shard], send_sem=small_sem.at[0, k - 1],
            recv_sem=small_sem.at[1, k - 1], device_id=(section, later(k)), device_id_type=MESH,
        )

    QUARTERS = 4

    def part_rows(i):
        return slice(i * length // QUARTERS, (i + 1) * length // QUARTERS)

    def send_lo(source, i):
        return swap_copy(source.at[part_rows(i), :], lo.at[own, part_rows(i), :], 2 + i)

    def send_gin(i):
        return swap_copy(dp.at[part_rows(i), :], gin_land.at[part_rows(i), :], 2 + QUARTERS + i)

    def swap_copy(src, dst, index):
        return pltpu.make_async_remote_copy(
            src_ref=src, dst_ref=dst, send_sem=swap_sem.at[0, index], recv_sem=swap_sem.at[1, index],
            device_id=half_peer, device_id_type=MESH,
        )

    def for_rows(body):
        def step(r, carry):
            body(rows_at(r))
            return carry

        lax.fori_loop(0, blocks, step, 0)

    lane_ids = lax.broadcasted_iota(jnp.int32, (RB, LANES), 1)

    def keep_inverse(index, rows, inverse):
        rs[rows, :] = jnp.where(lane_ids == index, inverse, rs[rows, :])

    def kept_inverse(index, rows):
        return jnp.sum(jnp.where(lane_ids == index, rs[rows, :], 0.0), axis=-1, keepdims=True)

    piece_rows = features // shards // 4
    far = len(far_peers)
    AT_Z, AT_FAR, AT_BACK, AT_CORE = 2, 2 + len(turns), 2 + len(turns) + far, 3 + len(turns) + far
    FREE_Z, FREE_FAR = 2, 3
    trio = 3 * LANES
    unit_set = [0, 1, 0, 1, 0, 1, 0, 0, 0, 0]
    first_set = [0, 1, 2, 0, 1, 2, 0, 0, 0, 0]
    unit_cols = [slice(0, hidden)] * 6 + [
        slice(3 * width, hidden), slice(0, 2 * trio), slice(2 * trio, 3 * trio), slice(3 * trio, 4 * trio)
    ]
    unit_far_first = [u in (1, 4) for u in range(UNITS)]
    unit_at = [4, 6, 2, 3, 5, other] + [own] * 4
    next_unit = {0: 2, 1: 3, 2: 4, 3: 5, 4: 6}
    next_first = {0: 3, 1: 4, 2: 5, 3: 6}
    parts_of_own = [6, 7, 8, 9]

    def first_bit(unit):
        return role if unit_far_first[unit] else side

    def first_peer(unit):
        return half_peer if unit_far_first[unit] else side_peer

    def far_list(unit):
        return [side_peer] + far_peers[:-1] if unit_far_first[unit] else far_peers

    def reduce_copy(unit, stage, src, dst, peer):
        return pltpu.make_async_remote_copy(
            src_ref=src, dst_ref=dst, send_sem=rs_send.at[unit, stage], recv_sem=rs_recv.at[unit, stage],
            device_id=peer, device_id_type=MESH,
        )

    def rows_of(first, count):
        return pl.ds(pl.multiple_of(first * piece_rows, piece_rows), count * piece_rows)

    def copy_core(unit):
        where, cols = unit_set[unit], unit_cols[unit]
        src = gs.at[where, :, rows_of(2 - 2 * core, 2), cols]
        return reduce_copy(unit, 0, src, r0.at[where, :, :, cols], core_peer)

    def copy_first(unit):
        where, cols = unit_set[unit], unit_cols[unit]
        src = r0.at[where, :, rows_of(1 - first_bit(unit), 1), cols]
        return reduce_copy(unit, 1, src, r1.at[first_set[unit], :, :, cols], first_peer(unit))

    def copy_z(unit, k):
        where, cols = unit_set[unit], unit_cols[unit]
        return reduce_copy(
            unit, AT_Z + k - 1, r1.at[first_set[unit], later(k), :, cols], r2.at[where, k - 1, :, cols],
            (section, later(k)),
        )

    def crosses(unit, b):
        return unit >= 5 and b == far - 1

    def copy_far(unit, b):
        where, cols = unit_set[unit], unit_cols[unit]
        there = 1 - where if crosses(unit, b) else where
        return reduce_copy(
            unit, AT_FAR + b, r3s.at[where, :, cols], r3r.at[there, b, :, cols], far_list(unit)[b]
        )

    def spend(unit, kind, where, count=1):
        if unit >= 2 and unit <= 6:
            pl.semaphore_wait(free.at[kind, where], count)

    def gain(unit, kind, peers_of):
        following = (next_first if kind == 1 else next_unit).get(unit)
        where = (first_set if kind == 1 else unit_set)[unit]
        if following is not None:
            for peer in peers_of(following):
                pl.semaphore_signal(free.at[kind, where], inc=1, device_id=peer, device_id_type=MESH)

    def start_far(unit, b):
        where = unit_set[unit]
        spend(unit, FREE_FAR + b, 1 - where if crosses(unit, b) else where)
        copy_far(unit, b).start()

    def take_far(unit, b):
        if not crosses(unit, b):
            copy_far(unit, b).wait_recv()
        elif unit == 5:
            for part in parts_of_own:
                cols = unit_cols[part]
                arrived = r3r.at[1, b, :, cols]
                reduce_copy(part, AT_FAR + b, arrived, arrived, half_peer).wait_recv()
        elif unit == 6:
            arrived = r3r.at[0, b]
            reduce_copy(5, AT_FAR + b, arrived, arrived, half_peer).wait_recv()

    def out_rows(unit, first, count):
        return gout.at[unit_at[unit], rows_of(first, count), unit_cols[unit]]

    def copy_back(unit):
        mine = 2 * core + first_bit(unit)
        src = r3s.at[unit_set[unit], :, unit_cols[unit]]
        return reduce_copy(unit, AT_BACK, src, out_rows(unit, mine, 1), first_peer(unit))

    def copy_keep(unit):
        mine = 2 * core + first_bit(unit)
        src = r3s.at[unit_set[unit], :, unit_cols[unit]]
        return pltpu.make_async_copy(src, out_rows(unit, mine, 1), rs_keep.at[unit])

    def copy_back_core(unit):
        rows = out_rows(unit, 2 * core, 2)
        return reduce_copy(unit, AT_CORE, rows, rows, core_peer)

    def sum_start(unit):
        spend(unit, 0, unit_set[unit])
        copy_core(unit).start()

    def sum_core(unit):
        where, cols = unit_set[unit], unit_cols[unit]
        copy_core(unit).wait()

        def add(block, carry):
            mine = gs[where, block, rows_of(2 * core, 2), cols].astype(F32)
            r0[where, block, :, cols] = (r0[where, block, :, cols].astype(F32) + mine).astype(BF)
            return carry

        lax.fori_loop(0, shards, add, 0)
        if unit >= 3:
            spend(unit, 1, first_set[unit])
        copy_first(unit).start()

    def sum_first(unit):
        where, cols = unit_set[unit], unit_cols[unit]
        copy_first(unit).wait()

        def add(block, carry):
            mine = r0[where, block, rows_of(first_bit(unit), 1), cols].astype(F32)
            held = r1[first_set[unit], block, :, cols].astype(F32)
            r1[first_set[unit], block, :, cols] = (held + mine).astype(BF)
            return carry

        lax.fori_loop(0, shards, add, 0)
        gain(unit, 0, lambda following: [core_peer])
        spend(unit, FREE_Z, where, len(turns))
        for k in turns:
            copy_z(unit, k).start()

    def sum_z(unit):
        where, cols = unit_set[unit], unit_cols[unit]
        for k in turns:
            copy_z(unit, k).wait()
        total = r1[first_set[unit], shard, :, cols].astype(F32)
        for k in turns:
            total += r2[where, k - 1, :, cols].astype(F32)
        r3s[where, :, cols] = total.astype(BF)
        gain(unit, 1, lambda following: [first_peer(following)])
        gain(unit, FREE_Z, lambda following: [(section, later(k)) for k in turns])
        start_far(unit, 0)

    def sum_far(unit):
        where, cols = unit_set[unit], unit_cols[unit]
        for b in range(far):
            copy_far(unit, b).wait_send()
            take_far(unit, b)
            total = r3s[where, :, cols].astype(F32) + r3r[where, b, :, cols].astype(F32)
            r3s[where, :, cols] = total.astype(BF)
            gain(unit, FREE_FAR + b, lambda following, b=b: [far_list(following)[b]])
            if b + 1 < far:
                start_far(unit, b + 1)
        copy_keep(unit).start()
        copy_back(unit).start()

    def sum_back(unit):
        copy_keep(unit).wait()
        copy_back(unit).wait_send()
        arrived = out_rows(unit, 2 * core + 1 - first_bit(unit), 1)
        reduce_copy(unit, AT_BACK, arrived, arrived, first_peer(unit)).wait_recv()
        copy_back_core(unit).start()

    def sum_end(unit):
        copy_back_core(unit).wait_send()
        arrived = out_rows(unit, 2 - 2 * core, 2)
        reduce_copy(unit, AT_CORE, arrived, arrived, core_peer).wait_recv()

    small_peers = [core_peer] + far_peers + [side_peer]
    SMALL_SIDE = len(small_peers) - 1

    def copy_small(b):
        src = sg.at[shard] if b == SMALL_SIDE else sg
        dst = sgz.at[len(turns)] if b == SMALL_SIDE else sgr.at[b]
        return pltpu.make_async_remote_copy(
            src_ref=src, dst_ref=dst, send_sem=sg_send.at[len(turns) + b],
            recv_sem=sg_recv.at[len(turns) + b], device_id=small_peers[b], device_id_type=MESH,
        )

    def copy_small_z(k):
        return pltpu.make_async_remote_copy(
            src_ref=sg.at[later(k)], dst_ref=sgz.at[k - 1], send_sem=sg_send.at[k - 1],
            recv_sem=sg_recv.at[k - 1], device_id=(section, later(k)), device_id_type=MESH,
        )

    def small_start():
        for owner in range(shards):
            cols = slice(owner * LANES, (owner + 1) * LANES)
            rows = [gacc[row, :, cols] for row in range(MASK_ROW + 1)]
            rest = jnp.zeros((SMALL_ROWS - MASK_ROW - 1, LANES), F32)
            sg[owner] = jnp.concatenate(rows + [rest], axis=0) + pick[...] * gacc[STEP_ROW, :, cols]
        copy_small(0).start()

    def small_add(b):
        copy_small(b).wait()
        sg[...] += sgr[b]
        if b + 1 < SMALL_SIDE:
            copy_small(b + 1).start()
        else:
            for k in turns:
                copy_small_z(k).start()

    def small_z():
        for k in turns:
            copy_small_z(k).wait()
        sg[shard] += sum(sgz[k - 1] for k in turns)
        copy_small(SMALL_SIDE).start()

    def small_end():
        copy_small(SMALL_SIDE).wait()
        gv[...] = sg[shard] + sgz[len(turns)]

    def embed(layer):
        flag = layer.astype(F32)

        def body(rows):
            source = x[layer, rows, :].astype(F32)
            masked = aux[rows, 0:1] * flag > 0.5
            value = jnp.where(masked, vec[MASK_ROW], source) + vec[STEP_ROW] * flag
            res[layer, rows, :] = value
            x[layer, rows, :] = value.astype(BF)

        for_rows(body)

    def project(source, weight, target, first, last):
        for c in range(first, last):
            cols = slice(c * width, (c + 1) * width)

            def body(rows, cols=cols):
                target[rows, cols] = dot(source[rows, :], weight[:, cols]).astype(BF)

            for_rows(body)

    queries = length // AB

    def attend(which, polls=()):
        source, target, saved = qkv.at[which], oa.at[which], p_hbm.at[which]
        steps = pairs * queries

        def store(t):
            slot = lax.rem(t, 2)
            return pltpu.make_async_copy(big.at[pl.ds(2 * slot, 2)], saved.at[t], big_sem.at[slot])

        def step(t, carry):
            hp, qb = t // queries, lax.rem(t, queries)
            slot = lax.rem(t, 2)
            rows = rows_at(qb, AB)
            q = source[rows, lanes_at(hp)] * jnp.asarray(0.125, BF)
            k = source[:, lanes_at(pairs + hp)]
            v = source[:, lanes_at(2 * pairs + hp)]

            @pl.when(t >= 2)
            def _():
                store(t - 2).wait()

            for when, act in polls:
                pl.when(t == when)(act)

            low = low_half((AB, LANES))
            zero = jnp.zeros_like(q)
            scores = [dot(jnp.where(low if j == 0 else ~low, q, zero), k, NT) for j in range(2)]
            parts = []
            for j in range(2):
                e = jnp.exp(scores[j] - jnp.max(scores[j], axis=-1, keepdims=True))
                weights = (e * (1.0 / jnp.sum(e, axis=-1, keepdims=True))).astype(BF)
                for h in range(2):
                    big[2 * slot + j, h * AB : (h + 1) * AB, :] = weights[:, h * width : (h + 1) * width]
                parts.append(dot(weights, v))
            target[rows, lanes_at(hp)] = jnp.where(low, parts[0], parts[1]).astype(BF)
            store(t).start()
            return carry

        lax.fori_loop(0, steps, step, 0)
        for t in range(steps - 2, steps):
            store(t).wait()

    def out_norm(which, res_at, xh_at, gain_row, shift_row, hb_at):
        def body(rows):
            value = dot(oa[which, rows, :], wa[which, :, 3 * width :]) + res[res_at, rows, :]
            normal, inverse = norm_rows(value)
            result = normal * vec[gain_row] + vec[shift_row]
            xh[xh_at, rows, :] = normal.astype(BF)
            keep_inverse(xh_at, rows, inverse)
            res[res_at, rows, :] = result
            hb[hb_at, rows, :] = result.astype(BF)

        for_rows(body)

    chunks = hidden // width

    def feed_store(layer, c):
        slot = c % 2
        return pltpu.make_async_copy(big.at[2 * slot : 2 * slot + 2], f_hbm.at[layer, c], big_sem.at[slot])

    def feed_load(layer, c):
        slot = c % 2
        return pltpu.make_async_copy(f_hbm.at[layer, c], big.at[2 * slot : 2 * slot + 2], big_sem.at[slot])

    def feed(layer, hb_at, polls=()):
        for c in range(chunks):
            slot = c % 2
            cols = slice(c * width, (c + 1) * width)
            if c >= 2:
                feed_store(layer, c - 2).wait()

            def body(rows, slot=slot, cols=cols):
                value, slope = gelu_both(dot(hb[hb_at, rows, :], wu[layer, :, cols]))
                value = value.astype(BF)
                big[2 * slot, rows, :] = value
                big[2 * slot + 1, rows, :] = slope.astype(BF)
                res[layer, rows, :] += dot(value, wd[layer, cols, :])

            for_rows(body)
            feed_store(layer, c).start()
            for when, act in polls:
                if when == c:
                    act()
        for c in range(chunks - 2, chunks):
            feed_store(layer, c).wait()

    def final_norm(layer, xh_at, gain_row, shift_row, target, kept=None):
        kept = xh.at[xh_at] if kept is None else kept

        def body(rows):
            normal, inverse = norm_rows(res[layer, rows, :])
            kept[rows, :] = normal.astype(BF)
            keep_inverse(xh_at, rows, inverse)
            target[rows, :] = (normal * vec[gain_row] + vec[shift_row]).astype(BF)

        for_rows(body)

    def norm_back(load, res_at, xh_at, gain_row, shift_row, kept=None):
        kept = xh.at[xh_at] if kept is None else kept

        def body(rows):
            upstream = load(rows)
            normal = kept[rows, :].astype(F32)
            result = norm_rows_back(upstream, normal, kept_inverse(xh_at, rows), vec[gain_row])
            gacc[gain_row] += jnp.sum(upstream * normal, axis=0, keepdims=True)
            gacc[shift_row] += jnp.sum(upstream, axis=0, keepdims=True)
            res[res_at, rows, :] = result
            dfb[rows, :] = result.astype(BF)

        for_rows(body)

    def feed_back(layer, hb_at, up, down, polls=()):
        feed_load(layer, 0).start()
        feed_load(layer, 1).start()
        for c in range(chunks):
            slot = c % 2
            cols = slice(c * width, (c + 1) * width)
            feed_load(layer, c).wait()

            def body(rows, slot=slot, cols=cols):
                grad = dot(dfb[rows, :], wd[layer, cols, :], NT)
                grad = (grad * big[2 * slot + 1, rows, :].astype(F32)).astype(BF)
                dp[rows, :] = grad
                res[layer, rows, :] += dot(grad, wu[layer, :, cols], NT)

            for_rows(body)
            by_owner(up, cols, dot(hb[hb_at], dp[...], TN))
            rest = dot(big[2 * slot], dfb[...], TN).astype(BF)
            count = width // shards
            for j in range(shards):
                down[c, :, j * width : (j + 1) * width] = rest[j * count : (j + 1) * count, :]
            if c + 2 < chunks:
                feed_load(layer, c + 2).start()
            for when, act in polls:
                if when == c:
                    act()

    def by_owner(target, cols, value):
        target[:, :, cols] = value.astype(BF).reshape(shards, features // shards, -1)

    def attend_back(which, polls=()):
        source, output, saved = qkv.at[which], oa.at[which], p_hbm.at[which]
        steps = pairs * queries

        def fetch(t):
            slot = lax.rem(t, 2)
            return pltpu.make_async_copy(saved.at[t], big.at[pl.ds(2 * slot, 2)], big_sem.at[slot])

        fetch(0).start()

        def step(t, carry):
            hp, qb = t // queries, lax.rem(t, queries)
            slot = lax.rem(t, 2)
            rows = rows_at(qb, AB)

            @pl.when(t + 1 < steps)
            def _():
                fetch(t + 1).start()

            for when, act in polls:
                pl.when(t == when)(act)

            fetch(t).wait()

            @pl.when(qb == 0)
            def _():
                kvt[...] = jnp.zeros_like(kvt)

            q = source[rows, lanes_at(hp)]
            k = source[:, lanes_at(pairs + hp)]
            v = source[:, lanes_at(2 * pairs + hp)]
            do = dob[rows, lanes_at(hp)]
            inner = do.astype(F32) * output[rows, lanes_at(hp)].astype(F32)
            low = low_half((AB, LANES))
            zero = jnp.zeros_like(q)
            parts = []
            for j in range(2):
                mine = low if j == 0 else ~low
                dom = jnp.where(mine, do, zero)
                delta = jnp.sum(jnp.where(mine, inner, 0.0), axis=-1, keepdims=True)
                weights = jnp.concatenate(
                    [big[2 * slot + j, h * AB : (h + 1) * AB, :] for h in range(2)], axis=1
                )
                ds = (weights.astype(F32) * (dot(dom, v, NT) - delta)).astype(BF)
                kvt[1] += dot(dom, weights, TN)
                kvt[0] += dot(jnp.where(mine, q, zero), ds, TN)
                parts.append(dot(ds, k))
            source[rows, lanes_at(hp)] = (jnp.where(low, parts[0], parts[1]) * 0.125).astype(BF)

            @pl.when(qb == queries - 1)
            def _():
                source[:, lanes_at(pairs + hp)] = jnp.transpose(kvt[0] * 0.125).astype(BF)
                source[:, lanes_at(2 * pairs + hp)] = jnp.transpose(kvt[1]).astype(BF)

            return carry

        lax.fori_loop(0, steps, step, 0)

    def grad_weight(target, first, last, left, which):
        for c in range(first, last):
            cols = slice(c * width, (c + 1) * width)
            by_owner(target, cols, dot(left[...], qkv[which, :, cols], TN))

    def grad_trio(target, left, which, hp):
        blocks_of = [qkv[which, :, lanes_at(n * pairs + hp)] for n in range(3)]
        value = dot(left[...], jnp.concatenate(blocks_of, axis=1), TN)
        by_owner(target, slice(hp * trio, (hp + 1) * trio), value)

    def out_grad(which, target):
        by_owner(target, slice(3 * width, 4 * width), dot(oa[which], dfb[...], TN))

    def out_back(which):

        def body(rows):
            dob[rows, :] = dot(dfb[rows, :], wa[which, :, 3 * width :], NT).astype(BF)

        for_rows(body)

    barrier = pltpu.get_barrier_semaphore()
    peers = [(section, later(k)) for k in turns] + [core_peer, side_peer] + far_peers
    for peer in peers:
        pl.semaphore_signal(barrier, inc=1, device_id=peer, device_id_type=MESH)
    for unit in range(5):
        load_masters(unit)
    load_x = pltpu.make_async_copy(x_in.at[own], x.at[own], cot_sem.at[0])
    load_x.start()
    gacc[...] = jnp.zeros_like(gacc)

    rows = [enc_gains[...], enc_shifts[...], dec_gains[...], dec_shifts[...], mask_embed[...], time_table[...]]
    count = sum(row.shape[0] for row in rows)
    rows.append(jnp.zeros((SMALL_ROWS - count, LANES), F32))
    small[shard] = jnp.concatenate(rows, axis=0).astype(BF)
    pair_row = ((section - (sections // 2) * role) * shards + shard) * 2 + role
    row_ids = lax.broadcasted_iota(jnp.int32, (SMALL_ROWS, LANES), 0)
    pick[...] = (row_ids == MASK_ROW + 1 + timestep[pair_row]).astype(F32)
    round_layer(own)
    pl.semaphore_wait(barrier, len(peers))

    for k in turns:
        small_copy(k).start()
    for item in range(4):
        send(item, 0)
    swap_x = swap_copy(x_in.at[other], x.at[own], 0)
    swap_x.start()
    round_layer(other)
    send(4, 0)
    load_masters(5)
    load_masters(6)
    round_master(2, wu, 0)
    send(5, 0)
    round_master(3, wd, 0, True)
    send(6, 0)
    round_master(4, wa, 2)
    send(7, 0)
    round_master(5, wu, 1)
    send(8, 0)
    round_master(6, wd, 1, True)
    send(9, 0)
    swap_cot = swap_copy(cot_in.at[other], cot_land, 1)
    swap_cot.start()

    batch = marks.shape[1]
    total_rows = route.shape[0]
    mine = jnp.zeros((2, length), F32)
    tally = jnp.zeros((1, 1), F32)
    for first in range(0, total_rows, batch):
        for n, array in enumerate((route, remask)):
            copy = pltpu.make_async_copy(array.at[first : first + batch, :], marks.at[n], lo_sem.at[n])
            copy.start()
            copy.wait()
        ids = lax.broadcasted_iota(jnp.int32, (batch, length), 0) + first
        routed = marks[0].astype(F32)
        same = jnp.where(lax.rem(ids, 2) == role, routed, 0.0)
        tally += jnp.sum(jnp.sum(same, axis=0, keepdims=True), axis=1, keepdims=True)
        picked = [
            jnp.sum(jnp.where(ids == pair_row, value, 0.0), axis=0, keepdims=True)
            for value in (marks[1].astype(F32), routed)
        ]
        mine += jnp.concatenate(picked, axis=0)
    scale = mine[1:2, :] * float(total_rows // 2 * length) / tally
    wide_ids = lax.broadcasted_iota(jnp.int32, (LANES, length), 0)
    wide = jnp.where(wide_ids == 0, mine[0:1, :], jnp.where(wide_ids == 1, scale, 0.0))
    aux[...] = jnp.transpose(wide)

    for k in turns:
        small_copy(k).wait_recv()
    for owner in range(shards):
        values = small[owner].astype(F32)
        cols = slice(owner * LANES, (owner + 1) * LANES)
        for row in range(MASK_ROW + 1):
            vec[row, :, cols] = values[row : row + 1, :]
        vec[STEP_ROW, :, cols] = jnp.sum(values * pick[...], axis=0, keepdims=True)
    load_x.wait()
    embed(own)

    def pass_side(item):
        take(item, 0)
        send(item, 1)

    def pass_core(item):
        take(item, 1)
        send(item, 2)

    def ready(item):
        take(item, 2)

    def polls_of(*acts):
        return [(when, functools.partial(act, item)) for when, act, item in acts]

    pass_side(0)
    pass_side(1)
    pass_core(0)
    pass_side(2)
    pass_core(1)
    for c in range(3):
        ready(c)
        project(x.at[own], wa.at[own], qkv.at[own], c, c + 1)
        if c == 0:
            pass_core(2)
            pass_side(3)
    attend(own, polls_of((2, pass_core, 3), (4, pass_side, 4)))
    ready(3)
    out_norm(own, own, own, 4 * own, 2 + 5 * own, own)
    swap_copy(x_in.at[other], x.at[other], 0).wait_recv()
    pass_core(4)
    pass_side(5)
    embed(other)
    ready(4)
    project(x.at[other], wa.at[other], qkv.at[other], 0, 3)
    attend(other, polls_of((4, pass_core, 5), (4, pass_side, 6)))
    out_norm(other, other, other, 4 * other, 2 + 5 * other, other)
    pass_core(6)
    pass_side(7)
    ready(5)
    h_store = pltpu.make_async_copy(hb.at[0], h_land, h_sem)
    h_load = pltpu.make_async_copy(h_land, hb.at[0], h_sem)
    h_store.start()
    ready(6)
    feed(0, 0, polls_of((3, pass_core, 7), (3, pass_side, 8)))
    h_store.wait()
    final_norm(0, 2, 1, 3, hb.at[2])
    keep_memory = pltpu.make_async_copy(hb.at[2], lo.at[own], lo_sem.at[0])
    pl.when(role == 0)(keep_memory.start)
    for i in range(QUARTERS):
        pl.when(role == 1)(send_lo(hb.at[2], i).start)
    ready(7)
    project(hb.at[1], wa.at[2], qkv.at[2], 0, 1)
    project(hb.at[2], wa.at[2], qkv.at[2], 1, 3)
    attend(2, polls_of((4, pass_core, 8), (4, pass_side, 9)))
    out_norm(2, 1, 3, 5, 8, 0)
    pass_core(9)
    ready(8)
    ready(9)
    def load_cot(layer):
        here = pltpu.make_async_copy(cot_in.at[own], dp, cot_sem.at[1])
        there = pltpu.make_async_copy(cot_land, dp, cot_sem.at[1])
        pl.when(own == layer)(here.start)
        pl.when(own != layer)(there.start)
        return here

    swap_copy(cot_in.at[other], cot_land, 1).wait_recv()
    load_result_cot = load_cot(1)
    feed(1, 0)
    final_norm(1, 4, 6, 9, dob, big.at[3])
    keep_result = pltpu.make_async_copy(dob, lo.at[own], lo_sem.at[0])
    stage_result = pltpu.make_async_copy(dob, out_land, lo_sem.at[1])
    pl.when(role == 1)(keep_result.start)
    stage_result.start()

    def result_upstream(rows):
        return dp[rows, :].astype(F32) * aux[rows, 1:2]

    load_result_cot.wait()
    norm_back(result_upstream, 1, 4, 6, 9, big.at[3])
    stage_result.wait()
    keep_result.wait()
    feed_back(1, 0, gs.at[0], gs.at[1])
    h_load.start()
    load_memory_cot = load_cot(0)
    sum_start(0)
    sum_start(1)
    norm_back(lambda rows: res[1, rows, :], 1, 3, 5, 8)
    out_back(2)

    def lo_part(i):
        pl.when(role == 0)(send_lo(out_land, i).start)

    attend_back(
        2,
        polls_of((1, sum_core, 0), (1, sum_core, 1), (6, sum_first, 0), (6, sum_first, 1), (6, lo_part, 0)),
    )
    out_grad(2, gs.at[0])
    grad_weight(gs.at[0], 0, 1, hb.at[1], 2)
    grad_weight(gs.at[0], 1, 3, hb.at[2], 2)
    sum_start(2)
    load_memory_cot.wait()

    def cross_body(rows):
        res[1, rows, :] += dot(qkv[2, rows, :width], wa[2, :, :width], NT)
        res[0, rows, :] = dp[rows, :].astype(F32) + dot(
            qkv[2, rows, width:], wa[2, :, width : 3 * width], NT
        )

    for_rows(cross_body)
    sum_core(2)
    norm_back(lambda rows: res[0, rows, :], 0, 2, 1, 3)
    sum_z(0)
    h_load.wait()
    feed_back(
        0, 0, gs.at[1], gs.at[0],
        polls_of(
            (0, sum_far, 0), (0, lo_part, 1), (1, sum_z, 1), (2, sum_back, 0),
            (2, sum_first, 2), (2, sum_far, 1), (2, lo_part, 2), (3, sum_back, 1), (3, sum_end, 0),
        ),
    )
    sum_start(3)
    sum_start(4)
    sum_end(1)
    def gin_part(i):
        send_gin(i).start()

    for turn, layer in enumerate((other, own)):
        slot = 1 - turn
        flag = layer.astype(F32)
        source = x.at[layer]
        target = gs.at[slot]
        norm_back(lambda rows: res[layer, rows, :], layer, layer, 4 * layer, 2 + 5 * layer)
        out_back(layer)

        def last_part(unit):
            for hp in {7: (0, 1), 8: (2,), 9: (3,)}[unit]:
                grad_trio(target, source, layer, hp)
            sum_start(unit)

        if turn == 0:
            acts = polls_of(
                (0, sum_z, 2), (1, sum_core, 3), (1, sum_core, 4), (2, sum_far, 2), (4, sum_back, 2),
                (5, sum_end, 2), (6, lo_part, 3), (7, sum_first, 3), (7, sum_first, 4),
            )
        else:
            out_grad(layer, target)
            sum_start(6)
            acts = polls_of(
                (0, sum_far, 3), (0, gin_part, 1), (1, sum_core, 6), (2, sum_back, 3), (2, sum_z, 4),
                (2, gin_part, 2), (3, sum_end, 3), (4, sum_first, 5), (4, last_part, 7), (4, sum_far, 4),
                (5, sum_first, 6), (5, sum_core, 7), (5, gin_part, 3), (6, sum_back, 4),
                (6, last_part, 8), (7, sum_end, 4), (7, sum_core, 8),
            )
        attend_back(layer, acts)
        if turn == 0:
            out_grad(layer, target)
            for hp in range(pairs):
                grad_trio(target, source, layer, hp)
            sum_start(5)
        else:
            last_part(9)
            sum_first(7)
            sum_z(5)

        def body(rows):
            value = res[layer, rows, :] + dot(qkv[layer, rows, :], wa[layer, :, : 3 * width], NT)
            masked = aux[rows, 0:1] * flag > 0.5
            gacc[MASK_ROW] += jnp.sum(jnp.where(masked, value, 0.0), axis=0, keepdims=True)
            gacc[STEP_ROW] += jnp.sum(value, axis=0, keepdims=True) * flag
            value = jnp.where(masked, 0.0, value)
            res[layer, rows, :] = value
            if turn == 0:
                dp[rows, :] = value.astype(BF)

        for_rows(body)
        if turn == 0:
            sum_core(5)
            sum_z(3)
            gin_part(0)
        else:
            keep_gin = pltpu.make_async_copy(res.at[layer], gin.at[layer], gin_sem.at[0])
            keep_gin.start()
    sum_core(9)
    small_start()
    sum_first(8)
    small_add(0)
    for i in range(QUARTERS):
        send_gin(i).wait()
    load_gin = pltpu.make_async_copy(gin_land, dob, gin_sem.at[1])
    load_gin.start()
    load_gin.wait()

    def widen(rows):
        res[other, rows, :] = dob[rows, :].astype(F32)

    for_rows(widen)
    keep_other = pltpu.make_async_copy(res.at[other], gin.at[other], gin_sem.at[1])
    keep_other.start()
    sum_first(9)
    sum_z(6)
    sum_far(6)
    sum_z(7)
    for b in range(1, far + 1):
        small_add(b)
    sum_z(8)
    sum_far(7)
    sum_z(9)
    sum_far(8)
    small_z()
    sum_far(9)
    sum_far(5)
    sum_back(6)
    sum_back(7)
    sum_back(8)
    small_end()
    sum_back(9)
    sum_back(5)
    for unit in (6, 7, 8, 9, 5):
        sum_end(unit)
    keep_other.wait()
    keep_gin.wait()
    for i in range(QUARTERS):
        send_lo(out_land, i).wait()
    swap_x.wait_send()
    swap_cot.wait_send()
    for k in turns:
        small_copy(k).wait_send()
    for item in range(len(items)):
        for stage in range(3):
            for k in turns:
                src, dst, peer = hop(item, stage, k)
                remote(src, dst, (item, stage, k - 1), peer).wait_send()


def run_pair(tokens, cotangent, route, remask, timestep, masters, small):
    _, length, features = tokens.shape
    shards = lax.axis_size("shard")
    hidden = masters[2].shape[1]
    pairs = features // LANES
    quarters = features // shards
    far = (lax.axis_size("section") // 4).bit_length() - 1
    hbm = pl.BlockSpec(memory_space=pl.ANY)
    vmem = pl.BlockSpec(memory_space=pltpu.VMEM)
    smem = pl.BlockSpec(memory_space=pltpu.SMEM)
    dma = pltpu.SemaphoreType.DMA
    full_a = (3, features, 4 * features)
    full_u = (2, features, hidden)
    full_d = (2, hidden, features)
    out = jax.ShapeDtypeStruct
    one = out(tokens.shape[1:], BF)
    return pl.pallas_call(
        kernel,
        name="pair",
        out_shape=[
            out(tokens.shape, BF),
            out(tokens.shape, F32),
            out((OWNED, features // shards, 4 * features), BF),
            out((SMALL_ROWS, LANES), F32),
            out((3, pairs * (length // AB), 2, length, features), BF),
            out((2, hidden // features, 2, length, features), BF),
            one, one, one, one,
        ],
        in_specs=[hbm] * 4 + [smem] + [hbm] * len(masters) + [vmem] * len(small),
        out_specs=[hbm] * 3 + [vmem] + [hbm] * 6,
        scratch_shapes=[
            pltpu.VMEM(full_a, BF),
            pltpu.VMEM(full_u, BF),
            pltpu.VMEM(full_d, BF),
            pltpu.VMEM((shards, SMALL_ROWS, LANES), BF),
            pltpu.VMEM((VEC_ROWS, 1, features), F32),
            pltpu.VMEM((length, LANES), F32),
            pltpu.VMEM((SMALL_ROWS, LANES), F32),
            pltpu.VMEM((2, min(32, route.shape[0]), length), jnp.int32),
            pltpu.VMEM((VEC_ROWS, 1, features), F32),
            pltpu.VMEM((2, length, features), BF),
            pltpu.VMEM((3, length, 3 * features), BF),
            pltpu.VMEM((3, length, features), BF),
            pltpu.VMEM((4, length, features), BF),
            pltpu.VMEM((length, LANES), F32),
            pltpu.VMEM((3, length, features), BF),
            pltpu.VMEM((2, length, features), F32),
            pltpu.VMEM((length, features), BF),
            pltpu.VMEM((length, features), BF),
            pltpu.VMEM((4, length, features), BF),
            pltpu.VMEM((length, features), BF),
            pltpu.VMEM((2, LANES, length), F32),
            pltpu.VMEM((2, shards, quarters, hidden), BF),
            pltpu.VMEM((2, shards, quarters // 2, hidden), BF),
            pltpu.VMEM((3, shards, quarters // 4, hidden), BF),
            pltpu.VMEM((2, shards - 1, quarters // 4, hidden), BF),
            pltpu.VMEM((2, quarters // 4, hidden), BF),
            pltpu.VMEM((2, far, quarters // 4, hidden), BF),
            pltpu.VMEM((shards, SMALL_ROWS, LANES), F32),
            pltpu.VMEM((1 + far, shards, SMALL_ROWS, LANES), F32),
            pltpu.VMEM((shards, SMALL_ROWS, LANES), F32),
            dma((ITEMS, 3, shards - 1)),
            dma((ITEMS, 3, shards - 1)),
            dma((OWNED, 4)),
            dma((3, shards - 1)),
            dma((2, 10)),
            dma((2,)),
            dma,
            dma((4,)),
            dma((2,)),
            dma((2,)),
            dma((UNITS, 3 + shards + far)),
            dma((UNITS, 3 + shards + far)),
            dma((UNITS,)),
            dma((shards + 1 + far,)),
            dma((shards + 1 + far,)),
            pltpu.SemaphoreType.REGULAR((3 + far, 3)),
        ],
        compiler_params=pltpu.CompilerParams(
            vmem_limit_bytes=64 << 20, has_side_effects=True, collective_id=0
        ),
    )(tokens, cotangent, route, remask, timestep, *masters, *small)


def finish_kernel(
    gout, gv,
    enc_qkv, enc_out, enc_up, enc_down, enc_gains, enc_shifts,
    dec_qkv, dec_out, cross_query, cross_kv, cross_out, dec_up, dec_down, dec_gains, dec_shifts,
    time_table, mask_embed,
):
    width = enc_out.shape[1]
    pairs = width // LANES
    for unit, qkv, out in ((0, enc_qkv, enc_out), (1, dec_qkv, dec_out)):
        for hp in range(pairs):
            for n in range(3):
                to, at = (n * pairs + hp) * LANES, (hp * 3 + n) * LANES
                qkv[:, to : to + LANES] = gout[unit, :, at : at + LANES].astype(F32)
        out[...] = gout[unit, :, 3 * width :].astype(F32)
    cross_query[...] = gout[2, :, :width].astype(F32)
    cross_kv[...] = gout[2, :, width : 3 * width].astype(F32)
    cross_out[...] = gout[2, :, 3 * width :].astype(F32)
    enc_up[...] = gout[3].astype(F32)
    dec_up[...] = gout[4].astype(F32)
    for unit, down in ((5, enc_down), (6, dec_down)):
        count = gout.shape[1]
        for j in range(down.shape[0] // count):
            down[j * count : (j + 1) * count, :] = gout[unit, :, j * width : (j + 1) * width].astype(F32)
    enc_gains[...] = gv[0:2, :]
    enc_shifts[...] = gv[2:4, :]
    dec_gains[...] = gv[4:7, :]
    dec_shifts[...] = gv[7:10, :]
    mask_embed[...] = gv[MASK_ROW : MASK_ROW + 1, :]
    time_table[...] = gv[MASK_ROW + 1 : MASK_ROW + 1 + time_table.shape[0], :]


def per_device(
    tokens, cotangent, route, remask, timestep,
    enc_qkv, enc_out, enc_up, enc_down, enc_gains, enc_shifts,
    dec_qkv, dec_out, cross_query, cross_kv, cross_out, dec_up, dec_down, dec_gains, dec_shifts,
    time_table, mask_embed,
):
    masters = (
        enc_qkv, enc_out, enc_up, enc_down, dec_qkv, dec_out,
        cross_query, cross_kv, cross_out, dec_up, dec_down,
    )
    mask_row = mask_embed[None, :]
    small = (enc_gains, enc_shifts, dec_gains, dec_shifts, mask_row, time_table)
    layer_out, grad_in, gout, gv = run_pair(
        tokens, cotangent, route, remask, timestep, masters, small
    )[:4]
    owned = (
        enc_qkv, enc_out, enc_up, enc_down, enc_gains, enc_shifts,
        dec_qkv, dec_out, cross_query, cross_kv, cross_out, dec_up, dec_down, dec_gains, dec_shifts,
        time_table, mask_row,
    )
    vmem = pl.BlockSpec(memory_space=pltpu.VMEM)
    grads = pl.pallas_call(
        finish_kernel,
        name="finish",
        out_shape=[jax.ShapeDtypeStruct(array.shape, F32) for array in owned],
        in_specs=[vmem] * 2,
        out_specs=[vmem] * len(owned),
        compiler_params=pltpu.CompilerParams(vmem_limit_bytes=48 << 20),
    )(gout, gv)
    return (layer_out, grad_in, *grads[:-1], grads[-1][0])


def solution(mesh):
    rows = P(("section", "shard"), None, None)
    first, second, copied = P("shard", None), P(None, "shard"), P()
    return jax.shard_map(
        per_device,
        mesh=mesh,
        in_specs=(rows, rows, copied, copied, copied)
        + (first,) * 4 + (second,) * 2 + (first,) * 7 + (second,) * 3 + (P("shard"),),
        out_specs=(rows, rows)
        + (first,) * 4 + (second,) * 2 + (first,) * 7 + (second,) * 3 + (P("shard"),),
        check_vma=False,
    )
```

```python
import functools

import jax
import jax.numpy as jnp
from jax import lax
from jax.experimental import pallas as pl
from jax.experimental.pallas import tpu as pltpu
from jax.sharding import PartitionSpec as P

HEADS = 8
EPSILON = 1e-05
BF = jnp.bfloat16
F32 = jnp.float32
NN = (((1,), (0,)), ((), ()))
NT = (((1,), (1,)), ((), ()))
TN = (((0,), (0,)), ((), ()))
RB = 256
AB = 512
LANES = 128
WIDTH = 512
MASK_ROW = 10
STEP_ROW = 11
VEC_ROWS = 12
MASK_LANE = 8
SCALE_LANE = 9
SMALL_ROWS = 64
OWNED = 7
UNITS = 12
ITEMS = 10
MESH = pl.DeviceIdType.MESH


def dot(left, right, dims=NN):
    return lax.dot_general(left, right, dims, preferred_element_type=F32)


def rows_at(r, count=RB):
    return pl.ds(pl.multiple_of(r * count, count), count)


def lanes_at(c, count=LANES):
    return pl.ds(pl.multiple_of(c * count, count), count)


def low_half(shape):
    return lax.broadcasted_iota(jnp.int32, shape, 1) < LANES // 2


def norm_rows(value):
    average = jnp.mean(value, axis=-1, keepdims=True)
    centred = value - average
    spread = jnp.mean(centred * centred, axis=-1, keepdims=True)
    inverse = lax.rsqrt(spread + EPSILON)
    return centred * inverse, inverse


def norm_rows_back(upstream, normal, inverse, gain):
    scaled = upstream * gain
    first = jnp.mean(scaled, axis=-1, keepdims=True)
    second = jnp.mean(scaled * normal, axis=-1, keepdims=True)
    return inverse * (scaled - first - normal * second)


def gelu_both(p):
    a = 0.7978845608028654
    b = 0.044715
    u = p * (a + (a * b) * (p * p))
    half = 0.5 + 0.5 * jnp.tanh(u)
    slope = half + (half - half * half) * (6.0 * u - (4.0 * a) * p)
    return p * half, slope


def kernel(
    x_in, cot_in, route, remask, timestep,
    enc_qkv, enc_out, enc_up, enc_down, dec_qkv, dec_out,
    cross_query, cross_kv, cross_out, dec_up, dec_down,
    enc_gains, enc_shifts, dec_gains, dec_shifts, mask_embed, time_table,
    lo, gin, gout, gv, p_hbm, f_hbm, cot_land, out_land, gin_land, h_land,
    wa, wu, wd, small, vec, pick, marks,
    gacc, x, qkv, oa, xh, rs, hb, res, dfb, dob, big, dp, kvt, gs,
    r0, r1, r2, r3s, r3r, sg, sgr, sgz,
    send_sem, recv_sem, load_sem, small_sem, swap_sem,
    cot_sem, h_sem, big_sem, lo_sem, gin_sem, rs_send, rs_recv, rs_keep, sg_send, sg_recv, free,
):
    length, features = x.shape[1], x.shape[2]
    hidden = wu.shape[2]
    blocks = length // RB
    pairs = features // LANES
    width = features
    section = lax.axis_index("section")
    role = (section >= lax.axis_size("section") // 2).astype(jnp.int32)
    own, other = role, 1 - role
    sections, shards = lax.axis_size("section"), lax.axis_size("shard")
    shard = lax.axis_index("shard")
    core = lax.rem(section, 2)
    side = lax.rem(section // 2, 2)
    quarter = 2 * core + side
    core_peer = (section + 1 - 2 * core, shard)
    side_peer = (section + 2 - 4 * side, shard)
    turns = range(1, shards)

    def bit_peer(bit):
        return (section + bit * (1 - 2 * lax.rem(section // bit, 2)), shard)

    far_peers = [bit_peer(4 << b) for b in range((sections // 4).bit_length() - 1)]
    half_peer = far_peers[-1]

    def later(k):
        return lax.rem(shard + k, shards)

    items = [(wa, own, slice(c * width, (c + 1) * width)) for c in range(4)] + [
        (wa, other, slice(0, 4 * width)),
        (wu, 0, slice(0, hidden)),
        (wd, 0, slice(0, width)),
        (wa, 2, slice(0, 4 * width)),
        (wu, 1, slice(0, hidden)),
        (wd, 1, slice(0, width)),
    ]

    block_rows = width // shards

    def columns(*refs):
        return [
            ref.at[:, c * width : (c + 1) * width] for ref in refs for c in range(ref.shape[1] // width)
        ]

    def row_blocks(ref):
        return [ref.at[j * block_rows : (j + 1) * block_rows, :] for j in range(shards)]

    masters = [
        columns(enc_qkv, enc_out), columns(dec_qkv, dec_out), columns(enc_up), row_blocks(enc_down),
        columns(cross_query, cross_kv, cross_out), columns(dec_up), row_blocks(dec_down),
    ]

    def staged(unit, j):
        if unit == 4:
            return kvt.at[j // 2, 0:block_rows, (j % 2) * width : (j % 2 + 1) * width]
        half, start = [(0, 0), (0, 1), (1, 0), (1, 1), None, (0, 0), (0, 1)][unit]
        first = start * 4 * block_rows + j * block_rows
        return res.at[half, first : first + block_rows, :]

    def load_master(unit, j):
        return pltpu.make_async_copy(masters[unit][j], staged(unit, j), load_sem.at[unit, j])

    def load_masters(unit):
        for j in range(4):
            load_master(unit, j).start()

    def round_master(unit, full, lead, by_rows=False):
        for j in range(4):
            load_master(unit, j).wait()
            value = staged(unit, j)[...].astype(BF)
            if by_rows:
                first = shard * (4 * block_rows) + j * block_rows
                full[lead, pl.ds(pl.multiple_of(first, block_rows), block_rows), :] = value
            else:
                first = pl.multiple_of(shard * block_rows, block_rows)
                full[lead, pl.ds(first, block_rows), j * width : (j + 1) * width] = value

    def round_layer(layer):
        for j in range(4):
            first = pl.multiple_of(layer * (4 * block_rows) + j * block_rows, block_rows)
            place = res.at[0, pl.ds(first, block_rows), :]
            pltpu.make_async_copy(place, place, load_sem.at[layer, j]).wait()
            rows = pl.ds(pl.multiple_of(shard * block_rows, block_rows), block_rows)
            wa[layer, rows, j * width : (j + 1) * width] = place[...].astype(BF)

    def remote(src, dst, sems, peer):
        return pltpu.make_async_remote_copy(
            src_ref=src, dst_ref=dst, send_sem=send_sem.at[sems], recv_sem=recv_sem.at[sems],
            device_id=peer, device_id_type=MESH,
        )

    def piece(item, owner, first, count):
        full, lead, cols = items[item]
        size = full.shape[1] // (4 * shards)
        start = pl.multiple_of(owner * (4 * size) + first * size, size)
        return full.at[lead, pl.ds(start, count * size), cols]

    def hop(item, stage, k):
        if stage == 0:
            src = piece(item, shard, quarter, 1)
            return src, src, (section, later(k))
        if stage == 1:
            src = piece(item, later(k), quarter, 1)
            return src, src, side_peer
        src = piece(item, later(k), 2 * core, 2)
        return src, src, core_peer

    def arrival(item, stage, k):
        if stage == 0:
            return piece(item, later(shards - k), quarter, 1)
        if stage == 1:
            return piece(item, later(k), 2 * core + 1 - side, 1)
        return piece(item, later(k), 2 - 2 * core, 2)

    def send(item, stage):
        for k in turns:
            src, dst, peer = hop(item, stage, k)
            remote(src, dst, (item, stage, k - 1), peer).start()

    def take(item, stage):
        for k in turns:
            dst = arrival(item, stage, k)
            remote(dst, dst, (item, stage, k - 1), core_peer).wait_recv()

    def small_copy(k):
        return pltpu.make_async_remote_copy(
            src_ref=small.at[shard], dst_ref=small.at[shard], send_sem=small_sem.at[0, k - 1],
            recv_sem=small_sem.at[1, k - 1], device_id=(section, later(k)), device_id_type=MESH,
        )

    QUARTERS = 4

    def part_rows(i):
        return slice(i * length // QUARTERS, (i + 1) * length // QUARTERS)

    def send_lo(source, i):
        return swap_copy(source.at[part_rows(i), :], lo.at[own, part_rows(i), :], 2 + i)

    def send_gin(i):
        return swap_copy(dp.at[part_rows(i), :], gin_land.at[part_rows(i), :], 2 + QUARTERS + i)

    def swap_copy(src, dst, index):
        return pltpu.make_async_remote_copy(
            src_ref=src, dst_ref=dst, send_sem=swap_sem.at[0, index], recv_sem=swap_sem.at[1, index],
            device_id=half_peer, device_id_type=MESH,
        )

    def for_rows(body):
        def step(r, carry):
            body(rows_at(r))
            return carry

        lax.fori_loop(0, blocks, step, 0)

    lane_ids = lax.broadcasted_iota(jnp.int32, (RB, LANES), 1)

    def keep_inverse(index, rows, inverse):
        rs[rows, :] = jnp.where(lane_ids == index, inverse, rs[rows, :])

    def kept_inverse(index, rows):
        return jnp.sum(jnp.where(lane_ids == index, rs[rows, :], 0.0), axis=-1, keepdims=True)

    piece_rows = features // shards // 4
    far = len(far_peers)
    AT_Z, AT_FAR, AT_BACK, AT_CORE = 2, 2 + len(turns), 2 + len(turns) + far, 3 + len(turns) + far
    FREE_Z, FREE_FAR = 2, 3
    trio = 3 * LANES
    half = hidden // 2
    group = [0, 1, 2, 3, 3, 4, 4, 5, 6, 6, 6, 6]
    unit_set = [(0, 1, 0, 1, 0, 1, 0)[g] for g in group]
    first_set = [(0, 1, 2, 0, 1, 2, 0)[g] for g in group]
    halves = [slice(0, half), slice(half, hidden)]
    unit_cols = [slice(0, hidden)] * 3 + halves + halves + [slice(0, hidden)] + [
        slice(3 * width, hidden), slice(0, 2 * trio), slice(2 * trio, 3 * trio), slice(3 * trio, 4 * trio)
    ]
    unit_far_first = [g in (1, 4) for g in group]
    unit_at = [(4, 6, 2, 3, 5, other, own)[g] for g in group]
    opens = [u == 0 or group[u] != group[u - 1] for u in range(UNITS)]
    closes = [u + 1 == UNITS or group[u] != group[u + 1] for u in range(UNITS)]
    LAST_WHOLE = 7
    parts_of_own = [8, 9, 10, 11]

    def first_bit(unit):
        return role if unit_far_first[unit] else side

    def first_peer(unit):
        return half_peer if unit_far_first[unit] else side_peer

    def far_list(unit):
        return [side_peer] + far_peers[:-1] if unit_far_first[unit] else far_peers

    def reduce_copy(unit, stage, src, dst, peer):
        return pltpu.make_async_remote_copy(
            src_ref=src, dst_ref=dst, send_sem=rs_send.at[unit, stage], recv_sem=rs_recv.at[unit, stage],
            device_id=peer, device_id_type=MESH,
        )

    def rows_of(first, count):
        return pl.ds(pl.multiple_of(first * piece_rows, piece_rows), count * piece_rows)

    def copy_core(unit):
        where, cols = unit_set[unit], unit_cols[unit]
        src = gs.at[where, :, rows_of(2 - 2 * core, 2), cols]
        return reduce_copy(unit, 0, src, r0.at[where, :, :, cols], core_peer)

    def copy_first(unit):
        where, cols = unit_set[unit], unit_cols[unit]
        src = r0.at[where, :, rows_of(1 - first_bit(unit), 1), cols]
        return reduce_copy(unit, 1, src, r1.at[first_set[unit], :, :, cols], first_peer(unit))

    def copy_z(unit, k):
        where, cols = unit_set[unit], unit_cols[unit]
        return reduce_copy(
            unit, AT_Z + k - 1, r1.at[first_set[unit], later(k), :, cols], r2.at[where, k - 1, :, cols],
            (section, later(k)),
        )

    def crosses(unit, b):
        return unit >= LAST_WHOLE and b == far - 1

    def copy_far(unit, b):
        where, cols = unit_set[unit], unit_cols[unit]
        there = 1 - where if crosses(unit, b) else where
        return reduce_copy(
            unit, AT_FAR + b, r3s.at[where, :, cols], r3r.at[there, b, :, cols], far_list(unit)[b]
        )

    def spend(unit, kind, where, count=1):
        if opens[unit] and group[unit] >= (3 if kind == 1 else 2):
            pl.semaphore_wait(free.at[kind, where], count)

    def gain(unit, kind, peers_of):
        after = group[unit] + (3 if kind == 1 else 2)
        if closes[unit] and after in group:
            where = (first_set if kind == 1 else unit_set)[unit]
            for peer in peers_of(group.index(after)):
                pl.semaphore_signal(free.at[kind, where], inc=1, device_id=peer, device_id_type=MESH)

    def start_far(unit, b):
        where = unit_set[unit]
        spend(unit, FREE_FAR + b, 1 - where if crosses(unit, b) else where)
        copy_far(unit, b).start()

    def take_far(unit, b):
        if not crosses(unit, b):
            copy_far(unit, b).wait_recv()
        elif unit == LAST_WHOLE:
            for part in parts_of_own:
                cols = unit_cols[part]
                arrived = r3r.at[1, b, :, cols]
                reduce_copy(part, AT_FAR + b, arrived, arrived, half_peer).wait_recv()
        elif unit == parts_of_own[0]:
            arrived = r3r.at[0, b]
            reduce_copy(LAST_WHOLE, AT_FAR + b, arrived, arrived, half_peer).wait_recv()

    def out_rows(unit, first, count):
        return gout.at[unit_at[unit], rows_of(first, count), unit_cols[unit]]

    def copy_back(unit):
        mine = 2 * core + first_bit(unit)
        src = r3s.at[unit_set[unit], :, unit_cols[unit]]
        return reduce_copy(unit, AT_BACK, src, out_rows(unit, mine, 1), first_peer(unit))

    def copy_keep(unit):
        mine = 2 * core + first_bit(unit)
        src = r3s.at[unit_set[unit], :, unit_cols[unit]]
        return pltpu.make_async_copy(src, out_rows(unit, mine, 1), rs_keep.at[unit])

    def copy_back_core(unit):
        rows = out_rows(unit, 2 * core, 2)
        return reduce_copy(unit, AT_CORE, rows, rows, core_peer)

    def sum_start(unit):
        spend(unit, 0, unit_set[unit])
        copy_core(unit).start()

    def sum_core(unit):
        where, cols = unit_set[unit], unit_cols[unit]
        copy_core(unit).wait()

        def add(block, carry):
            mine = gs[where, block, rows_of(2 * core, 2), cols].astype(F32)
            r0[where, block, :, cols] = (r0[where, block, :, cols].astype(F32) + mine).astype(BF)
            return carry

        lax.fori_loop(0, shards, add, 0)
        spend(unit, 1, first_set[unit])
        copy_first(unit).start()

    def sum_first(unit):
        where, cols = unit_set[unit], unit_cols[unit]
        copy_first(unit).wait()

        def add(block, carry):
            mine = r0[where, block, rows_of(first_bit(unit), 1), cols].astype(F32)
            held = r1[first_set[unit], block, :, cols].astype(F32)
            r1[first_set[unit], block, :, cols] = (held + mine).astype(BF)
            return carry

        lax.fori_loop(0, shards, add, 0)
        gain(unit, 0, lambda following: [core_peer])
        spend(unit, FREE_Z, where, len(turns))
        for k in turns:
            copy_z(unit, k).start()

    def sum_z(unit):
        where, cols = unit_set[unit], unit_cols[unit]
        for k in turns:
            copy_z(unit, k).wait()
        total = r1[first_set[unit], shard, :, cols].astype(F32)
        for k in turns:
            total += r2[where, k - 1, :, cols].astype(F32)
        r3s[where, :, cols] = total.astype(BF)
        gain(unit, 1, lambda following: [first_peer(following)])
        gain(unit, FREE_Z, lambda following: [(section, later(k)) for k in turns])
        start_far(unit, 0)

    def sum_far(unit):
        where, cols = unit_set[unit], unit_cols[unit]
        for b in range(far):
            copy_far(unit, b).wait_send()
            take_far(unit, b)
            total = r3s[where, :, cols].astype(F32) + r3r[where, b, :, cols].astype(F32)
            r3s[where, :, cols] = total.astype(BF)
            gain(unit, FREE_FAR + b, lambda following, b=b: [far_list(following)[b]])
            if b + 1 < far:
                start_far(unit, b + 1)
        copy_keep(unit).start()
        copy_back(unit).start()

    def sum_back(unit):
        copy_keep(unit).wait()
        copy_back(unit).wait_send()
        arrived = out_rows(unit, 2 * core + 1 - first_bit(unit), 1)
        reduce_copy(unit, AT_BACK, arrived, arrived, first_peer(unit)).wait_recv()
        copy_back_core(unit).start()

    def sum_end(unit):
        copy_back_core(unit).wait_send()
        arrived = out_rows(unit, 2 - 2 * core, 2)
        reduce_copy(unit, AT_CORE, arrived, arrived, core_peer).wait_recv()

    small_peers = far_peers + [side_peer]

    def copy_small(b):
        at = len(turns) + b
        return pltpu.make_async_remote_copy(
            src_ref=sg.at[shard], dst_ref=sgz.at[at], send_sem=sg_send.at[at],
            recv_sem=sg_recv.at[at], device_id=small_peers[b], device_id_type=MESH,
        )

    def copy_small_core():
        at = len(turns) + len(small_peers)
        return pltpu.make_async_remote_copy(
            src_ref=sg, dst_ref=sgr, send_sem=sg_send.at[at],
            recv_sem=sg_recv.at[at], device_id=core_peer, device_id_type=MESH,
        )

    def copy_small_z(k):
        return pltpu.make_async_remote_copy(
            src_ref=sg.at[later(k)], dst_ref=sgz.at[k - 1], send_sem=sg_send.at[k - 1],
            recv_sem=sg_recv.at[k - 1], device_id=(section, later(k)), device_id_type=MESH,
        )

    def small_start():
        for owner in range(shards):
            cols = slice(owner * LANES, (owner + 1) * LANES)
            rows = [gacc[row, :, cols] for row in range(MASK_ROW + 1)]
            rest = jnp.zeros((SMALL_ROWS - MASK_ROW - 1, LANES), F32)
            sg[owner] = jnp.concatenate(rows + [rest], axis=0) + pick[...] * gacc[STEP_ROW, :, cols]
        copy_small_core().start()

    def small_core():
        copy_small_core().wait()
        sg[...] += sgr[...]
        for k in turns:
            copy_small_z(k).start()

    def small_z():
        for k in turns:
            copy_small_z(k).wait()
        sg[shard] += sum(sgz[k - 1] for k in turns)
        copy_small(0).start()

    def small_add(b):
        copy_small(b).wait()
        sg[shard] += sgz[len(turns) + b]
        if b + 1 < len(small_peers):
            copy_small(b + 1).start()
        else:
            gv[...] = sg[shard]

    def embed(layer):
        flag = layer.astype(F32)

        def body(rows):
            source = x[layer, rows, :].astype(F32)
            masked = rs[rows, MASK_LANE : MASK_LANE + 1] * flag > 0.5
            value = jnp.where(masked, vec[MASK_ROW], source) + vec[STEP_ROW] * flag
            res[layer, rows, :] = value
            x[layer, rows, :] = value.astype(BF)

        for_rows(body)

    def project(source, weight, target, first, last):
        for c in range(first, last):
            cols = slice(c * width, (c + 1) * width)

            def body(rows, cols=cols):
                target[rows, cols] = dot(source[rows, :], weight[:, cols]).astype(BF)

            for_rows(body)

    queries = length // AB

    def attend(which, polls=()):
        source, target, saved = qkv.at[which], oa.at[which], p_hbm.at[which]
        steps = pairs * queries

        def store(t):
            slot = lax.rem(t, 2)
            return pltpu.make_async_copy(big.at[pl.ds(2 * slot, 2)], saved.at[t], big_sem.at[slot])

        def step(t, carry):
            hp, qb = t // queries, lax.rem(t, queries)
            slot = lax.rem(t, 2)
            rows = rows_at(qb, AB)
            q = source[rows, lanes_at(hp)] * jnp.asarray(0.125, BF)
            k = source[:, lanes_at(pairs + hp)]
            v = source[:, lanes_at(2 * pairs + hp)]

            @pl.when(t >= 2)
            def _():
                store(t - 2).wait()

            for when, act in polls:
                pl.when(t == when)(act)

            low = low_half((AB, LANES))
            zero = jnp.zeros_like(q)
            scores = [dot(jnp.where(low if j == 0 else ~low, q, zero), k, NT) for j in range(2)]
            parts = []
            for j in range(2):
                e = jnp.exp(scores[j] - jnp.max(scores[j], axis=-1, keepdims=True))
                weights = (e * (1.0 / jnp.sum(e, axis=-1, keepdims=True))).astype(BF)
                for h in range(2):
                    big[2 * slot + j, h * AB : (h + 1) * AB, :] = weights[:, h * width : (h + 1) * width]
                parts.append(dot(weights, v))
            target[rows, lanes_at(hp)] = jnp.where(low, parts[0], parts[1]).astype(BF)
            store(t).start()
            return carry

        lax.fori_loop(0, steps, step, 0)
        for t in range(steps - 2, steps):
            store(t).wait()

    def out_norm(which, res_at, xh_at, gain_row, shift_row, hb_at):
        def body(rows):
            value = dot(oa[which, rows, :], wa[which, :, 3 * width :]) + res[res_at, rows, :]
            normal, inverse = norm_rows(value)
            result = normal * vec[gain_row] + vec[shift_row]
            xh[xh_at, rows, :] = normal.astype(BF)
            keep_inverse(xh_at, rows, inverse)
            res[res_at, rows, :] = result
            hb[hb_at, rows, :] = result.astype(BF)

        for_rows(body)

    chunks = hidden // width

    def up_chunk(layer, c):
        starts = [z * width + c * block_rows for z in range(shards)]
        return jnp.concatenate([wu[layer, :, i : i + block_rows] for i in starts], axis=1)

    def down_chunk(layer, c):
        starts = [z * width + c * block_rows for z in range(shards)]
        return jnp.concatenate([wd[layer, i : i + block_rows, :] for i in starts], axis=0)

    def feed_store(layer, c):
        slot = c % 2
        return pltpu.make_async_copy(big.at[2 * slot : 2 * slot + 2], f_hbm.at[layer, c], big_sem.at[slot])

    def feed_load(layer, c):
        slot = c % 2
        return pltpu.make_async_copy(f_hbm.at[layer, c], big.at[2 * slot : 2 * slot + 2], big_sem.at[slot])

    def feed(layer, hb_at, polls=()):
        for c in range(chunks):
            slot = c % 2
            cols = slice(c * width, (c + 1) * width)
            if c >= 2:
                feed_store(layer, c - 2).wait()

            parts = [slice(r * RB, (r + 1) * RB) for r in range(length // RB)]
            lifted = [dot(hb[hb_at, parts[0], :], up_chunk(layer, c))]
            for r, rows in enumerate(parts):
                if r + 1 < len(parts):
                    lifted.append(dot(hb[hb_at, parts[r + 1], :], up_chunk(layer, c)))
                value, slope = gelu_both(lifted[r])
                value = value.astype(BF)
                big[2 * slot, rows, :] = value
                big[2 * slot + 1, rows, :] = slope.astype(BF)
                res[layer, rows, :] += dot(value, down_chunk(layer, c))

            feed_store(layer, c).start()
            for when, act in polls:
                if when == c:
                    act()
        for c in range(chunks - 2, chunks):
            feed_store(layer, c).wait()

    def final_norm(layer, xh_at, gain_row, shift_row, target, kept=None):
        kept = xh.at[xh_at] if kept is None else kept

        def body(rows):
            normal, inverse = norm_rows(res[layer, rows, :])
            kept[rows, :] = normal.astype(BF)
            keep_inverse(xh_at, rows, inverse)
            target[rows, :] = (normal * vec[gain_row] + vec[shift_row]).astype(BF)

        for_rows(body)

    def norm_back(load, res_at, xh_at, gain_row, shift_row, kept=None):
        kept = xh.at[xh_at] if kept is None else kept

        def body(rows):
            upstream = load(rows)
            normal = kept[rows, :].astype(F32)
            result = norm_rows_back(upstream, normal, kept_inverse(xh_at, rows), vec[gain_row])
            gacc[gain_row] += jnp.sum(upstream * normal, axis=0, keepdims=True)
            gacc[shift_row] += jnp.sum(upstream, axis=0, keepdims=True)
            res[res_at, rows, :] = result
            dfb[rows, :] = result.astype(BF)

        for_rows(body)

    def feed_back(layer, hb_at, up, down, polls=()):
        feed_load(layer, 0).start()
        feed_load(layer, 1).start()
        for c in range(chunks):
            slot = c % 2
            cols = slice(c * width, (c + 1) * width)
            feed_load(layer, c).wait()

            parts = [slice(r * RB, (r + 1) * RB) for r in range(length // RB)]
            grads = [dot(dfb[parts[0], :], down_chunk(layer, c), NT)]
            for r, rows in enumerate(parts):
                if r + 1 < len(parts):
                    grads.append(dot(dfb[parts[r + 1], :], down_chunk(layer, c), NT))
                grad = (grads[r] * big[2 * slot + 1, rows, :].astype(F32)).astype(BF)
                dp[rows, :] = grad
                res[layer, rows, :] += dot(grad, up_chunk(layer, c), NT)
            by_owner(up, cols, dot(hb[hb_at], dp[...], TN))
            by_owner(down, cols, dot(big[2 * slot], dfb[...], TN))
            if c + 2 < chunks:
                feed_load(layer, c + 2).start()
            for when, act in polls:
                if when == c:
                    act()

    def by_owner(target, cols, value):
        target[:, :, cols] = value.astype(BF).reshape(shards, features // shards, -1)

    def attend_back(which, polls=()):
        source, output, saved = qkv.at[which], oa.at[which], p_hbm.at[which]
        steps = pairs * queries

        def fetch(t):
            slot = lax.rem(t, 2)
            return pltpu.make_async_copy(saved.at[t], big.at[pl.ds(2 * slot, 2)], big_sem.at[slot])

        fetch(0).start()

        def step(t, carry):
            hp, qb = t // queries, lax.rem(t, queries)
            slot = lax.rem(t, 2)
            rows = rows_at(qb, AB)

            @pl.when(t + 1 < steps)
            def _():
                fetch(t + 1).start()

            for when, act in polls:
                pl.when(t == when)(act)

            fetch(t).wait()

            @pl.when(qb == 0)
            def _():
                kvt[...] = jnp.zeros_like(kvt)

            q = source[rows, lanes_at(hp)]
            k = source[:, lanes_at(pairs + hp)]
            v = source[:, lanes_at(2 * pairs + hp)]
            do = dob[rows, lanes_at(hp)]
            inner = do.astype(F32) * output[rows, lanes_at(hp)].astype(F32)
            low = low_half((AB, LANES))
            zero = jnp.zeros_like(q)
            parts = []
            for j in range(2):
                mine = low if j == 0 else ~low
                dom = jnp.where(mine, do, zero)
                delta = jnp.sum(jnp.where(mine, inner, 0.0), axis=-1, keepdims=True)
                weights = jnp.concatenate(
                    [big[2 * slot + j, h * AB : (h + 1) * AB, :] for h in range(2)], axis=1
                )
                ds = (weights.astype(F32) * (dot(dom, v, NT) - delta)).astype(BF)
                kvt[1] += dot(dom, weights, TN)
                kvt[0] += dot(jnp.where(mine, q, zero), ds, TN)
                parts.append(dot(ds, k))
            source[rows, lanes_at(hp)] = (jnp.where(low, parts[0], parts[1]) * 0.125).astype(BF)

            @pl.when(qb == queries - 1)
            def _():
                source[:, lanes_at(pairs + hp)] = jnp.transpose(kvt[0] * 0.125).astype(BF)
                source[:, lanes_at(2 * pairs + hp)] = jnp.transpose(kvt[1]).astype(BF)

            return carry

        lax.fori_loop(0, steps, step, 0)

    def grad_weight(target, first, last, left, which):
        for c in range(first, last):
            cols = slice(c * width, (c + 1) * width)
            by_owner(target, cols, dot(left[...], qkv[which, :, cols], TN))

    def grad_trio(target, left, which, hp):
        blocks_of = [qkv[which, :, lanes_at(n * pairs + hp)] for n in range(3)]
        value = dot(left[...], jnp.concatenate(blocks_of, axis=1), TN)
        by_owner(target, slice(hp * trio, (hp + 1) * trio), value)

    def out_grad(which, target):
        by_owner(target, slice(3 * width, 4 * width), dot(oa[which], dfb[...], TN))

    def out_back(which):

        def body(rows):
            dob[rows, :] = dot(dfb[rows, :], wa[which, :, 3 * width :], NT).astype(BF)

        for_rows(body)

    barrier = pltpu.get_barrier_semaphore()
    peers = [(section, later(k)) for k in turns] + [core_peer, side_peer] + far_peers
    for peer in peers:
        pl.semaphore_signal(barrier, inc=1, device_id=peer, device_id_type=MESH)
    for unit in range(5):
        load_masters(unit)
    load_x = pltpu.make_async_copy(x_in.at[own], x.at[own], cot_sem.at[0])
    load_x.start()
    gacc[...] = jnp.zeros_like(gacc)

    rows = [enc_gains[...], enc_shifts[...], dec_gains[...], dec_shifts[...], mask_embed[...], time_table[...]]
    count = sum(row.shape[0] for row in rows)
    rows.append(jnp.zeros((SMALL_ROWS - count, LANES), F32))
    small[shard] = jnp.concatenate(rows, axis=0).astype(BF)
    pair_row = ((section - (sections // 2) * role) * shards + shard) * 2 + role
    row_ids = lax.broadcasted_iota(jnp.int32, (SMALL_ROWS, LANES), 0)
    pick[...] = (row_ids == MASK_ROW + 1 + timestep[pair_row]).astype(F32)
    round_layer(own)
    pl.semaphore_wait(barrier, len(peers))

    for k in turns:
        small_copy(k).start()
    for item in range(4):
        send(item, 0)
    swap_x = swap_copy(x_in.at[other], x.at[own], 0)
    swap_x.start()
    round_layer(other)
    send(4, 0)
    load_masters(5)
    load_masters(6)
    round_master(2, wu, 0)
    send(5, 0)
    round_master(3, wd, 0, True)
    send(6, 0)
    round_master(4, wa, 2)
    send(7, 0)
    round_master(5, wu, 1)
    send(8, 0)
    round_master(6, wd, 1, True)
    send(9, 0)
    swap_cot = swap_copy(cot_in.at[other], cot_land, 1)
    swap_cot.start()

    batch = marks.shape[1]
    total_rows = route.shape[0]
    mine = jnp.zeros((2, length), F32)
    tally = jnp.zeros((1, 1), F32)
    for first in range(0, total_rows, batch):
        for n, array in enumerate((route, remask)):
            copy = pltpu.make_async_copy(array.at[first : first + batch, :], marks.at[n], lo_sem.at[n])
            copy.start()
            copy.wait()
        ids = lax.broadcasted_iota(jnp.int32, (batch, length), 0) + first
        routed = marks[0].astype(F32)
        same = jnp.where(lax.rem(ids, 2) == role, routed, 0.0)
        tally += jnp.sum(jnp.sum(same, axis=0, keepdims=True), axis=1, keepdims=True)
        picked = [
            jnp.sum(jnp.where(ids == pair_row, value, 0.0), axis=0, keepdims=True)
            for value in (marks[1].astype(F32), routed)
        ]
        mine += jnp.concatenate(picked, axis=0)
    scale = mine[1:2, :] * float(total_rows // 2 * length) / tally
    wide_ids = lax.broadcasted_iota(jnp.int32, (LANES, length), 0)
    wide = jnp.where(wide_ids == MASK_LANE, mine[0:1, :], jnp.where(wide_ids == SCALE_LANE, scale, 0.0))
    rs[...] = jnp.transpose(wide)

    for k in turns:
        small_copy(k).wait_recv()
    for owner in range(shards):
        values = small[owner].astype(F32)
        cols = slice(owner * LANES, (owner + 1) * LANES)
        for row in range(MASK_ROW + 1):
            vec[row, :, cols] = values[row : row + 1, :]
        vec[STEP_ROW, :, cols] = jnp.sum(values * pick[...], axis=0, keepdims=True)
    load_x.wait()
    embed(own)

    def pass_side(item):
        take(item, 0)
        send(item, 1)

    def pass_core(item):
        take(item, 1)
        send(item, 2)

    def ready(item):
        take(item, 2)

    def polls_of(*acts):
        return [(when, functools.partial(act, item)) for when, act, item in acts]

    pass_side(0)
    pass_side(1)
    pass_core(0)
    pass_side(2)
    pass_core(1)
    for c in range(3):
        ready(c)
        project(x.at[own], wa.at[own], qkv.at[own], c, c + 1)
        if c == 0:
            pass_core(2)
            pass_side(3)
    attend(own, polls_of((2, pass_core, 3), (4, pass_side, 4)))
    ready(3)
    pass_core(4)
    out_norm(own, own, own, 4 * own, 2 + 5 * own, own)
    swap_copy(x_in.at[other], x.at[other], 0).wait_recv()
    pass_side(5)
    embed(other)
    ready(4)
    project(x.at[other], wa.at[other], qkv.at[other], 0, 3)
    attend(other, polls_of((4, pass_core, 5), (4, pass_side, 6), (7, pass_side, 7)))
    pass_core(6)
    out_norm(other, other, other, 4 * other, 2 + 5 * other, other)
    ready(5)
    h_store = pltpu.make_async_copy(hb.at[0], h_land, h_sem)
    h_load = pltpu.make_async_copy(h_land, hb.at[0], h_sem)
    h_store.start()
    ready(6)
    feed(0, 0, polls_of((3, pass_core, 7), (3, pass_side, 8)))
    h_store.wait()
    final_norm(0, 2, 1, 3, hb.at[2])
    keep_memory = pltpu.make_async_copy(hb.at[2], lo.at[own], lo_sem.at[0])
    pl.when(role == 0)(keep_memory.start)
    for i in range(QUARTERS):
        pl.when(role == 1)(send_lo(hb.at[2], i).start)
    ready(7)
    project(hb.at[1], wa.at[2], qkv.at[2], 0, 1)
    project(hb.at[2], wa.at[2], qkv.at[2], 1, 3)
    attend(2, polls_of((4, pass_core, 8), (4, pass_side, 9)))
    pass_core(9)
    out_norm(2, 1, 3, 5, 8, 0)
    ready(8)
    ready(9)
    def load_cot(layer):
        here = pltpu.make_async_copy(cot_in.at[own], dp, cot_sem.at[1])
        there = pltpu.make_async_copy(cot_land, dp, cot_sem.at[1])
        pl.when(own == layer)(here.start)
        pl.when(own != layer)(there.start)
        return here

    swap_copy(cot_in.at[other], cot_land, 1).wait_recv()
    load_result_cot = load_cot(1)
    feed(1, 0)
    final_norm(1, 4, 6, 9, dob, big.at[3])
    keep_result = pltpu.make_async_copy(dob, lo.at[own], lo_sem.at[0])
    stage_result = pltpu.make_async_copy(dob, out_land, lo_sem.at[1])
    pl.when(role == 1)(keep_result.start)
    stage_result.start()

    def result_upstream(rows):
        return dp[rows, :].astype(F32) * rs[rows, SCALE_LANE : SCALE_LANE + 1]

    load_result_cot.wait()
    norm_back(result_upstream, 1, 4, 6, 9, big.at[3])
    stage_result.wait()
    keep_result.wait()
    feed_back(1, 0, gs.at[0], gs.at[1])
    h_load.start()
    load_memory_cot = load_cot(0)
    sum_start(0)
    sum_start(1)
    norm_back(lambda rows: res[1, rows, :], 1, 3, 5, 8)
    out_back(2)

    def lo_part(i):
        pl.when(role == 0)(send_lo(out_land, i).start)

    attend_back(
        2,
        polls_of((1, sum_core, 0), (1, sum_core, 1), (6, sum_first, 0), (6, sum_first, 1), (6, lo_part, 0)),
    )
    out_grad(2, gs.at[0])
    grad_weight(gs.at[0], 0, 1, hb.at[1], 2)
    grad_weight(gs.at[0], 1, 3, hb.at[2], 2)
    sum_start(2)
    load_memory_cot.wait()

    def cross_body(rows):
        res[1, rows, :] += dot(qkv[2, rows, :width], wa[2, :, :width], NT)
        res[0, rows, :] = dp[rows, :].astype(F32) + dot(
            qkv[2, rows, width:], wa[2, :, width : 3 * width], NT
        )

    for_rows(cross_body)
    sum_core(2)
    norm_back(lambda rows: res[0, rows, :], 0, 2, 1, 3)
    sum_z(0)
    h_load.wait()
    feed_back(
        0, 0, gs.at[1], gs.at[0],
        polls_of(
            (0, sum_far, 0), (0, lo_part, 1), (1, sum_start, 3), (2, sum_first, 2), (2, sum_start, 5),
            (2, sum_z, 1), (2, sum_core, 3), (2, sum_back, 0), (3, sum_core, 5), (3, sum_far, 1),
            (3, sum_end, 0),
        ),
    )
    sum_start(4)
    sum_start(6)

    def gin_part(i):
        send_gin(i).start()

    for turn, layer in enumerate((other, own)):
        slot = 1 - turn
        flag = layer.astype(F32)
        source = x.at[layer]
        target = gs.at[slot]
        norm_back(lambda rows: res[layer, rows, :], layer, layer, 4 * layer, 2 + 5 * layer)
        out_back(layer)

        def last_part(unit):
            for hp in {9: (0, 1), 10: (2,), 11: (3,)}[unit]:
                grad_trio(target, source, layer, hp)
            sum_start(unit)

        if turn == 0:
            acts = polls_of(
                (1, sum_z, 2), (1, sum_core, 4), (1, sum_core, 6), (2, sum_first, 3), (2, sum_back, 1),
                (2, sum_first, 5), (3, sum_end, 1), (3, sum_far, 2), (4, sum_first, 4), (5, sum_first, 6),
                (5, sum_back, 2), (5, sum_z, 3), (6, sum_end, 2), (6, lo_part, 2), (7, sum_z, 5),
                (7, sum_far, 3),
            )
        else:
            out_grad(layer, target)
            sum_start(8)
            acts = polls_of(
                (0, sum_far, 5), (0, sum_z, 6), (0, sum_far, 4), (1, sum_core, 8), (1, lo_part, 3),
                (1, sum_back, 5), (2, sum_first, 7), (2, sum_far, 6), (2, sum_back, 4), (3, gin_part, 1),
                (3, sum_end, 5), (4, last_part, 9), (4, sum_first, 8), (4, sum_end, 4),
                (4, gin_part, 2), (5, sum_core, 9), (5, sum_back, 6), (6, last_part, 10), (6, sum_end, 6),
                (6, gin_part, 3), (7, sum_core, 10), (7, sum_z, 7), (7, sum_first, 9),
            )
        attend_back(layer, acts)
        if turn == 0:
            sum_z(4)
            out_grad(layer, target)
            for hp in range(pairs):
                grad_trio(target, source, layer, hp)
            sum_start(7)
            sum_back(3)
        else:
            last_part(11)
            sum_first(10)
            sum_z(8)

        def body(rows):
            value = res[layer, rows, :] + dot(qkv[layer, rows, :], wa[layer, :, : 3 * width], NT)
            masked = rs[rows, MASK_LANE : MASK_LANE + 1] * flag > 0.5
            gacc[MASK_ROW] += jnp.sum(jnp.where(masked, value, 0.0), axis=0, keepdims=True)
            gacc[STEP_ROW] += jnp.sum(value, axis=0, keepdims=True) * flag
            value = jnp.where(masked, 0.0, value)
            res[layer, rows, :] = value
            if turn == 0:
                dp[rows, :] = value.astype(BF)

        for_rows(body)
        if turn == 0:
            sum_core(7)
            sum_end(3)
            gin_part(0)
        else:
            keep_gin = pltpu.make_async_copy(res.at[layer], gin.at[layer], gin_sem.at[0])
            keep_gin.start()
    sum_core(11)
    small_start()
    sum_far(8)
    sum_z(9)
    small_core()
    for i in range(QUARTERS):
        send_gin(i).wait()
    load_gin = pltpu.make_async_copy(gin_land, dob, gin_sem.at[1])
    load_gin.start()
    load_gin.wait()

    def widen(rows):
        res[other, rows, :] = dob[rows, :].astype(F32)

    for_rows(widen)
    keep_other = pltpu.make_async_copy(res.at[other], gin.at[other], gin_sem.at[1])
    keep_other.start()
    sum_first(11)
    sum_z(10)
    sum_far(9)
    small_z()
    sum_z(11)
    sum_far(10)
    for b in range(far):
        small_add(b)
    sum_far(11)
    sum_far(7)
    for unit in (8, 9, 10, 11):
        sum_back(unit)
    small_add(far)
    sum_back(7)
    for unit in (8, 9, 10, 11, 7):
        sum_end(unit)
    keep_other.wait()
    keep_gin.wait()
    for i in range(QUARTERS):
        send_lo(out_land, i).wait()
    swap_x.wait_send()
    swap_cot.wait_send()
    for k in turns:
        small_copy(k).wait_send()
    for item in range(len(items)):
        for stage in range(3):
            for k in turns:
                src, dst, peer = hop(item, stage, k)
                remote(src, dst, (item, stage, k - 1), peer).wait_send()


def run_pair(tokens, cotangent, route, remask, timestep, masters, small):
    _, length, features = tokens.shape
    shards = lax.axis_size("shard")
    hidden = masters[2].shape[1]
    pairs = features // LANES
    quarters = features // shards
    far = (lax.axis_size("section") // 4).bit_length() - 1
    hbm = pl.BlockSpec(memory_space=pl.ANY)
    vmem = pl.BlockSpec(memory_space=pltpu.VMEM)
    smem = pl.BlockSpec(memory_space=pltpu.SMEM)
    dma = pltpu.SemaphoreType.DMA
    full_a = (3, features, 4 * features)
    full_u = (2, features, hidden)
    full_d = (2, hidden, features)
    out = jax.ShapeDtypeStruct
    one = out(tokens.shape[1:], BF)
    return pl.pallas_call(
        kernel,
        name="pair",
        out_shape=[
            out(tokens.shape, BF),
            out(tokens.shape, F32),
            out((OWNED, features // shards, 4 * features), BF),
            out((SMALL_ROWS, LANES), F32),
            out((3, pairs * (length // AB), 2, length, features), BF),
            out((2, hidden // features, 2, length, features), BF),
            one, one, one, one,
        ],
        in_specs=[hbm] * 4 + [smem] + [hbm] * len(masters) + [vmem] * len(small),
        out_specs=[hbm] * 3 + [vmem] + [hbm] * 6,
        scratch_shapes=[
            pltpu.VMEM(full_a, BF),
            pltpu.VMEM(full_u, BF),
            pltpu.VMEM(full_d, BF),
            pltpu.VMEM((shards, SMALL_ROWS, LANES), BF),
            pltpu.VMEM((VEC_ROWS, 1, features), F32),
            pltpu.VMEM((SMALL_ROWS, LANES), F32),
            pltpu.VMEM((2, min(32, route.shape[0]), length), jnp.int32),
            pltpu.VMEM((VEC_ROWS, 1, features), F32),
            pltpu.VMEM((2, length, features), BF),
            pltpu.VMEM((3, length, 3 * features), BF),
            pltpu.VMEM((3, length, features), BF),
            pltpu.VMEM((4, length, features), BF),
            pltpu.VMEM((length, LANES), F32),
            pltpu.VMEM((3, length, features), BF),
            pltpu.VMEM((2, length, features), F32),
            pltpu.VMEM((length, features), BF),
            pltpu.VMEM((length, features), BF),
            pltpu.VMEM((4, length, features), BF),
            pltpu.VMEM((length, features), BF),
            pltpu.VMEM((2, LANES, length), F32),
            pltpu.VMEM((2, shards, quarters, hidden), BF),
            pltpu.VMEM((2, shards, quarters // 2, hidden), BF),
            pltpu.VMEM((3, shards, quarters // 4, hidden), BF),
            pltpu.VMEM((2, shards - 1, quarters // 4, hidden), BF),
            pltpu.VMEM((2, quarters // 4, hidden), BF),
            pltpu.VMEM((2, far, quarters // 4, hidden), BF),
            pltpu.VMEM((shards, SMALL_ROWS, LANES), F32),
            pltpu.VMEM((shards, SMALL_ROWS, LANES), F32),
            pltpu.VMEM((shards + far, SMALL_ROWS, LANES), F32),
            dma((ITEMS, 3, shards - 1)),
            dma((ITEMS, 3, shards - 1)),
            dma((OWNED, 4)),
            dma((3, shards - 1)),
            dma((2, 10)),
            dma((2,)),
            dma,
            dma((4,)),
            dma((2,)),
            dma((2,)),
            dma((UNITS, 3 + shards + far)),
            dma((UNITS, 3 + shards + far)),
            dma((UNITS,)),
            dma((shards + 1 + far,)),
            dma((shards + 1 + far,)),
            pltpu.SemaphoreType.REGULAR((3 + far, 3)),
        ],
        compiler_params=pltpu.CompilerParams(
            vmem_limit_bytes=64 << 20, has_side_effects=True, collective_id=0
        ),
    )(tokens, cotangent, route, remask, timestep, *masters, *small)


def finish_kernel(
    gout, gv,
    enc_qkv, enc_out, enc_up, enc_down, enc_gains, enc_shifts,
    dec_qkv, dec_out, cross_query, cross_kv, cross_out, dec_up, dec_down, dec_gains, dec_shifts,
    time_table, mask_embed,
):
    width = enc_out.shape[1]
    pairs = width // LANES
    for unit, qkv, out in ((0, enc_qkv, enc_out), (1, dec_qkv, dec_out)):
        for hp in range(pairs):
            for n in range(3):
                to, at = (n * pairs + hp) * LANES, (hp * 3 + n) * LANES
                qkv[:, to : to + LANES] = gout[unit, :, at : at + LANES].astype(F32)
        out[...] = gout[unit, :, 3 * width :].astype(F32)
    cross_query[...] = gout[2, :, :width].astype(F32)
    cross_kv[...] = gout[2, :, width : 3 * width].astype(F32)
    cross_out[...] = gout[2, :, 3 * width :].astype(F32)
    count = gout.shape[1]
    owners = width // count
    for unit, up in ((3, enc_up), (4, dec_up)):
        for c in range(owners):
            for z in range(owners):
                to, at = z * width + c * count, c * width + z * count
                up[:, to : to + count] = gout[unit, :, at : at + count].astype(F32)
    for unit, down in ((5, enc_down), (6, dec_down)):
        for j in range(down.shape[0] // count):
            down[j * count : (j + 1) * count, :] = gout[unit, :, j * width : (j + 1) * width].astype(F32)
    enc_gains[...] = gv[0:2, :]
    enc_shifts[...] = gv[2:4, :]
    dec_gains[...] = gv[4:7, :]
    dec_shifts[...] = gv[7:10, :]
    mask_embed[...] = gv[MASK_ROW : MASK_ROW + 1, :]
    time_table[...] = gv[MASK_ROW + 1 : MASK_ROW + 1 + time_table.shape[0], :]


def per_device(
    tokens, cotangent, route, remask, timestep,
    enc_qkv, enc_out, enc_up, enc_down, enc_gains, enc_shifts,
    dec_qkv, dec_out, cross_query, cross_kv, cross_out, dec_up, dec_down, dec_gains, dec_shifts,
    time_table, mask_embed,
):
    masters = (
        enc_qkv, enc_out, enc_up, enc_down, dec_qkv, dec_out,
        cross_query, cross_kv, cross_out, dec_up, dec_down,
    )
    mask_row = mask_embed[None, :]
    small = (enc_gains, enc_shifts, dec_gains, dec_shifts, mask_row, time_table)
    layer_out, grad_in, gout, gv = run_pair(
        tokens, cotangent, route, remask, timestep, masters, small
    )[:4]
    owned = (
        enc_qkv, enc_out, enc_up, enc_down, enc_gains, enc_shifts,
        dec_qkv, dec_out, cross_query, cross_kv, cross_out, dec_up, dec_down, dec_gains, dec_shifts,
        time_table, mask_row,
    )
    vmem = pl.BlockSpec(memory_space=pltpu.VMEM)
    grads = pl.pallas_call(
        finish_kernel,
        name="finish",
        out_shape=[jax.ShapeDtypeStruct(array.shape, F32) for array in owned],
        in_specs=[vmem] * 2,
        out_specs=[vmem] * len(owned),
        compiler_params=pltpu.CompilerParams(vmem_limit_bytes=48 << 20),
    )(gout, gv)
    return (layer_out, grad_in, *grads[:-1], grads[-1][0])


def solution(mesh):
    rows = P(("section", "shard"), None, None)
    first, second, copied = P("shard", None), P(None, "shard"), P()
    return jax.shard_map(
        per_device,
        mesh=mesh,
        in_specs=(rows, rows, copied, copied, copied)
        + (first,) * 4 + (second,) * 2 + (first,) * 7 + (second,) * 3 + (P("shard"),),
        out_specs=(rows, rows)
        + (first,) * 4 + (second,) * 2 + (first,) * 7 + (second,) * 3 + (P("shard"),),
        check_vma=False,
    )
```

```python
import functools

import jax
import jax.numpy as jnp
from jax import lax
from jax.experimental import pallas as pl
from jax.experimental.pallas import tpu as pltpu
from jax.sharding import PartitionSpec as P

HEADS = 8
EPSILON = 1e-05
BF = jnp.bfloat16
F32 = jnp.float32
NN = (((1,), (0,)), ((), ()))
NT = (((1,), (1,)), ((), ()))
TN = (((0,), (0,)), ((), ()))
RB = 256
AB = 512
LANES = 128
WIDTH = 512
MASK_ROW = 10
STEP_ROW = 11
VEC_ROWS = 12
MASK_LANE = 8
SCALE_LANE = 9
SMALL_ROWS = 64
OWNED = 7
UNITS = 16
ITEMS = 10
MESH = pl.DeviceIdType.MESH


def dot(left, right, dims=NN):
    return lax.dot_general(left, right, dims, preferred_element_type=F32)


def rows_at(r, count=RB):
    return pl.ds(pl.multiple_of(r * count, count), count)


def lanes_at(c, count=LANES):
    return pl.ds(pl.multiple_of(c * count, count), count)


def low_half(shape):
    return lax.broadcasted_iota(jnp.int32, shape, 1) < LANES // 2


def norm_rows(value):
    average = jnp.mean(value, axis=-1, keepdims=True)
    centred = value - average
    spread = jnp.mean(centred * centred, axis=-1, keepdims=True)
    inverse = lax.rsqrt(spread + EPSILON)
    return centred * inverse, inverse


def norm_rows_back(upstream, normal, inverse, gain):
    scaled = upstream * gain
    first = jnp.mean(scaled, axis=-1, keepdims=True)
    second = jnp.mean(scaled * normal, axis=-1, keepdims=True)
    return inverse * (scaled - first - normal * second)


def gelu_both(p):
    a = 0.7978845608028654
    b = 0.044715
    u = p * (a + (a * b) * (p * p))
    half = 0.5 + 0.5 * jnp.tanh(u)
    slope = half + (half - half * half) * (6.0 * u - (4.0 * a) * p)
    return p * half, slope


def kernel(
    x_in, cot_in, route, remask, timestep,
    enc_qkv, enc_out, enc_up, enc_down, dec_qkv, dec_out,
    cross_query, cross_kv, cross_out, dec_up, dec_down,
    enc_gains, enc_shifts, dec_gains, dec_shifts, mask_embed, time_table,
    lo, gin, gout, gv, p_hbm, f_hbm, cot_land, out_land, gin_land, h_land,
    wa, wu, wd, small, vec, pick, marks,
    gacc, x, qkv, oa, xh, rs, hb, res, dfb, dob, big, dp, kvt, gs,
    r0, r1, r2, r3s, r3r, sg, sgr, sgz,
    send_sem, recv_sem, load_sem, small_sem, swap_sem,
    cot_sem, h_sem, big_sem, lo_sem, gin_sem, rs_send, rs_recv, rs_keep, sg_send, sg_recv, free,
):
    length, features = x.shape[1], x.shape[2]
    hidden = wu.shape[2]
    blocks = length // RB
    pairs = features // LANES
    width = features
    section = lax.axis_index("section")
    role = (section >= lax.axis_size("section") // 2).astype(jnp.int32)
    own, other = role, 1 - role
    sections, shards = lax.axis_size("section"), lax.axis_size("shard")
    shard = lax.axis_index("shard")
    core = lax.rem(section, 2)
    side = lax.rem(section // 2, 2)
    quarter = 2 * core + side
    core_peer = (section + 1 - 2 * core, shard)
    side_peer = (section + 2 - 4 * side, shard)
    turns = range(1, shards)

    def bit_peer(bit):
        return (section + bit * (1 - 2 * lax.rem(section // bit, 2)), shard)

    far_peers = [bit_peer(4 << b) for b in range((sections // 4).bit_length() - 1)]
    half_peer = far_peers[-1]

    def later(k):
        return lax.rem(shard + k, shards)

    items = [(wa, own, slice(c * width, (c + 1) * width)) for c in range(4)] + [
        (wa, other, slice(0, 4 * width)),
        (wu, 0, slice(0, hidden)),
        (wd, 0, slice(0, width)),
        (wa, 2, slice(0, 4 * width)),
        (wu, 1, slice(0, hidden)),
        (wd, 1, slice(0, width)),
    ]

    block_rows = width // shards

    def columns(*refs):
        return [
            ref.at[:, c * width : (c + 1) * width] for ref in refs for c in range(ref.shape[1] // width)
        ]

    def row_blocks(ref):
        return [ref.at[j * block_rows : (j + 1) * block_rows, :] for j in range(shards)]

    masters = [
        columns(enc_qkv, enc_out), columns(dec_qkv, dec_out), columns(enc_up), row_blocks(enc_down),
        columns(cross_query, cross_kv, cross_out), columns(dec_up), row_blocks(dec_down),
    ]

    def staged(unit, j):
        if unit == 4:
            return kvt.at[j // 2, 0:block_rows, (j % 2) * width : (j % 2 + 1) * width]
        half, start = [(0, 0), (0, 1), (1, 0), (1, 1), None, (0, 0), (0, 1)][unit]
        first = start * 4 * block_rows + j * block_rows
        return res.at[half, first : first + block_rows, :]

    def load_master(unit, j):
        return pltpu.make_async_copy(masters[unit][j], staged(unit, j), load_sem.at[unit, j])

    def load_masters(unit):
        for j in range(4):
            load_master(unit, j).start()

    def round_master(unit, full, lead, by_rows=False):
        for j in range(4):
            load_master(unit, j).wait()
            value = staged(unit, j)[...].astype(BF)
            if by_rows:
                first = shard * (4 * block_rows) + j * block_rows
                full[lead, pl.ds(pl.multiple_of(first, block_rows), block_rows), :] = value
            else:
                first = pl.multiple_of(shard * block_rows, block_rows)
                full[lead, pl.ds(first, block_rows), j * width : (j + 1) * width] = value

    def round_layer(layer):
        for j in range(4):
            first = pl.multiple_of(layer * (4 * block_rows) + j * block_rows, block_rows)
            place = res.at[0, pl.ds(first, block_rows), :]
            pltpu.make_async_copy(place, place, load_sem.at[layer, j]).wait()
            rows = pl.ds(pl.multiple_of(shard * block_rows, block_rows), block_rows)
            wa[layer, rows, j * width : (j + 1) * width] = place[...].astype(BF)

    def remote(src, dst, sems, peer):
        return pltpu.make_async_remote_copy(
            src_ref=src, dst_ref=dst, send_sem=send_sem.at[sems], recv_sem=recv_sem.at[sems],
            device_id=peer, device_id_type=MESH,
        )

    def piece(item, owner, first, count):
        full, lead, cols = items[item]
        size = full.shape[1] // (4 * shards)
        start = pl.multiple_of(owner * (4 * size) + first * size, size)
        return full.at[lead, pl.ds(start, count * size), cols]

    def hop(item, stage, k):
        if stage == 0:
            src = piece(item, shard, quarter, 1)
            return src, src, (section, later(k))
        if stage == 1:
            src = piece(item, later(k), quarter, 1)
            return src, src, side_peer
        src = piece(item, later(k), 2 * core, 2)
        return src, src, core_peer

    def arrival(item, stage, k):
        if stage == 0:
            return piece(item, later(shards - k), quarter, 1)
        if stage == 1:
            return piece(item, later(k), 2 * core + 1 - side, 1)
        return piece(item, later(k), 2 - 2 * core, 2)

    def send(item, stage):
        for k in turns:
            src, dst, peer = hop(item, stage, k)
            remote(src, dst, (item, stage, k - 1), peer).start()

    def take(item, stage):
        for k in turns:
            dst = arrival(item, stage, k)
            remote(dst, dst, (item, stage, k - 1), core_peer).wait_recv()

    def small_copy(k):
        return pltpu.make_async_remote_copy(
            src_ref=small.at[shard], dst_ref=small.at[shard], send_sem=small_sem.at[0, k - 1],
            recv_sem=small_sem.at[1, k - 1], device_id=(section, later(k)), device_id_type=MESH,
        )

    QUARTERS = 4

    def part_rows(i):
        return slice(i * length // QUARTERS, (i + 1) * length // QUARTERS)

    def send_lo(source, i):
        return swap_copy(source.at[part_rows(i), :], lo.at[own, part_rows(i), :], 2 + i)

    def send_gin(i):
        return swap_copy(dp.at[part_rows(i), :], gin_land.at[part_rows(i), :], 2 + QUARTERS + i)

    def swap_copy(src, dst, index):
        return pltpu.make_async_remote_copy(
            src_ref=src, dst_ref=dst, send_sem=swap_sem.at[0, index], recv_sem=swap_sem.at[1, index],
            device_id=half_peer, device_id_type=MESH,
        )

    def for_rows(body):
        def step(r, carry):
            body(rows_at(r))
            return carry

        lax.fori_loop(0, blocks, step, 0)

    def for_wide_rows(body):
        def step(r, carry):
            body(rows_at(r, AB))
            return carry

        lax.fori_loop(0, length // AB, step, 0)

    lane_ids = lax.broadcasted_iota(jnp.int32, (RB, LANES), 1)

    def keep_inverse(index, rows, inverse):
        rs[rows, :] = jnp.where(lane_ids == index, inverse, rs[rows, :])

    def kept_inverse(index, rows):
        return jnp.sum(jnp.where(lane_ids == index, rs[rows, :], 0.0), axis=-1, keepdims=True)

    piece_rows = features // shards // 4
    far = len(far_peers)
    AT_Z, AT_FAR, AT_BACK, AT_CORE = 2, 2 + len(turns), 2 + len(turns) + far, 3 + len(turns) + far
    FREE_Z, FREE_FAR = 2, 3
    trio = 3 * LANES
    half = hidden // 2
    group = [0, 1, 2, 3, 3, 4, 4, 5, 6, 6, 6, 6, 5, 5, 5, 5]
    unit_set = [(0, 1, 0, 1, 0, 1, 0)[g] for g in group]
    first_set = [(0, 1, 2, 0, 1, 2, 0)[g] for g in group]
    halves = [slice(0, half), slice(half, hidden)]
    unit_cols = [slice(0, hidden)] * 3 + halves + halves + [slice(0, hidden)] + [
        slice(3 * width, hidden), slice(0, 2 * trio), slice(2 * trio, 3 * trio), slice(3 * trio, 4 * trio)
    ] * 2
    unit_far_first = [g in (1, 4) for g in group]
    unit_at = [(4, 6, 2, 3, 5, other, own)[g] for g in group]
    opens = [u == 0 or group[u] != group[u - 1] for u in range(UNITS)]
    closes = [u + 1 == UNITS or group[u] != group[u + 1] for u in range(UNITS)]
    LAST_WHOLE = 7
    parts_of_own = [8, 9, 10, 11]

    def first_bit(unit):
        return role if unit_far_first[unit] else side

    def first_peer(unit):
        return half_peer if unit_far_first[unit] else side_peer

    def far_list(unit):
        return [side_peer] + far_peers[:-1] if unit_far_first[unit] else far_peers

    def reduce_copy(unit, stage, src, dst, peer):
        return pltpu.make_async_remote_copy(
            src_ref=src, dst_ref=dst, send_sem=rs_send.at[unit, stage], recv_sem=rs_recv.at[unit, stage],
            device_id=peer, device_id_type=MESH,
        )

    def rows_of(first, count):
        return pl.ds(pl.multiple_of(first * piece_rows, piece_rows), count * piece_rows)

    def copy_core(unit):
        where, cols = unit_set[unit], unit_cols[unit]
        src = gs.at[where, :, rows_of(2 - 2 * core, 2), cols]
        return reduce_copy(unit, 0, src, r0.at[where, :, :, cols], core_peer)

    def copy_first(unit):
        where, cols = unit_set[unit], unit_cols[unit]
        src = r0.at[where, :, rows_of(1 - first_bit(unit), 1), cols]
        return reduce_copy(unit, 1, src, r1.at[first_set[unit], :, :, cols], first_peer(unit))

    def copy_z(unit, k):
        where, cols = unit_set[unit], unit_cols[unit]
        return reduce_copy(
            unit, AT_Z + k - 1, r1.at[first_set[unit], later(k), :, cols], r2.at[where, k - 1, :, cols],
            (section, later(k)),
        )

    def crosses(unit, b):
        return unit >= LAST_WHOLE and b == far - 1

    def copy_far(unit, b):
        where, cols = unit_set[unit], unit_cols[unit]
        there = 1 - where if crosses(unit, b) else where
        return reduce_copy(
            unit, AT_FAR + b, r3s.at[where, :, cols], r3r.at[there, b, :, cols], far_list(unit)[b]
        )

    def spend(unit, kind, where, count=1):
        if opens[unit] and group[unit] >= (3 if kind == 1 else 2):
            pl.semaphore_wait(free.at[kind, where], count)

    def gain(unit, kind, peers_of):
        after = group[unit] + (3 if kind == 1 else 2)
        if closes[unit] and after in group:
            where = (first_set if kind == 1 else unit_set)[unit]
            for peer in peers_of(group.index(after)):
                pl.semaphore_signal(free.at[kind, where], inc=1, device_id=peer, device_id_type=MESH)

    def start_far(unit, b):
        where = unit_set[unit]
        spend(unit, FREE_FAR + b, 1 - where if crosses(unit, b) else where)
        copy_far(unit, b).start()

    def take_far(unit, b):
        if not crosses(unit, b):
            copy_far(unit, b).wait_recv()
        elif unit == parts_of_own[0]:
            arrived = r3r.at[0, b]
            reduce_copy(LAST_WHOLE, AT_FAR + b, arrived, arrived, half_peer).wait_recv()

    def out_rows(unit, first, count):
        return gout.at[unit_at[unit], rows_of(first, count), unit_cols[unit]]

    def copy_back(unit):
        mine = 2 * core + first_bit(unit)
        src = r3s.at[unit_set[unit], :, unit_cols[unit]]
        return reduce_copy(unit, AT_BACK, src, out_rows(unit, mine, 1), first_peer(unit))

    def copy_keep(unit):
        mine = 2 * core + first_bit(unit)
        src = r3s.at[unit_set[unit], :, unit_cols[unit]]
        return pltpu.make_async_copy(src, out_rows(unit, mine, 1), rs_keep.at[unit])

    def copy_back_core(unit):
        rows = out_rows(unit, 2 * core, 2)
        return reduce_copy(unit, AT_CORE, rows, rows, core_peer)

    def sum_start(unit):
        spend(unit, 0, unit_set[unit])
        copy_core(unit).start()

    def sum_core(unit):
        where, cols = unit_set[unit], unit_cols[unit]
        copy_core(unit).wait()

        def add(block, carry):
            mine = gs[where, block, rows_of(2 * core, 2), cols].astype(F32)
            r0[where, block, :, cols] = (r0[where, block, :, cols].astype(F32) + mine).astype(BF)
            return carry

        lax.fori_loop(0, shards, add, 0)
        spend(unit, 1, first_set[unit])
        copy_first(unit).start()

    def sum_first(unit):
        where, cols = unit_set[unit], unit_cols[unit]
        copy_first(unit).wait()

        def add(block, carry):
            mine = r0[where, block, rows_of(first_bit(unit), 1), cols].astype(F32)
            held = r1[first_set[unit], block, :, cols].astype(F32)
            r1[first_set[unit], block, :, cols] = (held + mine).astype(BF)
            return carry

        lax.fori_loop(0, shards, add, 0)
        gain(unit, 0, lambda following: [core_peer])
        spend(unit, FREE_Z, where, len(turns))
        for k in turns:
            copy_z(unit, k).start()

    def sum_z(unit):
        where, cols = unit_set[unit], unit_cols[unit]
        for k in turns:
            copy_z(unit, k).wait()
        total = r1[first_set[unit], shard, :, cols].astype(F32)
        for k in turns:
            total += r2[where, k - 1, :, cols].astype(F32)
        r3s[where, :, cols] = total.astype(BF)
        gain(unit, 1, lambda following: [first_peer(following)])
        gain(unit, FREE_Z, lambda following: [(section, later(k)) for k in turns])
        start_far(unit, 0)

    def sum_far(unit):
        where, cols = unit_set[unit], unit_cols[unit]
        for b in range(far - 1 if unit == LAST_WHOLE else far):
            copy_far(unit, b).wait_send()
            take_far(unit, b)
            total = r3s[where, :, cols].astype(F32) + r3r[where, b, :, cols].astype(F32)
            r3s[where, :, cols] = total.astype(BF)
            gain(unit, FREE_FAR + b, lambda following, b=b: [far_list(following)[b]])
            if b + 1 < far:
                start_far(unit, b + 1)
        if unit != LAST_WHOLE:
            copy_keep(unit).start()
            copy_back(unit).start()

    def sum_cross(unit):
        part = unit - 4
        where, cols = unit_set[unit], unit_cols[unit]
        if unit == 12:
            copy_far(LAST_WHOLE, far - 1).wait_send()
        arrived = r3r.at[where, far - 1, :, cols]
        reduce_copy(part, AT_FAR + far - 1, arrived, arrived, half_peer).wait_recv()
        total = r3s[where, :, cols].astype(F32) + arrived[...].astype(F32)
        r3s[where, :, cols] = total.astype(BF)
        copy_keep(unit).start()
        copy_back(unit).start()

    def sum_back(unit):
        copy_keep(unit).wait()
        copy_back(unit).wait_send()
        arrived = out_rows(unit, 2 * core + 1 - first_bit(unit), 1)
        reduce_copy(unit, AT_BACK, arrived, arrived, first_peer(unit)).wait_recv()
        copy_back_core(unit).start()

    def sum_end(unit):
        copy_back_core(unit).wait_send()
        arrived = out_rows(unit, 2 - 2 * core, 2)
        reduce_copy(unit, AT_CORE, arrived, arrived, core_peer).wait_recv()

    small_peers = far_peers + [side_peer]

    def copy_small(b):
        at = len(turns) + b
        return pltpu.make_async_remote_copy(
            src_ref=sg.at[shard], dst_ref=sgz.at[at], send_sem=sg_send.at[at],
            recv_sem=sg_recv.at[at], device_id=small_peers[b], device_id_type=MESH,
        )

    def copy_small_core():
        at = len(turns) + len(small_peers)
        return pltpu.make_async_remote_copy(
            src_ref=sg, dst_ref=sgr, send_sem=sg_send.at[at],
            recv_sem=sg_recv.at[at], device_id=core_peer, device_id_type=MESH,
        )

    def copy_small_z(k):
        return pltpu.make_async_remote_copy(
            src_ref=sg.at[later(k)], dst_ref=sgz.at[k - 1], send_sem=sg_send.at[k - 1],
            recv_sem=sg_recv.at[k - 1], device_id=(section, later(k)), device_id_type=MESH,
        )

    def small_start():
        for owner in range(shards):
            cols = slice(owner * LANES, (owner + 1) * LANES)
            rows = [gacc[row, :, cols] for row in range(MASK_ROW + 1)]
            rest = jnp.zeros((SMALL_ROWS - MASK_ROW - 1, LANES), F32)
            sg[owner] = jnp.concatenate(rows + [rest], axis=0) + pick[...] * gacc[STEP_ROW, :, cols]
        copy_small_core().start()

    def small_core():
        copy_small_core().wait()
        sg[...] += sgr[...]
        for k in turns:
            copy_small_z(k).start()

    def small_z():
        for k in turns:
            copy_small_z(k).wait()
        sg[shard] += sum(sgz[k - 1] for k in turns)
        copy_small(0).start()

    def small_add(b):
        copy_small(b).wait()
        sg[shard] += sgz[len(turns) + b]
        if b + 1 < len(small_peers):
            copy_small(b + 1).start()
        else:
            gv[...] = sg[shard]

    def embed(layer):
        flag = layer.astype(F32)

        def body(rows):
            source = x[layer, rows, :].astype(F32)
            masked = rs[rows, MASK_LANE : MASK_LANE + 1] * flag > 0.5
            value = jnp.where(masked, vec[MASK_ROW], source) + vec[STEP_ROW] * flag
            res[layer, rows, :] = value
            x[layer, rows, :] = value.astype(BF)

        for_rows(body)

    def project(source, weight, target, first, last):
        for c in range(first, last):
            cols = slice(c * width, (c + 1) * width)

            def body(rows, cols=cols):
                target[rows, cols] = dot(source[rows, :], weight[:, cols]).astype(BF)

            for_wide_rows(body)

    queries = length // AB

    def attend(which, polls=()):
        source, target, saved = qkv.at[which], oa.at[which], p_hbm.at[which]
        steps = pairs * queries

        def store(t):
            slot = lax.rem(t, 2)
            return pltpu.make_async_copy(big.at[pl.ds(2 * slot, 2)], saved.at[t], big_sem.at[slot])

        def step(t, carry):
            hp, qb = t // queries, lax.rem(t, queries)
            slot = lax.rem(t, 2)
            rows = rows_at(qb, AB)
            q = source[rows, lanes_at(hp)] * jnp.asarray(0.125, BF)
            k = source[:, lanes_at(pairs + hp)]
            v = source[:, lanes_at(2 * pairs + hp)]

            @pl.when(t >= 2)
            def _():
                store(t - 2).wait()

            for when, act in polls:
                pl.when(t == when)(act)

            low = low_half((AB, LANES))
            zero = jnp.zeros_like(q)
            scores = [dot(jnp.where(low if j == 0 else ~low, q, zero), k, NT) for j in range(2)]
            parts = []
            for j in range(2):
                e = jnp.exp(scores[j] - jnp.max(scores[j], axis=-1, keepdims=True))
                weights = (e * (1.0 / jnp.sum(e, axis=-1, keepdims=True))).astype(BF)
                for h in range(2):
                    big[2 * slot + j, h * AB : (h + 1) * AB, :] = weights[:, h * width : (h + 1) * width]
                parts.append(dot(weights, v))
            target[rows, lanes_at(hp)] = jnp.where(low, parts[0], parts[1]).astype(BF)
            store(t).start()
            return carry

        lax.fori_loop(0, steps, step, 0)
        for t in range(steps - 2, steps):
            store(t).wait()

    def out_norm(which, res_at, xh_at, gain_row, shift_row, hb_at):
        def body(rows):
            value = dot(oa[which, rows, :], wa[which, :, 3 * width :]) + res[res_at, rows, :]
            normal, inverse = norm_rows(value)
            result = normal * vec[gain_row] + vec[shift_row]
            xh[xh_at, rows, :] = normal.astype(BF)
            keep_inverse(xh_at, rows, inverse)
            res[res_at, rows, :] = result
            hb[hb_at, rows, :] = result.astype(BF)

        for_rows(body)

    chunks = hidden // width

    def up_chunk(layer, c):
        starts = [z * width + c * block_rows for z in range(shards)]
        return jnp.concatenate([wu[layer, :, i : i + block_rows] for i in starts], axis=1)

    def down_chunk(layer, c):
        starts = [z * width + c * block_rows for z in range(shards)]
        return jnp.concatenate([wd[layer, i : i + block_rows, :] for i in starts], axis=0)

    def feed_store(layer, c):
        slot = c % 2
        return pltpu.make_async_copy(big.at[2 * slot : 2 * slot + 2], f_hbm.at[layer, c], big_sem.at[slot])

    def feed_load(layer, c):
        slot = c % 2
        return pltpu.make_async_copy(f_hbm.at[layer, c], big.at[2 * slot : 2 * slot + 2], big_sem.at[slot])

    def feed(layer, hb_at, polls=()):
        for c in range(chunks):
            slot = c % 2
            cols = slice(c * width, (c + 1) * width)
            if c >= 2:
                feed_store(layer, c - 2).wait()

            parts = [slice(r * RB, (r + 1) * RB) for r in range(length // RB)]
            lifted = [dot(hb[hb_at, parts[0], :], up_chunk(layer, c))]
            for r, rows in enumerate(parts):
                if r + 1 < len(parts):
                    lifted.append(dot(hb[hb_at, parts[r + 1], :], up_chunk(layer, c)))
                value, slope = gelu_both(lifted[r])
                value = value.astype(BF)
                big[2 * slot, rows, :] = value
                big[2 * slot + 1, rows, :] = slope.astype(BF)
                res[layer, rows, :] += dot(value, down_chunk(layer, c))

            feed_store(layer, c).start()
            for when, act in polls:
                if when == c:
                    act()
        for c in range(chunks - 2, chunks):
            feed_store(layer, c).wait()

    def final_norm(layer, xh_at, gain_row, shift_row, target, kept=None):
        kept = xh.at[xh_at] if kept is None else kept

        def body(rows):
            normal, inverse = norm_rows(res[layer, rows, :])
            kept[rows, :] = normal.astype(BF)
            keep_inverse(xh_at, rows, inverse)
            target[rows, :] = (normal * vec[gain_row] + vec[shift_row]).astype(BF)

        for_rows(body)

    def norm_back(load, res_at, xh_at, gain_row, shift_row, kept=None):
        kept = xh.at[xh_at] if kept is None else kept

        def body(rows):
            upstream = load(rows)
            normal = kept[rows, :].astype(F32)
            result = norm_rows_back(upstream, normal, kept_inverse(xh_at, rows), vec[gain_row])
            gacc[gain_row] += jnp.sum(upstream * normal, axis=0, keepdims=True)
            gacc[shift_row] += jnp.sum(upstream, axis=0, keepdims=True)
            res[res_at, rows, :] = result
            dfb[rows, :] = result.astype(BF)

        for_rows(body)

    def feed_back(layer, hb_at, up, down, polls=()):
        feed_load(layer, 0).start()
        feed_load(layer, 1).start()
        for c in range(chunks):
            slot = c % 2
            cols = slice(c * width, (c + 1) * width)
            feed_load(layer, c).wait()

            parts = [slice(r * RB, (r + 1) * RB) for r in range(length // RB)]
            grads = [dot(dfb[parts[0], :], down_chunk(layer, c), NT)]
            for r, rows in enumerate(parts):
                if r + 1 < len(parts):
                    grads.append(dot(dfb[parts[r + 1], :], down_chunk(layer, c), NT))
                grad = (grads[r] * big[2 * slot + 1, rows, :].astype(F32)).astype(BF)
                dp[rows, :] = grad
                res[layer, rows, :] += dot(grad, up_chunk(layer, c), NT)
            by_owner(up, cols, dot(hb[hb_at], dp[...], TN))
            by_owner(down, cols, dot(big[2 * slot], dfb[...], TN))
            if c + 2 < chunks:
                feed_load(layer, c + 2).start()
            for when, act in polls:
                if when == c:
                    act()

    def by_owner(target, cols, value):
        target[:, :, cols] = value.astype(BF).reshape(shards, features // shards, -1)

    def attend_back(which, polls=()):
        source, output, saved = qkv.at[which], oa.at[which], p_hbm.at[which]
        steps = pairs * queries

        def fetch(t):
            slot = lax.rem(t, 2)
            return pltpu.make_async_copy(saved.at[t], big.at[pl.ds(2 * slot, 2)], big_sem.at[slot])

        fetch(0).start()

        def step(t, carry):
            hp, qb = t // queries, lax.rem(t, queries)
            slot = lax.rem(t, 2)
            rows = rows_at(qb, AB)

            @pl.when(t + 1 < steps)
            def _():
                fetch(t + 1).start()

            for when, act in polls:
                pl.when(t == when)(act)

            fetch(t).wait()

            @pl.when(qb == 0)
            def _():
                kvt[...] = jnp.zeros_like(kvt)

            q = source[rows, lanes_at(hp)]
            k = source[:, lanes_at(pairs + hp)]
            v = source[:, lanes_at(2 * pairs + hp)]
            do = dob[rows, lanes_at(hp)]
            inner = do.astype(F32) * output[rows, lanes_at(hp)].astype(F32)
            low = low_half((AB, LANES))
            zero = jnp.zeros_like(q)
            parts = []
            for j in range(2):
                mine = low if j == 0 else ~low
                dom = jnp.where(mine, do, zero)
                delta = jnp.sum(jnp.where(mine, inner, 0.0), axis=-1, keepdims=True)
                weights = jnp.concatenate(
                    [big[2 * slot + j, h * AB : (h + 1) * AB, :] for h in range(2)], axis=1
                )
                ds = (weights.astype(F32) * (dot(dom, v, NT) - delta)).astype(BF)
                kvt[1] += dot(dom, weights, TN)
                kvt[0] += dot(jnp.where(mine, q, zero), ds, TN)
                parts.append(dot(ds, k))
            source[rows, lanes_at(hp)] = (jnp.where(low, parts[0], parts[1]) * 0.125).astype(BF)

            @pl.when(qb == queries - 1)
            def _():
                source[:, lanes_at(pairs + hp)] = jnp.transpose(kvt[0] * 0.125).astype(BF)
                source[:, lanes_at(2 * pairs + hp)] = jnp.transpose(kvt[1]).astype(BF)

            return carry

        lax.fori_loop(0, steps, step, 0)

    def grad_weight(target, first, last, left, which):
        for c in range(first, last):
            cols = slice(c * width, (c + 1) * width)
            by_owner(target, cols, dot(left[...], qkv[which, :, cols], TN))

    def grad_trio(target, left, which, hp):
        blocks_of = [qkv[which, :, lanes_at(n * pairs + hp)] for n in range(3)]
        value = dot(left[...], jnp.concatenate(blocks_of, axis=1), TN)
        by_owner(target, slice(hp * trio, (hp + 1) * trio), value)

    def out_grad(which, target):
        by_owner(target, slice(3 * width, 4 * width), dot(oa[which], dfb[...], TN))

    def out_back(which):

        def body(rows):
            dob[rows, :] = dot(dfb[rows, :], wa[which, :, 3 * width :], NT).astype(BF)

        for_wide_rows(body)

    barrier = pltpu.get_barrier_semaphore()
    peers = [(section, later(k)) for k in turns] + [core_peer, side_peer] + far_peers
    for peer in peers:
        pl.semaphore_signal(barrier, inc=1, device_id=peer, device_id_type=MESH)
    for unit in range(5):
        load_masters(unit)
    load_x = pltpu.make_async_copy(x_in.at[own], x.at[own], cot_sem.at[0])
    load_x.start()
    gacc[...] = jnp.zeros_like(gacc)

    rows = [enc_gains[...], enc_shifts[...], dec_gains[...], dec_shifts[...], mask_embed[...], time_table[...]]
    count = sum(row.shape[0] for row in rows)
    rows.append(jnp.zeros((SMALL_ROWS - count, LANES), F32))
    small[shard] = jnp.concatenate(rows, axis=0).astype(BF)
    pair_row = ((section - (sections // 2) * role) * shards + shard) * 2 + role
    row_ids = lax.broadcasted_iota(jnp.int32, (SMALL_ROWS, LANES), 0)
    pick[...] = (row_ids == MASK_ROW + 1 + timestep[pair_row]).astype(F32)
    round_layer(own)
    pl.semaphore_wait(barrier, len(peers))

    for k in turns:
        small_copy(k).start()
    for item in range(4):
        send(item, 0)
    swap_x = swap_copy(x_in.at[other], x.at[own], 0)
    swap_x.start()
    round_layer(other)
    send(4, 0)
    load_masters(5)
    load_masters(6)
    round_master(2, wu, 0)
    send(5, 0)
    round_master(3, wd, 0, True)
    send(6, 0)
    round_master(4, wa, 2)
    send(7, 0)
    round_master(5, wu, 1)
    send(8, 0)
    round_master(6, wd, 1, True)
    send(9, 0)
    swap_cot = swap_copy(cot_in.at[other], cot_land, 1)
    swap_cot.start()

    batch = marks.shape[1]
    total_rows = route.shape[0]
    mine = jnp.zeros((2, length), F32)
    tally = jnp.zeros((1, 1), F32)
    for first in range(0, total_rows, batch):
        for n, array in enumerate((route, remask)):
            copy = pltpu.make_async_copy(array.at[first : first + batch, :], marks.at[n], lo_sem.at[n])
            copy.start()
            copy.wait()
        ids = lax.broadcasted_iota(jnp.int32, (batch, length), 0) + first
        routed = marks[0].astype(F32)
        same = jnp.where(lax.rem(ids, 2) == role, routed, 0.0)
        tally += jnp.sum(jnp.sum(same, axis=0, keepdims=True), axis=1, keepdims=True)
        picked = [
            jnp.sum(jnp.where(ids == pair_row, value, 0.0), axis=0, keepdims=True)
            for value in (marks[1].astype(F32), routed)
        ]
        mine += jnp.concatenate(picked, axis=0)
    scale = mine[1:2, :] * float(total_rows // 2 * length) / tally
    wide_ids = lax.broadcasted_iota(jnp.int32, (LANES, length), 0)
    wide = jnp.where(wide_ids == MASK_LANE, mine[0:1, :], jnp.where(wide_ids == SCALE_LANE, scale, 0.0))
    rs[...] = jnp.transpose(wide)

    for k in turns:
        small_copy(k).wait_recv()
    for owner in range(shards):
        values = small[owner].astype(F32)
        cols = slice(owner * LANES, (owner + 1) * LANES)
        for row in range(MASK_ROW + 1):
            vec[row, :, cols] = values[row : row + 1, :]
        vec[STEP_ROW, :, cols] = jnp.sum(values * pick[...], axis=0, keepdims=True)
    load_x.wait()
    embed(own)

    def pass_side(item):
        take(item, 0)
        send(item, 1)

    def pass_core(item):
        take(item, 1)
        send(item, 2)

    def ready(item):
        take(item, 2)

    def polls_of(*acts):
        return [(when, functools.partial(act, item)) for when, act, item in acts]

    pass_side(0)
    pass_side(1)
    pass_core(0)
    pass_side(2)
    pass_core(1)
    for c in range(3):
        ready(c)
        project(x.at[own], wa.at[own], qkv.at[own], c, c + 1)
        if c == 0:
            pass_core(2)
            pass_side(3)
    attend(own, polls_of((2, pass_core, 3), (4, pass_side, 4)))
    ready(3)
    pass_core(4)
    out_norm(own, own, own, 4 * own, 2 + 5 * own, own)
    swap_copy(x_in.at[other], x.at[other], 0).wait_recv()
    pass_side(5)
    embed(other)
    ready(4)
    project(x.at[other], wa.at[other], qkv.at[other], 0, 3)
    attend(other, polls_of((4, pass_core, 5), (4, pass_side, 6), (7, pass_side, 7)))
    pass_core(6)
    out_norm(other, other, other, 4 * other, 2 + 5 * other, other)
    ready(5)
    h_store = pltpu.make_async_copy(hb.at[0], h_land, h_sem)
    h_load = pltpu.make_async_copy(h_land, hb.at[0], h_sem)
    h_store.start()
    ready(6)
    feed(0, 0, polls_of((3, pass_core, 7), (3, pass_side, 8)))
    h_store.wait()
    final_norm(0, 2, 1, 3, hb.at[2])
    keep_memory = pltpu.make_async_copy(hb.at[2], lo.at[own], lo_sem.at[0])
    pl.when(role == 0)(keep_memory.start)
    for i in range(QUARTERS):
        pl.when(role == 1)(send_lo(hb.at[2], i).start)
    ready(7)
    project(hb.at[1], wa.at[2], qkv.at[2], 0, 1)
    project(hb.at[2], wa.at[2], qkv.at[2], 1, 3)
    attend(2, polls_of((4, pass_core, 8), (4, pass_side, 9)))
    pass_core(9)
    out_norm(2, 1, 3, 5, 8, 0)
    ready(8)
    ready(9)
    def load_cot(layer):
        here = pltpu.make_async_copy(cot_in.at[own], dp, cot_sem.at[1])
        there = pltpu.make_async_copy(cot_land, dp, cot_sem.at[1])
        pl.when(own == layer)(here.start)
        pl.when(own != layer)(there.start)
        return here

    swap_copy(cot_in.at[other], cot_land, 1).wait_recv()
    load_result_cot = load_cot(1)
    feed(1, 0)
    final_norm(1, 4, 6, 9, dob, big.at[3])
    keep_result = pltpu.make_async_copy(dob, lo.at[own], lo_sem.at[0])
    stage_result = pltpu.make_async_copy(dob, out_land, lo_sem.at[1])
    pl.when(role == 1)(keep_result.start)
    stage_result.start()

    def result_upstream(rows):
        return dp[rows, :].astype(F32) * rs[rows, SCALE_LANE : SCALE_LANE + 1]

    load_result_cot.wait()
    norm_back(result_upstream, 1, 4, 6, 9, big.at[3])
    stage_result.wait()
    keep_result.wait()
    feed_back(1, 0, gs.at[0], gs.at[1])
    h_load.start()
    load_memory_cot = load_cot(0)
    sum_start(0)
    sum_start(1)
    norm_back(lambda rows: res[1, rows, :], 1, 3, 5, 8)
    out_back(2)

    def lo_part(i):
        pl.when(role == 0)(send_lo(out_land, i).start)

    attend_back(
        2,
        polls_of((1, sum_core, 0), (1, sum_core, 1), (6, sum_first, 0), (6, sum_first, 1), (6, lo_part, 0)),
    )
    out_grad(2, gs.at[0])
    grad_weight(gs.at[0], 0, 1, hb.at[1], 2)
    grad_weight(gs.at[0], 1, 3, hb.at[2], 2)
    sum_start(2)
    load_memory_cot.wait()

    def cross_body(rows):
        res[1, rows, :] += dot(qkv[2, rows, :width], wa[2, :, :width], NT)
        res[0, rows, :] = dp[rows, :].astype(F32) + dot(
            qkv[2, rows, width:], wa[2, :, width : 3 * width], NT
        )

    for_wide_rows(cross_body)
    sum_core(2)
    norm_back(lambda rows: res[0, rows, :], 0, 2, 1, 3)
    sum_z(0)
    h_load.wait()
    feed_back(
        0, 0, gs.at[1], gs.at[0],
        polls_of(
            (0, sum_far, 0), (0, lo_part, 1), (1, sum_start, 3), (2, sum_first, 2), (2, sum_start, 5),
            (2, sum_z, 1), (2, sum_core, 3), (2, sum_back, 0), (3, sum_core, 5), (3, sum_far, 1),
            (3, sum_end, 0),
        ),
    )
    sum_start(4)
    sum_start(6)

    def gin_part(i):
        send_gin(i).start()

    for turn, layer in enumerate((other, own)):
        slot = 1 - turn
        flag = layer.astype(F32)
        source = x.at[layer]
        target = gs.at[slot]
        norm_back(lambda rows: res[layer, rows, :], layer, layer, 4 * layer, 2 + 5 * layer)
        out_back(layer)

        def last_part(unit):
            for hp in {9: (0, 1), 10: (2,), 11: (3,)}[unit]:
                grad_trio(target, source, layer, hp)
            sum_start(unit)

        if turn == 0:
            acts = polls_of(
                (1, sum_z, 2), (1, sum_core, 4), (1, sum_core, 6), (2, sum_first, 3), (2, sum_back, 1),
                (2, sum_first, 5), (3, sum_end, 1), (3, sum_far, 2), (4, sum_first, 4), (5, sum_first, 6),
                (5, sum_back, 2), (5, sum_z, 3), (6, sum_end, 2), (6, lo_part, 2), (7, sum_z, 5),
                (7, sum_far, 3),
            )
        else:
            out_grad(layer, target)
            sum_start(8)
            acts = polls_of(
                (0, sum_far, 5), (0, sum_z, 6), (0, sum_far, 4), (1, sum_core, 8), (1, lo_part, 3),
                (1, sum_back, 5), (2, sum_first, 7), (2, sum_far, 6), (2, sum_back, 4), (3, gin_part, 1),
                (3, sum_end, 5), (4, last_part, 9), (4, sum_first, 8), (4, sum_end, 4),
                (4, gin_part, 2), (5, sum_core, 9), (5, sum_back, 6), (6, last_part, 10), (6, sum_end, 6),
                (6, gin_part, 3), (7, sum_core, 10), (7, sum_z, 7), (7, sum_first, 9),
            )
        attend_back(layer, acts)
        if turn == 0:
            sum_z(4)
            out_grad(layer, target)
            for hp in range(pairs):
                grad_trio(target, source, layer, hp)
            sum_start(7)
            sum_back(3)
        else:
            last_part(11)
            sum_first(10)
            sum_z(8)
            sum_core(11)

        def body(rows):
            value = res[layer, rows, :] + dot(qkv[layer, rows, :], wa[layer, :, : 3 * width], NT)
            masked = rs[rows, MASK_LANE : MASK_LANE + 1] * flag > 0.5
            gacc[MASK_ROW] += jnp.sum(jnp.where(masked, value, 0.0), axis=0, keepdims=True)
            gacc[STEP_ROW] += jnp.sum(value, axis=0, keepdims=True) * flag
            value = jnp.where(masked, 0.0, value)
            res[layer, rows, :] = value
            if turn == 0:
                dp[rows, :] = value.astype(BF)

        for_wide_rows(body)
        if turn == 0:
            sum_core(7)
            sum_end(3)
            gin_part(0)
        else:
            keep_gin = pltpu.make_async_copy(res.at[layer], gin.at[layer], gin_sem.at[0])
            keep_gin.start()
    sum_first(11)
    small_start()
    sum_far(8)
    sum_z(9)
    sum_z(10)
    sum_far(LAST_WHOLE)
    sum_cross(12)
    small_core()
    for i in range(QUARTERS):
        send_gin(i).wait()
    load_gin = pltpu.make_async_copy(gin_land, dob, gin_sem.at[1])
    load_gin.start()
    sum_far(9)
    sum_cross(13)
    sum_far(10)
    sum_cross(14)
    load_gin.wait()

    def widen(rows):
        res[other, rows, :] = dob[rows, :].astype(F32)

    for_rows(widen)
    keep_other = pltpu.make_async_copy(res.at[other], gin.at[other], gin_sem.at[1])
    keep_other.start()
    small_z()
    sum_z(11)
    sum_back(8)
    sum_back(12)
    for b in range(far):
        small_add(b)
    sum_far(11)
    sum_cross(15)
    for unit in (9, 13, 10, 14):
        sum_back(unit)
    small_add(far)
    sum_back(11)
    sum_back(15)
    for unit in (8, 12, 9, 13, 10, 14, 11, 15):
        sum_end(unit)
    keep_other.wait()
    keep_gin.wait()
    for i in range(QUARTERS):
        send_lo(out_land, i).wait()
    swap_x.wait_send()
    swap_cot.wait_send()
    for k in turns:
        small_copy(k).wait_send()
    for item in range(len(items)):
        for stage in range(3):
            for k in turns:
                src, dst, peer = hop(item, stage, k)
                remote(src, dst, (item, stage, k - 1), peer).wait_send()


def run_pair(tokens, cotangent, route, remask, timestep, masters, small):
    _, length, features = tokens.shape
    shards = lax.axis_size("shard")
    hidden = masters[2].shape[1]
    pairs = features // LANES
    quarters = features // shards
    far = (lax.axis_size("section") // 4).bit_length() - 1
    hbm = pl.BlockSpec(memory_space=pl.ANY)
    vmem = pl.BlockSpec(memory_space=pltpu.VMEM)
    smem = pl.BlockSpec(memory_space=pltpu.SMEM)
    dma = pltpu.SemaphoreType.DMA
    full_a = (3, features, 4 * features)
    full_u = (2, features, hidden)
    full_d = (2, hidden, features)
    out = jax.ShapeDtypeStruct
    one = out(tokens.shape[1:], BF)
    return pl.pallas_call(
        kernel,
        name="pair",
        out_shape=[
            out(tokens.shape, BF),
            out(tokens.shape, F32),
            out((OWNED, features // shards, 4 * features), BF),
            out((SMALL_ROWS, LANES), F32),
            out((3, pairs * (length // AB), 2, length, features), BF),
            out((2, hidden // features, 2, length, features), BF),
            one, one, one, one,
        ],
        in_specs=[hbm] * 4 + [smem] + [hbm] * len(masters) + [vmem] * len(small),
        out_specs=[hbm] * 3 + [vmem] + [hbm] * 6,
        scratch_shapes=[
            pltpu.VMEM(full_a, BF),
            pltpu.VMEM(full_u, BF),
            pltpu.VMEM(full_d, BF),
            pltpu.VMEM((shards, SMALL_ROWS, LANES), BF),
            pltpu.VMEM((VEC_ROWS, 1, features), F32),
            pltpu.VMEM((SMALL_ROWS, LANES), F32),
            pltpu.VMEM((2, min(32, route.shape[0]), length), jnp.int32),
            pltpu.VMEM((VEC_ROWS, 1, features), F32),
            pltpu.VMEM((2, length, features), BF),
            pltpu.VMEM((3, length, 3 * features), BF),
            pltpu.VMEM((3, length, features), BF),
            pltpu.VMEM((4, length, features), BF),
            pltpu.VMEM((length, LANES), F32),
            pltpu.VMEM((3, length, features), BF),
            pltpu.VMEM((2, length, features), F32),
            pltpu.VMEM((length, features), BF),
            pltpu.VMEM((length, features), BF),
            pltpu.VMEM((4, length, features), BF),
            pltpu.VMEM((length, features), BF),
            pltpu.VMEM((2, LANES, length), F32),
            pltpu.VMEM((2, shards, quarters, hidden), BF),
            pltpu.VMEM((2, shards, quarters // 2, hidden), BF),
            pltpu.VMEM((3, shards, quarters // 4, hidden), BF),
            pltpu.VMEM((2, shards - 1, quarters // 4, hidden), BF),
            pltpu.VMEM((2, quarters // 4, hidden), BF),
            pltpu.VMEM((2, far, quarters // 4, hidden), BF),
            pltpu.VMEM((shards, SMALL_ROWS, LANES), F32),
            pltpu.VMEM((shards, SMALL_ROWS, LANES), F32),
            pltpu.VMEM((shards + far, SMALL_ROWS, LANES), F32),
            dma((ITEMS, 3, shards - 1)),
            dma((ITEMS, 3, shards - 1)),
            dma((OWNED, 4)),
            dma((3, shards - 1)),
            dma((2, 10)),
            dma((2,)),
            dma,
            dma((4,)),
            dma((2,)),
            dma((2,)),
            dma((UNITS, 3 + shards + far)),
            dma((UNITS, 3 + shards + far)),
            dma((UNITS,)),
            dma((shards + 1 + far,)),
            dma((shards + 1 + far,)),
            pltpu.SemaphoreType.REGULAR((3 + far, 3)),
        ],
        compiler_params=pltpu.CompilerParams(
            vmem_limit_bytes=64 << 20, has_side_effects=True, collective_id=0
        ),
    )(tokens, cotangent, route, remask, timestep, *masters, *small)


def finish_kernel(
    gout, gv,
    enc_qkv, enc_out, enc_up, enc_down, enc_gains, enc_shifts,
    dec_qkv, dec_out, cross_query, cross_kv, cross_out, dec_up, dec_down, dec_gains, dec_shifts,
    time_table, mask_embed,
):
    width = enc_out.shape[1]
    pairs = width // LANES
    for unit, qkv, out in ((0, enc_qkv, enc_out), (1, dec_qkv, dec_out)):
        for hp in range(pairs):
            for n in range(3):
                to, at = (n * pairs + hp) * LANES, (hp * 3 + n) * LANES
                qkv[:, to : to + LANES] = gout[unit, :, at : at + LANES].astype(F32)
        out[...] = gout[unit, :, 3 * width :].astype(F32)
    cross_query[...] = gout[2, :, :width].astype(F32)
    cross_kv[...] = gout[2, :, width : 3 * width].astype(F32)
    cross_out[...] = gout[2, :, 3 * width :].astype(F32)
    count = gout.shape[1]
    owners = width // count
    for unit, up in ((3, enc_up), (4, dec_up)):
        for c in range(owners):
            for z in range(owners):
                to, at = z * width + c * count, c * width + z * count
                up[:, to : to + count] = gout[unit, :, at : at + count].astype(F32)
    for unit, down in ((5, enc_down), (6, dec_down)):
        for j in range(down.shape[0] // count):
            down[j * count : (j + 1) * count, :] = gout[unit, :, j * width : (j + 1) * width].astype(F32)
    enc_gains[...] = gv[0:2, :]
    enc_shifts[...] = gv[2:4, :]
    dec_gains[...] = gv[4:7, :]
    dec_shifts[...] = gv[7:10, :]
    mask_embed[...] = gv[MASK_ROW : MASK_ROW + 1, :]
    time_table[...] = gv[MASK_ROW + 1 : MASK_ROW + 1 + time_table.shape[0], :]


def per_device(
    tokens, cotangent, route, remask, timestep,
    enc_qkv, enc_out, enc_up, enc_down, enc_gains, enc_shifts,
    dec_qkv, dec_out, cross_query, cross_kv, cross_out, dec_up, dec_down, dec_gains, dec_shifts,
    time_table, mask_embed,
):
    masters = (
        enc_qkv, enc_out, enc_up, enc_down, dec_qkv, dec_out,
        cross_query, cross_kv, cross_out, dec_up, dec_down,
    )
    mask_row = mask_embed[None, :]
    small = (enc_gains, enc_shifts, dec_gains, dec_shifts, mask_row, time_table)
    layer_out, grad_in, gout, gv = run_pair(
        tokens, cotangent, route, remask, timestep, masters, small
    )[:4]
    owned = (
        enc_qkv, enc_out, enc_up, enc_down, enc_gains, enc_shifts,
        dec_qkv, dec_out, cross_query, cross_kv, cross_out, dec_up, dec_down, dec_gains, dec_shifts,
        time_table, mask_row,
    )
    vmem = pl.BlockSpec(memory_space=pltpu.VMEM)
    grads = pl.pallas_call(
        finish_kernel,
        name="finish",
        out_shape=[jax.ShapeDtypeStruct(array.shape, F32) for array in owned],
        in_specs=[vmem] * 2,
        out_specs=[vmem] * len(owned),
        compiler_params=pltpu.CompilerParams(vmem_limit_bytes=48 << 20),
    )(gout, gv)
    return (layer_out, grad_in, *grads[:-1], grads[-1][0])


def solution(mesh):
    rows = P(("section", "shard"), None, None)
    first, second, copied = P("shard", None), P(None, "shard"), P()
    return jax.shard_map(
        per_device,
        mesh=mesh,
        in_specs=(rows, rows, copied, copied, copied)
        + (first,) * 4 + (second,) * 2 + (first,) * 7 + (second,) * 3 + (P("shard"),),
        out_specs=(rows, rows)
        + (first,) * 4 + (second,) * 2 + (first,) * 7 + (second,) * 3 + (P("shard"),),
        check_vma=False,
    )
```
